32 devices in a mesh: dp: 8 (over z, x), mlp: 4 (over y, core).
Axes of the slice: x: 2, y: 2, z: 4, core: 2. Of those that a mesh axis runs over, the one named last changes fastest.
Arguments:
- tokens: bfloat16 [2, 6304, 768], P(None, ('dp', 'mlp')), may hold values from -6 to 6
- keep_mask: int32 [2, 6304], P(None, ('dp', 'mlp')), may hold values 0 or 1
- position_index: int32 [197, 197], replicated, may hold values from 0 to 731
- cotangent: bfloat16 [2, 6304, 768], P(None, ('dp', 'mlp')), may hold values from -6 to 6
- first_gain: float32 [768], replicated, may hold values from 0.5 to 1.5
- first_shift: float32 [768], replicated, may hold values from -4 to 4
- inner_weight: bfloat16 [768, 2304], P(('dp', 'mlp')), may hold values from -0.21875 to 0.21875
- query_bias: float32 [768], replicated, may hold values from -6 to 6
- value_bias: float32 [768], replicated, may hold values from -6 to 6
- outer_weight: bfloat16 [768, 768], P(('dp', 'mlp')), may hold values from -0.875 to 0.875
- outer_bias: float32 [768], replicated, may hold values from -4 to 4
- attend_scale: float32 [768], replicated, may hold values from 0.5 to 1.5
- second_gain: float32 [768], replicated, may hold values from 0.5 to 1.5
- second_shift: float32 [768], replicated, may hold values from -4 to 4
- up_weight: bfloat16 [768, 3072], P('dp', 'mlp'), may hold values from -0.21875 to 0.21875
- up_bias: float32 [3072], replicated, may hold values from -6 to 6
- down_weight: bfloat16 [3072, 768], P('mlp', 'dp'), may hold values from -0.109375 to 0.109375
- down_bias: float32 [768], replicated, may hold values from -4 to 4
- feed_scale: float32 [768], replicated, may hold values from 0.5 to 1.5
- position_table: float32 [732, 12], replicated, may hold values from -6 to 6
Outputs:
- result: bfloat16 [2, 6304, 768], P(None, ('dp', 'mlp'))
- gradient_tokens: bfloat16 [2, 6304, 768], P(None, ('dp', 'mlp'))
- gradient_inner: float32 [768, 2304], P(('dp', 'mlp'))
- gradient_outer: float32 [768, 768], P(('dp', 'mlp'))
- gradient_up: float32 [768, 3072], P('dp', 'mlp')
- gradient_down: float32 [3072, 768], P('mlp', 'dp')
- gradient_first_gain: float32 [768], replicated
- gradient_first_shift: float32 [768], replicated
- gradient_query_bias: float32 [768], replicated
- gradient_value_bias: float32 [768], replicated
- gradient_outer_bias: float32 [768], replicated
- gradient_attend_scale: float32 [768], replicated
- gradient_second_gain: float32 [768], replicated
- gradient_second_shift: float32 [768], replicated
- gradient_up_bias: float32 [3072], replicated
- gradient_down_bias: float32 [768], replicated
- gradient_feed_scale: float32 [768], replicated
- gradient_table: float32 [732, 12], replicated
The draws below stay inside these ranges and needn't reach their ends.
All inputs are finite; a program needn't handle non-finite values. No bound on the sum of `keep_mask` on one device may be relied on, other than what follows from the above.
Results may differ from the reference program's by a relative error of at most 0.014.
Values may be sent and summed in bfloat16 or wider, within the bound.
A program may use at most 192 MiB of HBM per device.

```python
import jax
import jax.numpy as jnp
from jax import lax

D = 768
HEADS = 12
FF = 3072
NREL = 732
IMG = 197
MICRO = 2
ROWS = 6304
N_MLP = 4


def with_ends(drawn, key, least, top_value):
    longest = drawn.shape.index(max(drawn.shape))
    spots = []
    for shift in (0, 1):
        where = [jax.random.randint(jax.random.fold_in(key, axis), (), 0, length) for axis, length in enumerate(drawn.shape)]
        where[longest] = (where[longest] + shift) % drawn.shape[longest]
        spots.append(tuple(where))
    return drawn.at[spots[0]].set(least).at[spots[1]].set(top_value)


def level_of(key, shape, pieces, smallest, top_value):
    factor_of = 1.0
    for position, parts in pieces:
        draws = jax.random.uniform(jax.random.fold_in(jax.random.fold_in(key, 6), position), (parts,), jnp.float32, smallest / len(pieces), top_value / len(pieces))
        factor_of = factor_of * jnp.repeat(jnp.exp(draws), shape[position] // parts).reshape((-1,) + (1,) * (len(shape) - 1 - position))
    return factor_of


def bell_draw(rng, extent, scale, reach, shards=(), dtype=jnp.bfloat16):
    array = jax.random.normal(rng, extent, jnp.float32) * scale
    if len(shards) > 0:
        array = level_of(rng, extent, shards, -0.22, 0.18) * array
    return jnp.clip(array, min=-reach, max=reach).astype(dtype)


def setup_inputs(seed: int = 0) -> dict:
    key_list = jax.random.split(jax.random.key(seed), 21)
    return {
        "tokens": bell_draw(key_list[0], (MICRO, ROWS, D), 1.0, 6.0, ((1, 32),)),
        "keep_mask": with_ends((jax.random.randint(key_list[1], (MICRO, ROWS), 0, 4) < 3).astype(jnp.int32), jax.random.fold_in(key_list[1], 1), 0, 1),
        "position_index": with_ends(jax.random.randint(key_list[2], (IMG, IMG), 0, NREL), jax.random.fold_in(key_list[2], 1), 0, NREL - 1).astype(jnp.int32),
        "cotangent": bell_draw(key_list[3], (MICRO, ROWS, D), 1.0, 6.0, ((1, 32),)),
        "first_gain": jnp.clip(1.0 + 0.1 * jax.random.normal(key_list[4], (D,), jnp.float32), 0.5, 1.5),
        "first_shift": bell_draw(key_list[5], (D,), 0.3, 4.0, (), jnp.float32),
        "inner_weight": bell_draw(key_list[6], (D, 3 * D), D ** -0.5, 0.21875, ((0, 32),)),
        "query_bias": bell_draw(key_list[7], (D,), 0.5, 6.0, (), jnp.float32),
        "value_bias": bell_draw(key_list[8], (D,), 0.5, 6.0, (), jnp.float32),
        "outer_weight": bell_draw(key_list[9], (D, D), (D // 16) ** -0.5, 0.875, ((0, 32),)),
        "outer_bias": bell_draw(key_list[10], (D,), 0.3, 4.0, (), jnp.float32),
        "attend_scale": jnp.clip(1.0 + 0.1 * jax.random.normal(key_list[11], (D,), jnp.float32), 0.5, 1.5),
        "second_gain": jnp.clip(1.0 + 0.1 * jax.random.normal(key_list[12], (D,), jnp.float32), 0.5, 1.5),
        "second_shift": bell_draw(key_list[13], (D,), 0.3, 4.0, (), jnp.float32),
        "up_weight": bell_draw(key_list[14], (D, FF), D ** -0.5, 0.21875, ((0, 8), (1, 4))),
        "up_bias": bell_draw(key_list[15], (FF,), 0.5, 6.0, (), jnp.float32),
        "down_weight": bell_draw(key_list[16], (FF, D), FF ** -0.5, 0.109375, ((0, 4), (1, 8))),
        "down_bias": bell_draw(key_list[17], (D,), 0.3, 4.0, (), jnp.float32),
        "feed_scale": jnp.clip(1.0 + 0.1 * jax.random.normal(key_list[18], (D,), jnp.float32), 0.5, 1.5),
        "position_table": bell_draw(key_list[19], (NREL, HEADS), 1.0, 6.0, (), jnp.float32),
    }


EPS = 1e-06
HIGH = lax.Precision.HIGHEST
ROOT_HALF = 0.7071067811865476

@jax.custom_vjp
def low(v):
    return lax.optimization_barrier(v.astype(jnp.bfloat16)).astype(jnp.float32)

@jax.custom_vjp
def low_back(v):
    return v

def low_keep(v):
    return (low(v), None)

def low_pass(kept, grad):
    return (grad,)

def back_keep(v):
    return (v, None)

def back_low(kept, grad):
    return (low(grad),)
low.defvjp(low_keep, low_pass)
low_back.defvjp(back_keep, back_low)

def layer_norm(values, gain, shift):
    mean = lax.optimization_barrier(jnp.mean(values, -1, keepdims=True))
    centred = values - mean
    variance = lax.optimization_barrier(jnp.mean(centred * centred, -1, keepdims=True))
    return centred * lax.rsqrt(variance + EPS) * gain + shift

def matmul(left, right):
    return jnp.einsum('bri,io->bro', left, right, precision=HIGH)

def layer(params, source, keeps, position_index):
    first_gain, first_shift, inner_weight, query_bias, value_bias, outer_weight, outer_bias, attend_scale, second_gain, second_shift, up_weight, up_bias, down_weight, down_bias, feed_scale, position_table = params
    images, rows, width = source.shape
    heads = position_table.shape[1]
    head_dim = width // heads
    normed_one = low(layer_norm(source, first_gain, first_shift))
    shift_vector = jnp.concatenate([query_bias, jnp.zeros_like(query_bias), value_bias])
    projected = low_back(low(matmul(normed_one, inner_weight) + shift_vector))
    query = projected[..., :width].reshape(images, rows, heads, head_dim)
    keys = projected[..., width:2 * width].reshape(images, rows, heads, head_dim)
    values = projected[..., 2 * width:].reshape(images, rows, heads, head_dim)
    raw = low_back(jnp.einsum('bqhd,bkhd->bhqk', query, keys, precision=HIGH) * head_dim ** (-0.5))
    bias = jnp.transpose(position_table[position_index], (2, 0, 1))
    seen = jnp.arange(rows)
    diagonal = (seen[:, None] == seen[None, :])[None, None]
    allowed = jnp.logical_or(keeps[:, None, None, :] == 1, diagonal)
    logits = jnp.where(allowed, raw + bias[None], -1e+30)
    top = lax.optimization_barrier(jnp.max(logits, -1, keepdims=True))
    expd = jnp.exp(logits - top)
    probs = low(expd / lax.optimization_barrier(jnp.sum(expd, -1, keepdims=True)))
    mixed = jnp.einsum('bhqk,bkhd->bqhd', probs, values, precision=HIGH).reshape(images, rows, width)
    mixed = low_back(low(mixed))
    attend = low_back(matmul(mixed, outer_weight)) + outer_bias
    resid = source + attend_scale * attend
    normed_two = low(layer_norm(resid, second_gain, second_shift))
    pre = low_back(matmul(normed_two, up_weight) + up_bias)
    hidden = low(0.5 * pre * (1.0 + lax.erf(pre * ROOT_HALF)))
    feed = low_back(matmul(hidden, down_weight)) + down_bias
    return resid + feed_scale * feed

def reference(tokens, keep_mask, position_index, cotangent, first_gain, first_shift, inner_weight, query_bias, value_bias, outer_weight, outer_bias, attend_scale, second_gain, second_shift, up_weight, up_bias, down_weight, down_bias, feed_scale, position_table):
    params = (first_gain.astype(jnp.float32), first_shift.astype(jnp.float32), inner_weight.astype(jnp.float32), query_bias.astype(jnp.float32), value_bias.astype(jnp.float32), outer_weight.astype(jnp.float32), outer_bias.astype(jnp.float32), attend_scale.astype(jnp.float32), second_gain.astype(jnp.float32), second_shift.astype(jnp.float32), up_weight.astype(jnp.float32), up_bias.astype(jnp.float32), down_weight.astype(jnp.float32), down_bias.astype(jnp.float32), feed_scale.astype(jnp.float32), position_table.astype(jnp.float32))
    micro, total_rows, width = tokens.shape
    rows = position_index.shape[0]
    blocks = micro * total_rows // (N_MLP * rows)
    sources = tokens.reshape(blocks, N_MLP, rows, width)
    keeps = keep_mask.reshape(blocks, N_MLP, rows)
    upstreams = cotangent.reshape(blocks, N_MLP, rows, width)

    def step(totals, item):
        source, keep, upstream = item

        def forward(prm, values):
            return layer(prm, values, keep, position_index)
        output, pull = jax.vjp(forward, params, source.astype(jnp.float32))
        grads, grad_source = pull(upstream.astype(jnp.float32))
        totals = jax.tree.map(jnp.add, totals, grads)
        return (totals, (output.astype(jnp.bfloat16), grad_source.astype(jnp.bfloat16)))
    zeros = jax.tree.map(jnp.zeros_like, params)
    totals, (outputs, grad_sources) = lax.scan(step, zeros, (sources, keeps, upstreams))
    result = outputs.reshape(micro, total_rows, width)
    gradient_tokens = grad_sources.reshape(micro, total_rows, width)
    return (result, gradient_tokens, totals[2], totals[5], totals[10], totals[12], totals[0], totals[1], totals[3], totals[4], totals[6], totals[7], totals[8], totals[9], totals[11], totals[13], totals[14], totals[15])
```

```python
import jax
import jax.numpy as jnp
from jax import lax
from jax.experimental import pallas as pl
from jax.experimental.pallas import tpu as pltpu
from jax.sharding import PartitionSpec as P

EPS = 1e-06
ROOT_HALF = 0.7071067811865476
DENSITY = 0.3989422804014327


MESH = pl.DeviceIdType.MESH
KINDS = (0, 0, 0, 0, 1, 1, 1, 1)
SLOT = (0, 1, 2, 3, 0, 1, 2, 3)
Y_LAST = (True, False, True, False, True, False, True, False)
N_COPY = 10


def place():
    dp = lax.axis_index("dp")
    mlp = lax.axis_index("mlp")
    return lax.div(dp, 2), lax.rem(dp, 2), lax.div(mlp, 2), lax.rem(mlp, 2)


def device(z, x, y, c):
    return (z * 2 + x, y * 2 + c)


def own(ref, kind, z, x, y, c):
    return ref.at[c, z, x, y] if kind == 0 else ref.at[y, c, z, x]


def line(ref, kind, x, y, c):
    return ref.at[c, :, x, y] if kind == 0 else ref.at[y, c, :, x]


def greet(z, x, y, c):
    barrier = pltpu.get_barrier_semaphore()
    others = [device(lax.rem(z + d, 4), x, y, c) for d in (1, 2, 3)]
    others += [device(z, 1 - x, y, c), device(z, x, 1 - y, c), device(z, x, y, 1 - c)]
    for other in others:
        pl.semaphore_signal(barrier, inc=1, device_id=other, device_id_type=MESH)
    pl.semaphore_wait(barrier, len(others))


class Link:
    def __init__(self, send, recv):
        self.send, self.recv, self.pending = send, recv, []

    def copy(self, src, dst, slot, target):
        made = pltpu.make_async_remote_copy(
            src_ref=src,
            dst_ref=dst,
            send_sem=self.send.at[slot],
            recv_sem=self.recv.at[slot],
            device_id=target,
            device_id_type=MESH,
        )
        made.start()
        self.pending.append(made)
        return made

    def drain(self):
        for made in self.pending:
            made.wait_send()
        self.pending = []


class Gather:
    def __init__(self, link, ref, unit, where):
        self.link, self.ref, self.unit, self.where = link, ref, unit, where
        self.kind = KINDS[unit]
        self.base = unit * N_COPY
        self.y_last = Y_LAST[unit]

    def put(self, part, slot, target):
        return self.link.copy(part, part, self.base + slot, target)

    def along_z(self):
        z, x, y, c = self.where
        part = own(self.ref, self.kind, z, x, y, c)
        self.z = [self.put(part, d - 1, device(lax.rem(z + d, 4), x, y, c)) for d in (1, 2, 3)]

    def line_out(self):
        z, x, y, c = self.where
        for made in self.z:
            made.wait_recv()
        part = line(self.ref, self.kind, x, y, c)
        self.to_x = self.put(part, 3, device(z, 1 - x, y, c))
        self.to_y = self.put(part, 4, device(z, x, 1 - y, c))
        self.to_c = [self.put(part, 6, device(z, x, y, 1 - c))]

    def plane_out(self):
        z, x, y, c = self.where
        mirror = device(z, x, y, 1 - c)
        if self.y_last:
            self.to_x.wait_recv()
            part = line(self.ref, self.kind, 1 - x, y, c)
            self.last = self.put(part, 5, device(z, x, 1 - y, c))
            self.to_c.append(self.put(part, 7, mirror))
            self.to_y.wait_recv()
            self.to_c.append(self.put(line(self.ref, self.kind, x, 1 - y, c), 8, mirror))
        else:
            self.to_y.wait_recv()
            part = line(self.ref, self.kind, x, 1 - y, c)
            self.last = self.put(part, 5, device(z, 1 - x, y, c))
            self.to_c.append(self.put(part, 7, mirror))
            self.to_x.wait_recv()
            self.to_c.append(self.put(line(self.ref, self.kind, 1 - x, y, c), 8, mirror))

    def core_out(self):
        z, x, y, c = self.where
        self.last.wait_recv()
        part = line(self.ref, self.kind, 1 - x, 1 - y, c)
        self.to_c.append(self.put(part, 9, device(z, x, y, 1 - c)))

    def finish(self):
        for made in self.to_c:
            made.wait_recv()


def gather_kernel(small_ref, large_ref, narrow_ref, wide_ref, pair, send, recv):
    where = z, x, y, c = place()
    greet(*where)
    link = Link(send, recv)
    pair[:, c] = small_ref[:, c]
    mate = link.copy(small_ref.at[:, 1 - c], pair.at[:, c], 8 * N_COPY, device(z, x, y, 1 - c))
    for unit in range(4):
        wide_ref[unit, y, c, z, x] = large_ref[unit]
    mate.wait_recv()
    for unit in range(4):
        narrow_ref[unit, c, z, x, y] = pair[unit].reshape(48, 384).astype(jnp.bfloat16)
    units = [Gather(link, (narrow_ref if KINDS[u] == 0 else wide_ref).at[SLOT[u]], u, where) for u in range(8)]
    for unit in units:
        unit.along_z()
    for step in range(8 + 2):
        if step < 8:
            units[step].line_out()
        if 0 <= step - 1 < 8:
            units[step - 1].plane_out()
        if 0 <= step - 2 < 8:
            units[step - 2].core_out()
    for unit in units:
        unit.finish()
    link.drain()


def gather_all(small, large):
    return pl.pallas_call(
        gather_kernel,
        out_shape=(
            jax.ShapeDtypeStruct((4, 2, 4, 2, 2, 48, 384), jnp.bfloat16),
            jax.ShapeDtypeStruct((4, 2, 2, 4, 2, 96, 384), jnp.bfloat16),
        ),
        in_specs=[pl.BlockSpec(memory_space=pltpu.VMEM)] * 2,
        out_specs=[pl.BlockSpec(memory_space=pltpu.VMEM)] * 2,
        scratch_shapes=[
            pltpu.VMEM((4, 2, 24, 384), jnp.float32),
            pltpu.SemaphoreType.DMA((8 * N_COPY + 1,)),
            pltpu.SemaphoreType.DMA((8 * N_COPY + 1,)),
        ],
        compiler_params=pltpu.CompilerParams(
            collective_id=0, has_side_effects=True, vmem_limit_bytes=56 * 2**20
        ),
    )(small, large)


class Scatter:
    def __init__(self, link, ref, half, quarter, eighth, parts, unit, where):
        self.link, self.ref, self.unit, self.where = link, ref, unit, where
        self.half, self.quarter, self.eighth, self.parts = half, quarter, eighth, parts
        self.kind = KINDS[unit]
        self.base = unit * N_COPY
        self.x_last = Y_LAST[unit]

    def put(self, src, dst, slot, target):
        return self.link.copy(src, dst, self.base + slot, target)

    def by_core(self, ref, c):
        return ref.at[c] if self.kind == 0 else ref.at[:, c]

    def by_y(self, ref, y, c):
        return ref.at[c, :, :, y] if self.kind == 0 else ref.at[y, c]

    def by_x(self, ref, x, c):
        return ref.at[c, :, x] if self.kind == 0 else ref.at[:, c, :, x]

    def mix(self, here, there):
        total = here[...].astype(jnp.float32) + there[...].astype(jnp.float32)
        here[...] = total.astype(jnp.bfloat16)

    def to_core(self):
        z, x, y, c = self.where
        self.made = self.put(self.by_core(self.ref, 1 - c), self.half, 0, device(z, x, y, 1 - c))

    def to_first(self):
        z, x, y, c = self.where
        self.made.wait_recv()
        self.mix(self.by_core(self.ref, c), self.half)
        if self.x_last:
            self.made = self.put(self.by_y(self.ref, 1 - y, c), self.quarter, 1, device(z, x, 1 - y, c))
        else:
            self.made = self.put(self.by_x(self.ref, 1 - x, c), self.quarter, 1, device(z, 1 - x, y, c))

    def to_second(self):
        z, x, y, c = self.where
        self.made.wait_recv()
        self.mix(self.by_y(self.ref, y, c) if self.x_last else self.by_x(self.ref, x, c), self.quarter)
        if self.x_last:
            self.made = self.put(line(self.ref, self.kind, 1 - x, y, c), self.eighth, 2, device(z, 1 - x, y, c))
        else:
            self.made = self.put(line(self.ref, self.kind, x, 1 - y, c), self.eighth, 2, device(z, x, 1 - y, c))

    def to_z(self):
        z, x, y, c = self.where
        self.made.wait_recv()
        self.mix(line(self.ref, self.kind, x, y, c), self.eighth)
        self.z = []
        for d in (1, 2, 3):
            far = lax.rem(z + d, 4)
            src = own(self.ref, self.kind, far, x, y, c)
            self.z.append(self.put(src, self.parts.at[d - 1], 2 + d, device(far, x, y, c)))

    def total(self):
        for made in self.z:
            made.wait_recv()
        total = own(self.ref, self.kind, *self.where)[...].astype(jnp.float32)
        for d in range(3):
            total = total + self.parts[d].astype(jnp.float32)
        return total


def reduce_kernel(narrow_in, wide_in, small_ref, large_ref, narrow_ref, wide_ref, half0, half1, quarter0, quarter1a, quarter1b, eighth0, eighth1, parts0, parts1, mine, send, recv, local):
    where = z, x, y, c = place()
    greet(*where)
    link = Link(send, recv)
    bring = [
        pltpu.make_async_copy(narrow_in, narrow_ref, local.at[0]),
        pltpu.make_async_copy(wide_in, wide_ref, local.at[1]),
    ]
    for made in bring:
        made.start()
    for made in bring:
        made.wait()
    units = []
    for u in range(8):
        s = SLOT[u]
        if KINDS[u] == 0:
            units.append(Scatter(link, narrow_ref.at[s], half0.at[s], quarter0.at[s], eighth0.at[s], parts0.at[s], u, where))
        else:
            quarter1 = quarter1a if Y_LAST[u] else quarter1b
            units.append(Scatter(link, wide_ref.at[s], half1.at[s], quarter1.at[s // 2], eighth1.at[s], parts1.at[s], u, where))
    for unit in units:
        unit.to_core()
    mates = []
    for step in range(8 + 3):
        if step < 8:
            units[step].to_first()
        if 0 <= step - 1 < 8:
            units[step - 1].to_second()
        if 0 <= step - 2 < 8:
            units[step - 2].to_z()
        u = step - 3
        if 0 <= u < 8:
            total = units[u].total()
            if KINDS[u] == 0:
                s = SLOT[u]
                mine[s] = total.reshape(2, 24, 384)
                small_ref[s, c] = mine[s, c]
                mates.append(link.copy(mine.at[s, 1 - c], small_ref.at[s, c], 8 * N_COPY + s, device(z, x, y, 1 - c)))
            else:
                large_ref[SLOT[u]] = total
    for made in mates:
        made.wait_recv()
    link.drain()


def reduce_all(narrow, wide):
    bf = jnp.bfloat16
    return pl.pallas_call(
        reduce_kernel,
        out_shape=(
            jax.ShapeDtypeStruct((4, 2, 24, 384), jnp.float32),
            jax.ShapeDtypeStruct((4, 96, 384), jnp.float32),
        ),
        in_specs=[pl.BlockSpec(memory_space=pl.ANY)] * 2,
        out_specs=[pl.BlockSpec(memory_space=pltpu.VMEM)] * 2,
        scratch_shapes=[
            pltpu.VMEM((4, 2, 4, 2, 2, 48, 384), bf),
            pltpu.VMEM((4, 2, 2, 4, 2, 96, 384), bf),
            pltpu.VMEM((4, 4, 2, 2, 48, 384), bf),
            pltpu.VMEM((4, 2, 4, 2, 96, 384), bf),
            pltpu.VMEM((4, 4, 2, 48, 384), bf),
            pltpu.VMEM((2, 4, 2, 96, 384), bf),
            pltpu.VMEM((2, 2, 4, 96, 384), bf),
            pltpu.VMEM((4, 4, 48, 384), bf),
            pltpu.VMEM((4, 4, 96, 384), bf),
            pltpu.VMEM((4, 3, 48, 384), bf),
            pltpu.VMEM((4, 3, 96, 384), bf),
            pltpu.VMEM((4, 2, 24, 384), jnp.float32),
            pltpu.SemaphoreType.DMA((8 * N_COPY + 4,)),
            pltpu.SemaphoreType.DMA((8 * N_COPY + 4,)),
            pltpu.SemaphoreType.DMA((2,)),
        ],
        compiler_params=pltpu.CompilerParams(
            collective_id=1, has_side_effects=True, vmem_limit_bytes=56 * 2**20
        ),
    )(narrow, wide)


def layer_norm(values, gain, shift):
    mean = jnp.mean(values, -1, keepdims=True)
    centred = values - mean
    variance = jnp.mean(centred * centred, -1, keepdims=True)
    scaled = lax.rsqrt(variance + EPS)
    unit = centred * scaled
    return (unit * gain + shift, unit, scaled)


def norm_back(upstream, unit, scaled, gain):
    inner = upstream * gain
    first = jnp.mean(inner, -1, keepdims=True)
    second = jnp.mean(inner * unit, -1, keepdims=True)
    return (
        scaled * (inner - first - unit * second),
        jnp.sum(upstream * unit, 0),
        jnp.sum(upstream, 0),
    )


def gelu_pair(pre):
    cumul = 0.5 * (1.0 + lax.erf(pre * ROOT_HALF))
    return (pre * cumul, cumul + pre * jnp.exp(-0.5 * pre * pre) * DENSITY)


def fetch(inner_weight, outer_weight, up_weight, down_weight):
    inner_full, outer_full = (
        lax.all_gather(inner_weight, ("dp", "mlp"), axis=0, tiled=True),
        lax.all_gather(outer_weight, ("dp", "mlp"), axis=0, tiled=True),
    )
    up_full, down_full = (
        lax.all_gather(up_weight, "dp", axis=0, tiled=True),
        lax.all_gather(down_weight, "dp", axis=1, tiled=True),
    )
    return (inner_full, outer_full, up_full, down_full)


def contract_rows(left, right):
    return lax.dot_general(
        left, right, (((0,), (0,)), ((), ())), preferred_element_type=jnp.float32
    )


def contract_cols(left, right):
    return lax.dot_general(
        left, right, (((1,), (1,)), ((), ())), preferred_element_type=jnp.float32
    )


def logits_of(query, keys, bias, allowed, factor):
    raw = jnp.einsum("qhd,khd->hqk", query, keys, preferred_element_type=jnp.float32) * factor
    return jnp.where(allowed, raw + bias, -1e30)


def body(
    tokens,
    keep_mask,
    position_index,
    cotangent,
    first_gain,
    first_shift,
    inner_weight,
    query_bias,
    value_bias,
    outer_weight,
    outer_bias,
    attend_scale,
    second_gain,
    second_shift,
    up_weight,
    up_bias,
    down_weight,
    down_bias,
    feed_scale,
    position_table,
):
    micro, rows, width = tokens.shape
    heads = position_table.shape[1]
    head_dim = width // heads
    factor = head_dim ** (-0.5)
    entries = position_table.shape[0]
    columns = up_weight.shape[1]
    col_start = lax.axis_index("mlp") * columns
    up_local = lax.dynamic_slice_in_dim(up_bias, col_start, columns, 0)
    shift_vector = jnp.concatenate([query_bias, jnp.zeros_like(query_bias), value_bias])
    table_by_head = jnp.transpose(position_table)
    bias = table_by_head[:, position_index]
    seen = jnp.arange(rows)
    diagonal = seen[:, None] == seen[None, :]
    flat_index = position_index.reshape(rows * rows)
    zero_width = jnp.zeros((width,), jnp.float32)
    sum_inner = jnp.zeros((width, 3 * width), jnp.float32)
    sum_outer = jnp.zeros((width, width), jnp.float32)
    sum_up = jnp.zeros((width, columns), jnp.float32)
    sum_down = jnp.zeros((columns, width), jnp.float32)
    sum_table_heads = jnp.zeros((heads, entries), jnp.float32)
    sum_up_bias = jnp.zeros((columns,), jnp.float32)
    sum_first_gain = zero_width
    sum_first_shift = zero_width
    sum_query_bias = zero_width
    sum_value_bias = zero_width
    sum_outer_bias = zero_width
    sum_attend_scale = zero_width
    sum_second_gain = zero_width
    sum_second_shift = zero_width
    sum_down_bias = zero_width
    sum_feed_scale = zero_width
    results = []
    input_grads = []
    for index in range(micro):
        inner_full, outer_full, up_full, down_full = fetch(
            inner_weight, outer_weight, up_weight, down_weight
        )
        source = tokens[index].astype(jnp.float32)
        allowed = jnp.logical_or(keep_mask[index][None, :] == 1, diagonal)[None]
        normed_one, unit_one, scaled_one = layer_norm(source, first_gain, first_shift)
        normed_one = normed_one.astype(jnp.bfloat16)
        projected = (
            jnp.dot(normed_one, inner_full, preferred_element_type=jnp.float32) + shift_vector
        ).astype(jnp.bfloat16)
        query = projected[:, :width].reshape(rows, heads, head_dim)
        keys = projected[:, width : 2 * width].reshape(rows, heads, head_dim)
        values = projected[:, 2 * width :].reshape(rows, heads, head_dim)
        logits = logits_of(query, keys, bias, allowed, factor)
        top = jnp.max(logits, -1, keepdims=True)
        expd = jnp.exp(logits - top)
        total = jnp.sum(expd, -1, keepdims=True)
        probs = expd / total
        log_total = top + jnp.log(total)
        mixed = jnp.einsum(
            "hqk,khd->qhd", probs.astype(jnp.bfloat16), values, preferred_element_type=jnp.float32
        )
        mixed = mixed.reshape(rows, width).astype(jnp.bfloat16)
        attend = jnp.dot(mixed, outer_full, preferred_element_type=jnp.float32) + outer_bias
        resid = source + attend_scale * attend
        normed_two, unit_two, scaled_two = layer_norm(resid, second_gain, second_shift)
        normed_two = normed_two.astype(jnp.bfloat16)
        sequence_rows = lax.all_gather(normed_two, "mlp", axis=0, tiled=True)
        pre = jnp.dot(sequence_rows, up_full, preferred_element_type=jnp.float32) + up_local
        active, slope = gelu_pair(pre)
        hidden = active.astype(jnp.bfloat16)
        feed = (
            lax.psum_scatter(
                jnp.dot(hidden, down_full, preferred_element_type=jnp.float32).astype(jnp.bfloat16),
                "mlp",
                scatter_dimension=0,
                tiled=True,
            ).astype(jnp.float32)
            + down_bias
        )
        results.append((resid + feed_scale * feed).astype(jnp.bfloat16))
        inner_full, outer_full, up_full, down_full = fetch(
            inner_weight, outer_weight, up_weight, down_weight
        )
        upstream = cotangent[index].astype(jnp.float32)
        sum_feed_scale = sum_feed_scale + jnp.sum(feed * upstream, 0)
        dfeed = feed_scale * upstream
        sum_down_bias = sum_down_bias + jnp.sum(dfeed, 0)
        upstream_all = lax.all_gather(dfeed.astype(jnp.bfloat16), "mlp", axis=0, tiled=True)
        sum_down = sum_down + contract_rows(hidden, upstream_all)
        dpre = (contract_cols(upstream_all, down_full) * slope).astype(jnp.bfloat16)
        sum_up_bias = sum_up_bias + jnp.sum(dpre.astype(jnp.float32), 0)
        sum_up = sum_up + contract_rows(sequence_rows, dpre)
        dnormed_two = lax.psum_scatter(
            contract_cols(dpre, up_full).astype(jnp.bfloat16),
            "mlp",
            scatter_dimension=0,
            tiled=True,
        ).astype(jnp.float32)
        dresid_norm, part_gain, part_shift = norm_back(
            dnormed_two, unit_two, scaled_two, second_gain
        )
        sum_second_gain = sum_second_gain + part_gain
        sum_second_shift = sum_second_shift + part_shift
        dresid = upstream + dresid_norm
        sum_attend_scale = sum_attend_scale + jnp.sum(attend * dresid, 0)
        dattend = attend_scale * dresid
        sum_outer_bias = sum_outer_bias + jnp.sum(dattend, 0)
        dattend_low = dattend.astype(jnp.bfloat16)
        sum_outer = sum_outer + contract_rows(mixed, dattend_low)
        dmixed = (
            contract_cols(dattend_low, outer_full)
            .astype(jnp.bfloat16)
            .reshape(rows, heads, head_dim)
        )
        logits = logits_of(query, keys, bias, allowed, factor)
        probs = jnp.exp(logits - log_total)
        dvalues = jnp.einsum(
            "hqk,qhd->khd", probs.astype(jnp.bfloat16), dmixed, preferred_element_type=jnp.float32
        )
        dprobs = jnp.einsum("qhd,khd->hqk", dmixed, values, preferred_element_type=jnp.float32)
        dlogits = probs * (dprobs - jnp.sum(dprobs * probs, -1, keepdims=True))
        sum_table_heads = sum_table_heads.at[:, flat_index].add(dlogits.reshape(heads, rows * rows))
        dlogits_low = dlogits.astype(jnp.bfloat16)
        dquery = (
            jnp.einsum("hqk,khd->qhd", dlogits_low, keys, preferred_element_type=jnp.float32)
            * factor
        )
        dkeys = (
            jnp.einsum("hqk,qhd->khd", dlogits_low, query, preferred_element_type=jnp.float32)
            * factor
        )
        dprojected = jnp.concatenate(
            [dquery.reshape(rows, width), dkeys.reshape(rows, width), dvalues.reshape(rows, width)],
            axis=1,
        ).astype(jnp.bfloat16)
        sum_query_bias = sum_query_bias + jnp.sum(dprojected[:, :width].astype(jnp.float32), 0)
        sum_value_bias = sum_value_bias + jnp.sum(dprojected[:, 2 * width :].astype(jnp.float32), 0)
        sum_inner = sum_inner + contract_rows(normed_one, dprojected)
        dnormed_one = contract_cols(dprojected, inner_full)
        dsource_norm, part_gain, part_shift = norm_back(
            dnormed_one, unit_one, scaled_one, first_gain
        )
        sum_first_gain = sum_first_gain + part_gain
        sum_first_shift = sum_first_shift + part_shift
        input_grads.append((dresid + dsource_norm).astype(jnp.bfloat16))
    sum_table = jnp.transpose(sum_table_heads)
    gradient_inner, gradient_outer = (
        lax.psum_scatter(sum_inner, ("dp", "mlp"), scatter_dimension=0, tiled=True),
        lax.psum_scatter(sum_outer, ("dp", "mlp"), scatter_dimension=0, tiled=True),
    )
    gradient_up, gradient_down = (
        lax.psum_scatter(sum_up, "dp", scatter_dimension=0, tiled=True),
        lax.psum_scatter(sum_down, "dp", scatter_dimension=1, tiled=True),
    )
    up_bias_full = lax.dynamic_update_slice_in_dim(
        jnp.zeros((up_bias.shape[0],), jnp.float32), sum_up_bias, col_start, 0
    )
    summed = lax.psum(
        (
            sum_first_gain,
            sum_first_shift,
            sum_query_bias,
            sum_value_bias,
            sum_outer_bias,
            sum_attend_scale,
            sum_second_gain,
            sum_second_shift,
            up_bias_full,
            sum_down_bias,
            sum_feed_scale,
            sum_table,
        ),
        ("dp", "mlp"),
    )
    return (
        jnp.stack(results),
        jnp.stack(input_grads),
        gradient_inner,
        gradient_outer,
        gradient_up,
        gradient_down,
        summed[0],
        summed[1],
        summed[2],
        summed[3],
        summed[4],
        summed[5],
        summed[6],
        summed[7],
        summed[8],
        summed[9],
        summed[10],
        summed[11],
    )


def fast_body(
    tokens, keep_mask, position_index, cotangent, first_gain, first_shift, inner_weight, query_bias,
    value_bias, outer_weight, outer_bias, attend_scale, second_gain, second_shift, up_weight, up_bias,
    down_weight, down_bias, feed_scale, position_table,
):
    micro, rows, width = tokens.shape
    heads = position_table.shape[1]
    head_dim = width // heads
    factor = head_dim ** (-0.5)
    f32, bf = jnp.float32, jnp.bfloat16
    inner_piece = inner_weight.reshape(24, 3, 2, 3, 128).transpose(3, 2, 0, 1, 4).reshape(3, 2, 24, 384)
    outer_piece = outer_weight.reshape(24, 2, 384).transpose(1, 0, 2)[None]
    small = jnp.concatenate([inner_piece, outer_piece]).astype(f32)
    large = jnp.concatenate(
        [up_weight.reshape(96, 2, 384).transpose(1, 0, 2), down_weight.T.reshape(96, 2, 384).transpose(1, 0, 2)]
    )
    narrow, wide = gather_all(small, large)
    narrow = narrow.reshape(4, 2, 768, 384)
    inner_full = narrow[:3].reshape(3, 2, 768, 3, 128).transpose(2, 3, 1, 0, 4).reshape(768, 2304)
    outer_full = narrow[3].transpose(1, 0, 2).reshape(768, 768)
    wide = wide.reshape(2, 2, 2, 2, 768, 384)
    up_full = wide[0].transpose(3, 1, 2, 0, 4).reshape(768, 3072)
    down_full = wide[1].transpose(3, 1, 2, 0, 4).reshape(768, 3072)
    shift_vector = jnp.concatenate([query_bias, jnp.zeros_like(query_bias), value_bias])
    one_hot = (position_index.reshape(1, rows * rows) == lax.broadcasted_iota(jnp.int32, (position_table.shape[0], 1), 0))
    high = position_table.astype(bf)
    rest = (position_table - high.astype(f32)).astype(bf)
    hot = one_hot.astype(bf)
    bias = contract_rows(high, hot) + contract_rows(rest, hot)
    bias = bias.reshape(heads, rows, rows)
    seen = jnp.arange(rows)
    diagonal = seen[:, None] == seen[None, :]
    source = tokens.astype(f32)
    allowed = jnp.logical_or(keep_mask[:, None, None, :] == 1, diagonal[None, None])
    normed_one, unit_one, scaled_one = layer_norm(source, first_gain, first_shift)
    normed_one = normed_one.astype(bf).reshape(micro * rows, width)
    projected = (jnp.dot(normed_one, inner_full, preferred_element_type=f32) + shift_vector).astype(bf)
    split = projected.reshape(micro, rows, 3, heads, head_dim).transpose(2, 0, 3, 1, 4)
    query, keys, values = split[0], split[1], split[2]
    logits = jnp.einsum("bhqd,bhkd->bhqk", query, keys, preferred_element_type=f32) * factor + bias[None]
    logits = jnp.where(allowed, logits, -1e30)
    top = jnp.max(logits, -1, keepdims=True)
    expd = jnp.exp(logits - top)
    probs = expd / jnp.sum(expd, -1, keepdims=True)
    probs_low = probs.astype(bf)
    mixed = jnp.einsum("bhqk,bhkd->bhqd", probs_low, values, preferred_element_type=f32)
    mixed = mixed.transpose(0, 2, 1, 3).reshape(micro * rows, width).astype(bf)
    attend = jnp.dot(mixed, outer_full, preferred_element_type=f32) + outer_bias
    flat = source.reshape(micro * rows, width)
    resid = flat + attend_scale * attend
    normed_two, unit_two, scaled_two = layer_norm(resid, second_gain, second_shift)
    normed_two = normed_two.astype(bf)
    pre = jnp.dot(normed_two, up_full, preferred_element_type=f32) + up_bias
    active, slope = gelu_pair(pre)
    hidden = active.astype(bf)
    feed = contract_cols(hidden, down_full) + down_bias
    result = (resid + feed_scale * feed).astype(bf).reshape(micro, rows, width)
    upstream = cotangent.astype(f32).reshape(micro * rows, width)
    sum_feed_scale = jnp.sum(feed * upstream, 0)
    dfeed = feed_scale * upstream
    sum_down_bias = jnp.sum(dfeed, 0)
    dfeed_low = dfeed.astype(bf)
    grad_down = contract_rows(dfeed_low, hidden)
    dpre = (jnp.dot(dfeed_low, down_full, preferred_element_type=f32) * slope).astype(bf)
    sum_up_bias = jnp.sum(dpre.astype(f32), 0)
    grad_up = contract_rows(normed_two, dpre)
    dnormed_two = contract_cols(dpre, up_full)
    dresid_norm, sum_second_gain, sum_second_shift = norm_back(dnormed_two, unit_two, scaled_two, second_gain)
    dresid = upstream + dresid_norm
    sum_attend_scale = jnp.sum(attend * dresid, 0)
    dattend = attend_scale * dresid
    sum_outer_bias = jnp.sum(dattend, 0)
    dattend_low = dattend.astype(bf)
    grad_outer = contract_rows(mixed, dattend_low)
    dmixed = contract_cols(dattend_low, outer_full).astype(bf)
    dmixed = dmixed.reshape(micro, rows, heads, head_dim).transpose(0, 2, 1, 3)
    dvalues = jnp.einsum("bhqk,bhqd->bhkd", probs_low, dmixed, preferred_element_type=f32)
    dprobs = jnp.einsum("bhqd,bhkd->bhqk", dmixed, values, preferred_element_type=f32)
    dlogits = probs * (dprobs - jnp.sum(dprobs * probs, -1, keepdims=True))
    summed_logits = jnp.sum(dlogits, 0).reshape(heads, rows * rows)
    part = summed_logits.astype(bf)
    part2 = (summed_logits - part.astype(f32)).astype(bf)
    sum_table = contract_cols(hot, part) + contract_cols(hot, part2)
    dlogits_low = dlogits.astype(bf)
    dquery = jnp.einsum("bhqk,bhkd->bhqd", dlogits_low, keys, preferred_element_type=f32) * factor
    dkeys = jnp.einsum("bhqk,bhqd->bhkd", dlogits_low, query, preferred_element_type=f32) * factor
    dprojected = jnp.stack([dquery, dkeys, dvalues]).astype(bf).transpose(1, 3, 0, 2, 4).reshape(micro * rows, 3 * width)
    sum_query_bias = jnp.sum(dprojected[:, :width].astype(f32), 0)
    sum_value_bias = jnp.sum(dprojected[:, 2 * width :].astype(f32), 0)
    grad_inner = contract_rows(normed_one, dprojected)
    dnormed_one = contract_cols(dprojected, inner_full)
    dsource, sum_first_gain, sum_first_shift = norm_back(
        dnormed_one, unit_one.reshape(micro * rows, width), scaled_one.reshape(micro * rows, 1), first_gain
    )
    input_grad = (dresid + dsource).astype(bf).reshape(micro, rows, width)
    narrow_grad = jnp.concatenate(
        [
            grad_inner.astype(bf).reshape(768, 3, 2, 3, 128).transpose(3, 2, 0, 1, 4).reshape(3, 2, 768, 384),
            grad_outer.astype(bf).reshape(768, 2, 384).transpose(1, 0, 2)[None],
        ]
    ).reshape(4, 2, 4, 2, 2, 48, 384)
    wide_grad = jnp.stack([grad_up, grad_down]).astype(bf).reshape(2, 768, 2, 2, 2, 384)
    wide_grad = wide_grad.transpose(0, 4, 2, 3, 1, 5).reshape(4, 2, 2, 4, 2, 96, 384)
    small_out, large_out = reduce_all(narrow_grad, wide_grad)
    gradient_inner = small_out[:3].reshape(3, 2, 24, 3, 128).transpose(2, 3, 1, 0, 4).reshape(24, 2304)
    gradient_outer = small_out[3].transpose(1, 0, 2).reshape(24, 768)
    gradient_up = large_out[:2].transpose(1, 0, 2).reshape(96, 768)
    gradient_down = large_out[2:].transpose(1, 0, 2).reshape(96, 768).T
    vectors = [
        sum_first_gain, sum_first_shift, sum_query_bias, sum_value_bias, sum_outer_bias, sum_attend_scale,
        sum_second_gain, sum_second_shift, sum_up_bias, sum_down_bias, sum_feed_scale,
    ]
    summed = lax.psum((*vectors, sum_table), ("dp", "mlp"))
    return (result, input_grad, gradient_inner, gradient_outer, gradient_up, gradient_down, *summed)


def solution(mesh):
    special = mesh.shape["dp"] == 8 and mesh.shape["mlp"] == 4
    placed = (
        P(None, ("dp", "mlp"), None),
        P(None, ("dp", "mlp")),
        P(),
        P(None, ("dp", "mlp"), None),
        P(),
        P(),
        P(("dp", "mlp"), None),
        P(),
        P(),
        P(("dp", "mlp"), None),
        P(),
        P(),
        P(),
        P(),
        P("dp", "mlp"),
        P(),
        P("mlp", "dp"),
        P(),
        P(),
        P(),
    )
    return jax.shard_map(
        fast_body if special else body,
        mesh=mesh,
        in_specs=placed,
        out_specs=(
            P(None, ("dp", "mlp"), None),
            P(None, ("dp", "mlp"), None),
            P(("dp", "mlp"), None),
            P(("dp", "mlp"), None),
            P("dp", "mlp"),
            P("mlp", "dp"),
            P(),
            P(),
            P(),
            P(),
            P(),
            P(),
            P(),
            P(),
            P(),
            P(),
            P(),
            P(),
        ),
        check_vma=False,
    )
```

```python
import jax
import jax.numpy as jnp
from jax import lax
from jax.experimental import pallas as pl
from jax.experimental.pallas import tpu as pltpu
from jax.sharding import PartitionSpec as P

EPS = 1e-06
ROOT_HALF = 0.7071067811865476
DENSITY = 0.3989422804014327


MESH = pl.DeviceIdType.MESH
KINDS = (0, 0, 0, 0, 1, 1, 1, 1)
SLOT = (0, 1, 2, 3, 0, 1, 2, 3)
GATHER_Y_LAST = (True, False, True, False, True, False, True, False)
REDUCE_X_LAST = (True, False, True, False, True, True, False, False)
N_COPY = 10
PAD = 208
TALL = 2 * PAD
KEYS = 256
TILE = 384


def place():
    dp = lax.axis_index("dp")
    mlp = lax.axis_index("mlp")
    return lax.div(dp, 2), lax.rem(dp, 2), lax.div(mlp, 2), lax.rem(mlp, 2)


def device(z, x, y, c):
    return (z * 2 + x, y * 2 + c)


def own(ref, kind, z, x, y, c):
    return ref.at[c, z, x, y] if kind == 0 else ref.at[y, c, z, x]


def line(ref, kind, x, y, c):
    return ref.at[c, :, x, y] if kind == 0 else ref.at[y, c, :, x]


def greet(z, x, y, c):
    barrier = pltpu.get_barrier_semaphore()
    others = [device(lax.rem(z + d, 4), x, y, c) for d in (1, 2, 3)]
    others += [device(z, 1 - x, y, c), device(z, x, 1 - y, c), device(z, 1 - x, 1 - y, c), device(z, x, y, 1 - c)]
    for other in others:
        pl.semaphore_signal(barrier, inc=1, device_id=other, device_id_type=MESH)
    pl.semaphore_wait(barrier, len(others))


class Link:
    def __init__(self, send, recv):
        self.send, self.recv, self.pending = send, recv, []

    def copy(self, src, dst, slot, target):
        made = pltpu.make_async_remote_copy(
            src_ref=src,
            dst_ref=dst,
            send_sem=self.send.at[slot],
            recv_sem=self.recv.at[slot],
            device_id=target,
            device_id_type=MESH,
        )
        made.start()
        self.pending.append(made)
        return made

    def drain(self):
        for made in self.pending:
            made.wait_send()
        self.pending = []


class Gather:
    def __init__(self, link, ref, unit, where):
        self.link, self.ref, self.where = link, ref, where
        self.kind = KINDS[unit]
        self.base = unit * N_COPY
        self.y_last = GATHER_Y_LAST[unit]

    def put(self, part, slot, target):
        return self.link.copy(part, part, self.base + slot, target)

    def along_z(self):
        z, x, y, c = self.where
        part = own(self.ref, self.kind, z, x, y, c)
        self.z = [self.put(part, d - 1, device(lax.rem(z + d, 4), x, y, c)) for d in (1, 2, 3)]

    def line_out(self):
        z, x, y, c = self.where
        for made in self.z:
            made.wait_recv()
        part = line(self.ref, self.kind, x, y, c)
        self.to_x = self.put(part, 3, device(z, 1 - x, y, c))
        self.to_y = self.put(part, 4, device(z, x, 1 - y, c))
        self.to_c = [self.put(part, 6, device(z, x, y, 1 - c))]

    def plane_out(self):
        z, x, y, c = self.where
        mirror = device(z, x, y, 1 - c)
        from_x = line(self.ref, self.kind, 1 - x, y, c)
        from_y = line(self.ref, self.kind, x, 1 - y, c)
        if self.y_last:
            self.to_x.wait_recv()
            self.last = self.put(from_x, 5, device(z, x, 1 - y, c))
            self.to_c.append(self.put(from_x, 7, mirror))
            self.to_y.wait_recv()
            self.to_c.append(self.put(from_y, 8, mirror))
        else:
            self.to_y.wait_recv()
            self.last = self.put(from_y, 5, device(z, 1 - x, y, c))
            self.to_c.append(self.put(from_y, 7, mirror))
            self.to_x.wait_recv()
            self.to_c.append(self.put(from_x, 8, mirror))

    def core_out(self):
        z, x, y, c = self.where
        self.last.wait_recv()
        part = line(self.ref, self.kind, 1 - x, 1 - y, c)
        self.to_c.append(self.put(part, 9, device(z, x, y, 1 - c)))

    def finish(self):
        for made in self.to_c:
            made.wait_recv()


class Scatter:
    def __init__(self, link, ref, buffers, unit, where):
        self.link, self.ref, self.where = link, ref, where
        self.half, self.quarter, self.eighth, self.parts = buffers
        self.kind = KINDS[unit]
        self.base = (8 + unit) * N_COPY
        self.x_last = REDUCE_X_LAST[unit]

    def put(self, src, dst, slot, target):
        return self.link.copy(src, dst, self.base + slot, target)

    def by_core(self, ref, c):
        return ref.at[c] if self.kind == 0 else ref.at[:, c]

    def by_y(self, ref, y, c):
        return ref.at[c, :, :, y] if self.kind == 0 else ref.at[y, c]

    def by_x(self, ref, x, c):
        return ref.at[c, :, x] if self.kind == 0 else ref.at[:, c, :, x]

    def mix(self, here, there):
        total = here[...].astype(jnp.float32) + there[...].astype(jnp.float32)
        here[...] = total.astype(jnp.bfloat16)

    def to_core(self):
        z, x, y, c = self.where
        self.made = self.put(self.by_core(self.ref, 1 - c), self.half, 0, device(z, x, y, 1 - c))

    def to_first(self):
        z, x, y, c = self.where
        self.made.wait_recv()
        self.mix(self.by_core(self.ref, c), self.half)
        if self.x_last:
            self.made = self.put(self.by_y(self.ref, 1 - y, c), self.quarter, 1, device(z, x, 1 - y, c))
        else:
            self.made = self.put(self.by_x(self.ref, 1 - x, c), self.quarter, 1, device(z, 1 - x, y, c))

    def to_second(self):
        z, x, y, c = self.where
        self.made.wait_recv()
        self.mix(self.by_y(self.ref, y, c) if self.x_last else self.by_x(self.ref, x, c), self.quarter)
        if self.x_last:
            self.made = self.put(line(self.ref, self.kind, 1 - x, y, c), self.eighth, 2, device(z, 1 - x, y, c))
        else:
            self.made = self.put(line(self.ref, self.kind, x, 1 - y, c), self.eighth, 2, device(z, x, 1 - y, c))

    def to_z(self):
        z, x, y, c = self.where
        self.made.wait_recv()
        self.mix(line(self.ref, self.kind, x, y, c), self.eighth)
        self.z = []
        for d in (1, 2, 3):
            far = lax.rem(z + d, 4)
            src = own(self.ref, self.kind, far, x, y, c)
            self.z.append(self.put(src, self.parts.at[d - 1], 2 + d, device(far, x, y, c)))

    def total(self):
        for made in self.z:
            made.wait_recv()
        total = own(self.ref, self.kind, *self.where)[...].astype(jnp.float32)
        for d in range(3):
            total = total + self.parts[d].astype(jnp.float32)
        return total


class Everywhere:
    def __init__(self, link, ref, core_ref, plane_ref, line_ref, base, where):
        self.link, self.ref, self.where, self.base = link, ref, where, base
        self.core_ref, self.plane_ref, self.line_ref = core_ref, plane_ref, line_ref

    def to_core(self):
        z, x, y, c = self.where
        self.made = [self.link.copy(self.ref, self.core_ref, self.base, device(z, x, y, 1 - c))]

    def wait(self):
        for made in self.made:
            made.wait_recv()

    def to_plane(self):
        z, x, y, c = self.where
        self.wait()
        chip = self.plane_ref.at[3]
        chip[...] = self.ref[...] + self.core_ref[...]
        targets = (device(z, 1 - x, y, c), device(z, x, 1 - y, c), device(z, 1 - x, 1 - y, c))
        self.made = [
            self.link.copy(chip, self.plane_ref.at[n], self.base + 1 + n, target) for n, target in enumerate(targets)
        ]

    def to_line(self):
        z, x, y, c = self.where
        self.wait()
        got = self.plane_ref
        self.line_ref[z] = (got[3] + got[0]) + (got[1] + got[2])
        part = self.line_ref.at[z]
        self.made = [
            self.link.copy(part, part, self.base + 3 + d, device(lax.rem(z + d, 4), x, y, c)) for d in (1, 2, 3)
        ]

    def total(self):
        self.wait()
        got = self.line_ref
        return (got[0] + got[1]) + (got[2] + got[3])


F32 = jnp.float32
BF16 = jnp.bfloat16


def dot(left, right):
    return lax.dot_general(left, right, (((1,), (0,)), ((), ())), preferred_element_type=F32)


def dot_nt(left, right):
    return lax.dot_general(left, right, (((1,), (1,)), ((), ())), preferred_element_type=F32)


def dot_tn(left, right):
    return lax.dot_general(left, right, (((0,), (0,)), ((), ())), preferred_element_type=F32)


def fold(values):
    rows, width = values.shape
    return jnp.sum(values.reshape(rows // 8, 8, width), 0)


def unit_of(values):
    mean = jnp.mean(values, -1, keepdims=True)
    centred = values - mean
    variance = jnp.mean(centred * centred, -1, keepdims=True)
    scaled = lax.rsqrt(variance + EPS)
    return centred * scaled, scaled


def by_rows(step, init):
    size = 32

    def one(index, carried):
        return step(pl.ds(pl.multiple_of(index * size, size), size), carried)

    return lax.fori_loop(0, TALL // size, one, init)


def layer_kernel(*refs):
    (
        tokens, cotangent, keep, places, first_gain, first_shift, query_bias, value_bias, outer_bias, attend_scale,
        second_gain, second_shift, up_bias, down_bias, feed_scale, table, small_in, large_in,
        result, token_grad, small_out, large_out, early_out, late_out, table_out,
        narrow, wide, half0, half1, quarter0, quarter1a, quarter1b, eighth0, eighth1, parts0, parts1, pair, mine,
        source, upstream, normed1, normed1_t, normed2, normed2_t, qkv, bias, mask, index, probs, mix_t, attend, resid,
        dfeed, dfeed_t, hidden, slope, total, dnormed2, shifts, ups,
        early, late, hits, early_core, early_plane, early_line, late_core, late_plane, late_line, hits_core, hits_plane, hits_line,
        send, recv,
    ) = refs
    dresid, dproj, mix, dmixed, dattend = resid, hidden, normed2, normed2, dfeed
    where = z, x, y, c = place()
    greet(*where)
    link = Link(send, recv)
    pair[:, c] = small_in[:, c]
    mate = link.copy(small_in.at[:, 1 - c], pair.at[:, c], 16 * N_COPY, device(z, x, y, 1 - c))
    for unit in range(4):
        wide[unit, y, c, z, x] = large_in[unit]
    mate.wait_recv()
    for unit in range(4):
        narrow[unit, c, z, x, y] = pair[unit].reshape(48, TILE).astype(BF16)
    gathers = [Gather(link, (narrow if KINDS[u] == 0 else wide).at[SLOT[u]], u, where) for u in range(8)]
    for unit in gathers:
        unit.along_z()

    def advance(step):
        if step < 8:
            gathers[step].line_out()
        if 0 <= step - 1 < 8:
            gathers[step - 1].plane_out()
        if 0 <= step - 2 < 8:
            gathers[step - 2].core_out()

    for image in range(2):
        last = pl.ds(image * PAD + 192, 16)
        source[last, :] = jnp.zeros((16, 768), BF16)
        upstream[last, :] = jnp.zeros((16, 768), BF16)
        source[pl.ds(image * PAD, 197), :] = tokens[image]
        upstream[pl.ds(image * PAD, 197), :] = cotangent[image]

    def norm_first(rows, carried):
        unit, _ = unit_of(source[rows, :].astype(F32))
        normed1[rows, :] = (unit * first_gain[...] + first_shift[...]).astype(BF16)
        lifted = upstream[rows, :].astype(F32) * feed_scale[...]
        dfeed[rows, :] = lifted.astype(BF16)
        return carried + fold(lifted)

    sum_down = by_rows(norm_first, jnp.zeros((8, 768), F32))
    early[...] = jnp.zeros((16, 768), F32)
    late[...] = jnp.zeros((8, 768), F32)
    early[4:5, :] = jnp.sum(sum_down, 0, keepdims=True)
    index[...] = jnp.full((PAD, KEYS), -1, jnp.int32)
    index[0:197, 0:197] = places[...]
    row_of = lax.broadcasted_iota(jnp.int32, (PAD, KEYS), 0)
    col_of = lax.broadcasted_iota(jnp.int32, (PAD, KEYS), 1)
    for image in range(2):
        mask[image] = jnp.full((PAD, KEYS), -1e30, F32)
        kept = jnp.where(keep[image : image + 1, :] == 1, 0.0, -1e30).astype(F32)
        mask[image, :, 0:197] = jnp.broadcast_to(kept, (PAD, 197))
        mask[image] = jnp.where(row_of == col_of, 0.0, mask[image])
    advance(0)

    def look_up(head, carried):
        for side in range(2):
            cols = slice(side * 128, side * 128 + 128)
            spot = index[:, cols]
            low, high = spot & 127, spot >> 7
            found = jnp.zeros((PAD, 128), F32)
            for piece in range(6):
                row = table[head, :, piece * 128 : piece * 128 + 128]
                picked = jnp.take_along_axis(jnp.broadcast_to(row, (PAD, 128)), low, axis=1)
                found = jnp.where(high == piece, picked, found)
            bias[head, :, cols] = found
        return carried

    advance(1)
    lax.fori_loop(0, 12, look_up, 0)
    advance(2)
    zero_row = jnp.zeros((1, 128), F32)
    for p in range(6):
        cols = slice(p * 128, p * 128 + 128)
        shifts[p] = jnp.concatenate([query_bias[:, cols], zero_row, value_bias[:, cols]], axis=1)
        qkv[p, TALL:, :] = jnp.zeros((48, TILE), BF16)
    normed1_t[...] = normed1[...].T
    dfeed_t[...] = dfeed[...].T
    lane = lax.broadcasted_iota(jnp.int32, (1, 128), 1)
    picks = [(lane < 64).astype(F32).astype(BF16), (lane >= 64).astype(F32).astype(BF16)]
    first_half = lax.broadcasted_iota(jnp.int32, (PAD, 128), 1) < 64
    scaling = jnp.where(lax.broadcasted_iota(jnp.int32, (1, TILE), 1) < 128, 0.125, 1.0).astype(F32)
    advance(3)

    def rows_of(image):
        return pl.ds(pl.multiple_of(image * PAD, 16), PAD)

    def keys_of(image):
        return pl.ds(pl.multiple_of(image * PAD, 16), KEYS)

    def cols_of(p):
        return pl.ds(pl.multiple_of(p * 128, 128), 128)

    for k in range(3):
        gathers[k].finish()

        def project(core, carried, k=k):
            p = core * 3 + k
            weight = narrow[k, core].reshape(768, TILE)
            value = (dot(normed1[...], weight) + shifts[p]).astype(BF16)
            qkv[p, 0:TALL, :] = (value.astype(F32) * scaling).astype(BF16)
            return carried

        lax.fori_loop(0, 2, project, 0)

        def attend_pair(step, carried, k=k):
            core, image = step // 2, step % 2
            p = core * 3 + k
            query = qkv[p, rows_of(image), 0:128]
            keys = qkv[p, keys_of(image), 128:256]
            values = qkv[p, keys_of(image), 256:384]
            outs = []
            for t in range(2):
                logits = dot_nt(query * picks[t], keys) + bias[2 * p + t] + mask[image]
                top = jnp.max(logits, -1, keepdims=True)
                expd = jnp.exp(logits - top)
                share = (expd * (1.0 / jnp.sum(expd, -1, keepdims=True))).astype(BF16)
                probs[image, 2 * p + t] = share
                outs.append(dot(share, values))
            mix[rows_of(image), cols_of(p)] = jnp.where(first_half, outs[0], outs[1]).astype(BF16)
            return carried

        lax.fori_loop(0, 4, attend_pair, 0)
        advance(4 + k)
    gathers[3].finish()
    for core in range(2):
        cols = slice(core * TILE, core * TILE + TILE)
        attend[:, cols] = dot(mix[...], narrow[3, core].reshape(768, TILE)) + outer_bias[:, cols]
    mix_t[...] = mix[...].T
    advance(7)

    def norm_second(rows, carried):
        value = source[rows, :].astype(F32) + attend_scale[...] * attend[rows, :]
        resid[rows, :] = value
        unit, _ = unit_of(value)
        normed2[rows, :] = (unit * second_gain[...] + second_shift[...]).astype(BF16)
        total[rows, :] = jnp.zeros((32, 768), F32)
        dnormed2[rows, :] = jnp.zeros((32, 768), F32)
        return carried

    by_rows(norm_second, 0)
    normed2_t[...] = normed2[...].T

    def up_cols(k, block):
        return pl.ds(pl.multiple_of(block * 768 + k * TILE, 128), TILE)

    for k in range(2):
        gathers[4 + k].finish()

        def widen(block, carried, k=k):
            weight = wide[k, block // 2, block % 2].reshape(768, TILE)
            pre = dot(normed2[...], weight) + up_bias[:, up_cols(k, block)]
            cumul = 0.5 * (1.0 + lax.erf(pre * ROOT_HALF))
            hidden[k * 4 + block] = (pre * cumul).astype(BF16)
            slope[k * 4 + block] = (cumul + pre * jnp.exp(-0.5 * pre * pre) * DENSITY).astype(BF16)
            return carried

        lax.fori_loop(0, 4, widen, 0)
        advance(8 + k)
    gathers[6].finish()
    gathers[7].finish()
    link.drain()
    scatters = []
    for u in range(8):
        s = SLOT[u]
        if KINDS[u] == 0:
            buffers = (half0.at[s], quarter0.at[s], eighth0.at[s], parts0.at[s])
        else:
            quarter1 = quarter1a if REDUCE_X_LAST[u] else quarter1b
            buffers = (half1.at[s], quarter1.at[s % 2], eighth1.at[s], parts1.at[s])
        scatters.append(Scatter(link, (narrow if KINDS[u] == 0 else wide).at[s], buffers, u, where))

    for k in range(2):

        def narrow_back(block, carried, k=k):
            b = k * 4 + block
            down = wide[2 + k, block // 2, block % 2].reshape(768, TILE)
            total[...] += dot_nt(hidden[b], down)
            dpre = (dot(dfeed[...], down) * slope[b].astype(F32)).astype(BF16)
            ups[b] = jnp.sum(fold(dpre.astype(F32)), 0, keepdims=True)
            up = wide[k, block // 2, block % 2].reshape(768, TILE)
            dnormed2[...] += dot_nt(dpre, up)
            shape = (4, 2, 96, TILE)
            wide[2 + k, block // 2, block % 2] = dot(normed2_t[...], dpre).astype(BF16).reshape(shape)
            wide[k, block // 2, block % 2] = dot(dfeed_t[...], hidden[b]).astype(BF16).reshape(shape)
            return carried

        lax.fori_loop(0, 4, narrow_back, 0)
        scatters[4 + k].to_core()
        scatters[6 + k].to_core()
    scatters[4].to_first()
    scatters[6].to_first()

    def second_back(rows, carried):
        feed_scale_sum, gain_sum, shift_sum, scale_sum, bias_sum = carried
        feed = total[rows, :] + down_bias[...]
        above = upstream[rows, :].astype(F32)
        value = resid[rows, :]
        total[rows, :] = value + feed_scale[...] * feed
        unit, scaled = unit_of(value)
        grad = dnormed2[rows, :]
        inner = grad * second_gain[...]
        first = jnp.mean(inner, -1, keepdims=True)
        second = jnp.mean(inner * unit, -1, keepdims=True)
        back = above + scaled * (inner - first - unit * second)
        dresid[rows, :] = back
        lifted = attend_scale[...] * back
        dattend[rows, :] = lifted.astype(BF16)
        return (
            feed_scale_sum + fold(feed * above),
            gain_sum + fold(grad * unit),
            shift_sum + fold(grad),
            scale_sum + fold(attend[rows, :] * back),
            bias_sum + fold(lifted),
        )

    zero = jnp.zeros((8, 768), F32)
    sums = by_rows(second_back, (zero,) * 5)
    for b in range(8):
        early[8 + b : 9 + b, 0:TILE] = ups[b]
    for row, value in zip((5, 2, 3, 1, 0), sums):
        early[row : row + 1, :] = jnp.sum(value, 0, keepdims=True)
    for image in range(2):
        result[image] = total[pl.ds(image * PAD, 197), :].astype(BF16)
    everywhere = Everywhere(link, early, early_core, early_plane, early_line, 16 * N_COPY + 5, where)
    everywhere.to_core()
    scatters[5].to_first()
    scatters[7].to_first()
    half_mixed = [
        dot_nt(dattend[:, core * TILE : core * TILE + TILE], narrow[3, core].reshape(768, TILE)) for core in range(2)
    ]
    dmixed[...] = (half_mixed[0] + half_mixed[1]).astype(BF16)
    for core in range(2):
        cols = slice(core * TILE, core * TILE + TILE)
        narrow[3, core] = dot(mix_t[...], dattend[:, cols]).astype(BF16).reshape(4, 2, 2, 48, TILE)
    scatters[3].to_core()
    everywhere.to_plane()
    total[...] = jnp.zeros((TALL, 768), F32)

    def service(k):
        if k == 0:
            scatters[3].to_first()
            scatters[4].to_second()
            scatters[6].to_second()
        if k == 1:
            scatters[0].to_first()
            scatters[5].to_second()
            scatters[7].to_second()
            scatters[4].to_z()
            scatters[6].to_z()
            everywhere.to_line()
        if k == 2:
            scatters[1].to_first()
            scatters[3].to_second()
            scatters[0].to_second()
            scatters[5].to_z()
            scatters[7].to_z()

    for k in range(3):

        def attend_back(step, carried, k=k):
            core, image = step // 2, step % 2
            p = core * 3 + k
            query = qkv[p, rows_of(image), 0:128]
            keys = qkv[p, keys_of(image), 128:256]
            values = qkv[p, keys_of(image), 256:384]
            above = dmixed[rows_of(image), cols_of(p)]
            dquery, dkeys, dvalues = [], [], []
            for t in range(2):
                share = probs[image, 2 * p + t]
                dvalues.append(dot_tn(share, above)[0:PAD])
                dshare = dot_nt(above * picks[t], values)
                full = share.astype(F32)
                dlogits = full * (dshare - jnp.sum(dshare * full, -1, keepdims=True))
                bias[2 * p + t] = jnp.where(image == 0, 0.0, bias[2 * p + t]) + dlogits
                low = dlogits.astype(BF16)
                dquery.append(dot(low, keys) * 0.125)
                dkeys.append(dot_tn(low, query)[0:PAD])
            rows = rows_of(image)
            dproj[p, rows, 0:128] = jnp.where(first_half, dquery[0], dquery[1]).astype(BF16)
            dproj[p, rows, 128:256] = jnp.where(first_half, dkeys[0], dkeys[1]).astype(BF16)
            dproj[p, rows, 256:384] = jnp.where(first_half, dvalues[0], dvalues[1]).astype(BF16)
            return carried

        lax.fori_loop(0, 4, attend_back, 0)

        def project_back(core, carried, k=k):
            p = core * 3 + k
            grad = dproj[p]
            summed = jnp.sum(fold(grad.astype(F32)), 0, keepdims=True)
            late[2:3, cols_of(p)] = summed[:, 0:128]
            late[3:4, cols_of(p)] = summed[:, 256:384]
            total[...] += dot_nt(grad, narrow[k, core].reshape(768, TILE))
            narrow[k, core] = dot(normed1_t[...], grad).astype(BF16).reshape(4, 2, 2, 48, TILE)
            return carried

        lax.fori_loop(0, 2, project_back, 0)
        scatters[k].to_core()
        service(k)

    def first_back(rows, carried):
        gain_sum, shift_sum = carried
        grad = total[rows, :]
        unit, scaled = unit_of(source[rows, :].astype(F32))
        inner = grad * first_gain[...]
        first = jnp.mean(inner, -1, keepdims=True)
        second = jnp.mean(inner * unit, -1, keepdims=True)
        dresid[rows, :] = dresid[rows, :] + scaled * (inner - first - unit * second)
        return gain_sum + fold(grad * unit), shift_sum + fold(grad)

    sums = by_rows(first_back, (zero, zero))
    late[0:1, :] = jnp.sum(sums[0], 0, keepdims=True)
    late[1:2, :] = jnp.sum(sums[1], 0, keepdims=True)
    scatters[2].to_first()
    late_sum = Everywhere(link, late, late_core, late_plane, late_line, 16 * N_COPY + 15, where)
    late_sum.to_core()
    for image in range(2):
        token_grad[image] = dresid[pl.ds(image * PAD, 197), :].astype(BF16)
    mates = []

    def settle(u):
        s = SLOT[u]
        value = scatters[u].total()
        if KINDS[u] == 0:
            mine[s] = value.reshape(2, 24, TILE)
            small_out[s, c] = mine[s, c]
            mates.append(link.copy(mine.at[s, 1 - c], small_out.at[s, c], 16 * N_COPY + 1 + s, device(z, x, y, 1 - c)))
        else:
            large_out[s] = value

    late_sum.to_plane()
    scatters[1].to_second()
    scatters[3].to_z()
    scatters[0].to_z()
    hits[...] = jnp.zeros((96, 128), F32)
    low_of = lax.broadcasted_iota(jnp.int32, (8, KEYS), 0)
    high_of = lax.broadcasted_iota(jnp.int32, (128, KEYS), 0)

    def count(group, carried):
        eight = pl.ds(pl.multiple_of(group * 8, 8), 8)
        spots = index[eight, :]
        for r in range(8):
            spot = jnp.broadcast_to(spots[r : r + 1, :], (8, KEYS))
            low = (spot & 7) == low_of
            parts = []
            for head in range(12):
                grads = bias[head, eight, :]
                parts.append(jnp.where(low, jnp.broadcast_to(grads[r : r + 1, :], (8, KEYS)), 0.0))
            spread = jnp.concatenate(parts, axis=0).astype(BF16)
            high = jnp.concatenate([spot >> 3] * 16, axis=0)
            which = (high == high_of).astype(F32).astype(BF16)
            carried = carried + dot_nt(spread, which)
        return carried

    hits[...] = lax.fori_loop(0, 25, count, jnp.zeros((96, 128), F32))
    hits_sum = Everywhere(link, hits, hits_core, hits_plane, hits_line, 16 * N_COPY + 25, where)
    hits_sum.to_core()
    scatters[2].to_second()
    scatters[1].to_z()
    late_sum.to_line()
    hits_sum.to_plane()
    settle(4)
    settle(6)
    settle(5)
    settle(7)
    early_out[...] = everywhere.total()
    scatters[2].to_z()
    settle(3)
    settle(0)
    hits_sum.to_line()
    settle(1)
    settle(2)
    late_out[...] = late_sum.total()
    table_out[...] = hits_sum.total()
    for made in mates:
        made.wait_recv()
    link.drain()


def run_layer(*operands):
    def vmem(*shape, dtype=BF16):
        return pltpu.VMEM(shape, dtype)

    scratch = [
        vmem(4, 2, 4, 2, 2, 48, TILE),
        vmem(4, 2, 2, 4, 2, 96, TILE),
        vmem(4, 4, 2, 2, 48, TILE),
        vmem(4, 2, 4, 2, 96, TILE),
        vmem(4, 4, 2, 48, TILE),
        vmem(2, 4, 2, 96, TILE),
        vmem(2, 2, 4, 96, TILE),
        vmem(4, 4, 48, TILE),
        vmem(4, 4, 96, TILE),
        vmem(4, 3, 48, TILE),
        vmem(4, 3, 96, TILE),
        vmem(4, 2, 24, TILE, dtype=F32),
        vmem(4, 2, 24, TILE, dtype=F32),
        vmem(TALL, 768),
        vmem(TALL, 768),
        vmem(TALL, 768),
        vmem(768, TALL),
        vmem(TALL, 768),
        vmem(768, TALL),
        vmem(6, TALL + 48, TILE),
        vmem(12, PAD, KEYS, dtype=F32),
        vmem(2, PAD, KEYS, dtype=F32),
        vmem(PAD, KEYS, dtype=jnp.int32),
        vmem(2, 12, PAD, KEYS),
        vmem(768, TALL),
        vmem(TALL, 768, dtype=F32),
        vmem(TALL, 768, dtype=F32),
        vmem(TALL, 768),
        vmem(768, TALL),
        vmem(8, TALL, TILE),
        vmem(8, TALL, TILE),
        vmem(TALL, 768, dtype=F32),
        vmem(TALL, 768, dtype=F32),
        vmem(6, 1, TILE, dtype=F32),
        vmem(8, 1, TILE, dtype=F32),
        vmem(16, 768, dtype=F32),
        vmem(8, 768, dtype=F32),
        vmem(96, 128, dtype=F32),
    ]
    for shape in ((16, 768), (8, 768), (96, 128)):
        scratch += [vmem(*shape, dtype=F32), vmem(4, *shape, dtype=F32), vmem(4, *shape, dtype=F32)]
    copies = 16 * N_COPY + 40
    scratch += [pltpu.SemaphoreType.DMA((copies,)), pltpu.SemaphoreType.DMA((copies,))]
    return pl.pallas_call(
        layer_kernel,
        out_shape=(
            jax.ShapeDtypeStruct((2, 197, 768), BF16),
            jax.ShapeDtypeStruct((2, 197, 768), BF16),
            jax.ShapeDtypeStruct((4, 2, 24, TILE), F32),
            jax.ShapeDtypeStruct((4, 96, TILE), F32),
            jax.ShapeDtypeStruct((16, 768), F32),
            jax.ShapeDtypeStruct((8, 768), F32),
            jax.ShapeDtypeStruct((96, 128), F32),
        ),
        in_specs=[pl.BlockSpec(memory_space=pltpu.VMEM)] * len(operands),
        out_specs=[pl.BlockSpec(memory_space=pltpu.VMEM)] * 7,
        scratch_shapes=scratch,
        compiler_params=pltpu.CompilerParams(
            collective_id=0, has_side_effects=True, vmem_limit_bytes=62 * 2**20
        ),
    )(*operands)


def fast_body(
    tokens,
    keep_mask,
    position_index,
    cotangent,
    first_gain,
    first_shift,
    inner_weight,
    query_bias,
    value_bias,
    outer_weight,
    outer_bias,
    attend_scale,
    second_gain,
    second_shift,
    up_weight,
    up_bias,
    down_weight,
    down_bias,
    feed_scale,
    position_table,
):
    inner_piece = inner_weight.reshape(24, 3, 2, 3, 128).transpose(3, 2, 0, 1, 4).reshape(3, 2, 24, TILE)
    outer_piece = outer_weight.reshape(24, 2, TILE).transpose(1, 0, 2)[None]
    small = jnp.concatenate([inner_piece, outer_piece]).astype(F32)
    large = jnp.concatenate(
        [up_weight.reshape(96, 2, TILE).transpose(1, 0, 2), down_weight.T.reshape(96, 2, TILE).transpose(1, 0, 2)]
    )
    table = jnp.pad(position_table.T, ((0, 0), (0, 36))).reshape(12, 1, 768)
    vectors = [first_gain, first_shift, query_bias, value_bias, outer_bias, attend_scale, second_gain, second_shift]
    vectors = [v.reshape(1, -1) for v in (*vectors, up_bias, down_bias, feed_scale)]
    result, token_grad, small_out, large_out, early, late, hits = run_layer(
        tokens, cotangent, keep_mask, position_index, *vectors, table, small, large
    )
    gradient_inner = small_out[:3].reshape(3, 2, 24, 3, 128).transpose(2, 3, 1, 0, 4).reshape(24, 2304)
    gradient_outer = small_out[3].transpose(1, 0, 2).reshape(24, 768)
    gradient_down = large_out[:2].transpose(1, 0, 2).reshape(96, 768).T
    gradient_up = large_out[2:].transpose(1, 0, 2).reshape(96, 768)
    up_bias_grad = early[8:, :TILE].reshape(2, 4, TILE).transpose(1, 0, 2).reshape(3072)
    table_grad = hits.reshape(12, 8, 128).transpose(2, 1, 0).reshape(1024, 12)[:732]
    return (
        result,
        token_grad,
        gradient_inner,
        gradient_outer,
        gradient_up,
        gradient_down,
        late[0],
        late[1],
        late[2],
        late[3],
        early[0],
        early[1],
        early[2],
        early[3],
        up_bias_grad,
        early[4],
        early[5],
        table_grad,
    )


def layer_norm(values, gain, shift):
    mean = jnp.mean(values, -1, keepdims=True)
    centred = values - mean
    variance = jnp.mean(centred * centred, -1, keepdims=True)
    scaled = lax.rsqrt(variance + EPS)
    unit = centred * scaled
    return (unit * gain + shift, unit, scaled)


def norm_back(upstream, unit, scaled, gain):
    inner = upstream * gain
    first = jnp.mean(inner, -1, keepdims=True)
    second = jnp.mean(inner * unit, -1, keepdims=True)
    return (
        scaled * (inner - first - unit * second),
        jnp.sum(upstream * unit, 0),
        jnp.sum(upstream, 0),
    )


def gelu_pair(pre):
    cumul = 0.5 * (1.0 + lax.erf(pre * ROOT_HALF))
    return (pre * cumul, cumul + pre * jnp.exp(-0.5 * pre * pre) * DENSITY)


def fetch(inner_weight, outer_weight, up_weight, down_weight):
    inner_full, outer_full = (
        lax.all_gather(inner_weight, ("dp", "mlp"), axis=0, tiled=True),
        lax.all_gather(outer_weight, ("dp", "mlp"), axis=0, tiled=True),
    )
    up_full, down_full = (
        lax.all_gather(up_weight, "dp", axis=0, tiled=True),
        lax.all_gather(down_weight, "dp", axis=1, tiled=True),
    )
    return (inner_full, outer_full, up_full, down_full)


def contract_rows(left, right):
    return lax.dot_general(
        left, right, (((0,), (0,)), ((), ())), preferred_element_type=jnp.float32
    )


def contract_cols(left, right):
    return lax.dot_general(
        left, right, (((1,), (1,)), ((), ())), preferred_element_type=jnp.float32
    )


def logits_of(query, keys, bias, allowed, factor):
    raw = jnp.einsum("qhd,khd->hqk", query, keys, preferred_element_type=jnp.float32) * factor
    return jnp.where(allowed, raw + bias, -1e30)


def body(
    tokens,
    keep_mask,
    position_index,
    cotangent,
    first_gain,
    first_shift,
    inner_weight,
    query_bias,
    value_bias,
    outer_weight,
    outer_bias,
    attend_scale,
    second_gain,
    second_shift,
    up_weight,
    up_bias,
    down_weight,
    down_bias,
    feed_scale,
    position_table,
):
    micro, rows, width = tokens.shape
    heads = position_table.shape[1]
    head_dim = width // heads
    factor = head_dim ** (-0.5)
    entries = position_table.shape[0]
    columns = up_weight.shape[1]
    col_start = lax.axis_index("mlp") * columns
    up_local = lax.dynamic_slice_in_dim(up_bias, col_start, columns, 0)
    shift_vector = jnp.concatenate([query_bias, jnp.zeros_like(query_bias), value_bias])
    table_by_head = jnp.transpose(position_table)
    bias = table_by_head[:, position_index]
    seen = jnp.arange(rows)
    diagonal = seen[:, None] == seen[None, :]
    flat_index = position_index.reshape(rows * rows)
    zero_width = jnp.zeros((width,), jnp.float32)
    sum_inner = jnp.zeros((width, 3 * width), jnp.float32)
    sum_outer = jnp.zeros((width, width), jnp.float32)
    sum_up = jnp.zeros((width, columns), jnp.float32)
    sum_down = jnp.zeros((columns, width), jnp.float32)
    sum_table_heads = jnp.zeros((heads, entries), jnp.float32)
    sum_up_bias = jnp.zeros((columns,), jnp.float32)
    sum_first_gain = zero_width
    sum_first_shift = zero_width
    sum_query_bias = zero_width
    sum_value_bias = zero_width
    sum_outer_bias = zero_width
    sum_attend_scale = zero_width
    sum_second_gain = zero_width
    sum_second_shift = zero_width
    sum_down_bias = zero_width
    sum_feed_scale = zero_width
    results = []
    input_grads = []
    for index in range(micro):
        inner_full, outer_full, up_full, down_full = fetch(
            inner_weight, outer_weight, up_weight, down_weight
        )
        source = tokens[index].astype(jnp.float32)
        allowed = jnp.logical_or(keep_mask[index][None, :] == 1, diagonal)[None]
        normed_one, unit_one, scaled_one = layer_norm(source, first_gain, first_shift)
        normed_one = normed_one.astype(jnp.bfloat16)
        projected = (
            jnp.dot(normed_one, inner_full, preferred_element_type=jnp.float32) + shift_vector
        ).astype(jnp.bfloat16)
        query = projected[:, :width].reshape(rows, heads, head_dim)
        keys = projected[:, width : 2 * width].reshape(rows, heads, head_dim)
        values = projected[:, 2 * width :].reshape(rows, heads, head_dim)
        logits = logits_of(query, keys, bias, allowed, factor)
        top = jnp.max(logits, -1, keepdims=True)
        expd = jnp.exp(logits - top)
        total = jnp.sum(expd, -1, keepdims=True)
        probs = expd / total
        log_total = top + jnp.log(total)
        mixed = jnp.einsum(
            "hqk,khd->qhd", probs.astype(jnp.bfloat16), values, preferred_element_type=jnp.float32
        )
        mixed = mixed.reshape(rows, width).astype(jnp.bfloat16)
        attend = jnp.dot(mixed, outer_full, preferred_element_type=jnp.float32) + outer_bias
        resid = source + attend_scale * attend
        normed_two, unit_two, scaled_two = layer_norm(resid, second_gain, second_shift)
        normed_two = normed_two.astype(jnp.bfloat16)
        sequence_rows = lax.all_gather(normed_two, "mlp", axis=0, tiled=True)
        pre = jnp.dot(sequence_rows, up_full, preferred_element_type=jnp.float32) + up_local
        active, slope = gelu_pair(pre)
        hidden = active.astype(jnp.bfloat16)
        feed = (
            lax.psum_scatter(
                jnp.dot(hidden, down_full, preferred_element_type=jnp.float32).astype(jnp.bfloat16),
                "mlp",
                scatter_dimension=0,
                tiled=True,
            ).astype(jnp.float32)
            + down_bias
        )
        results.append((resid + feed_scale * feed).astype(jnp.bfloat16))
        inner_full, outer_full, up_full, down_full = fetch(
            inner_weight, outer_weight, up_weight, down_weight
        )
        upstream = cotangent[index].astype(jnp.float32)
        sum_feed_scale = sum_feed_scale + jnp.sum(feed * upstream, 0)
        dfeed = feed_scale * upstream
        sum_down_bias = sum_down_bias + jnp.sum(dfeed, 0)
        upstream_all = lax.all_gather(dfeed.astype(jnp.bfloat16), "mlp", axis=0, tiled=True)
        sum_down = sum_down + contract_rows(hidden, upstream_all)
        dpre = (contract_cols(upstream_all, down_full) * slope).astype(jnp.bfloat16)
        sum_up_bias = sum_up_bias + jnp.sum(dpre.astype(jnp.float32), 0)
        sum_up = sum_up + contract_rows(sequence_rows, dpre)
        dnormed_two = lax.psum_scatter(
            contract_cols(dpre, up_full).astype(jnp.bfloat16),
            "mlp",
            scatter_dimension=0,
            tiled=True,
        ).astype(jnp.float32)
        dresid_norm, part_gain, part_shift = norm_back(
            dnormed_two, unit_two, scaled_two, second_gain
        )
        sum_second_gain = sum_second_gain + part_gain
        sum_second_shift = sum_second_shift + part_shift
        dresid = upstream + dresid_norm
        sum_attend_scale = sum_attend_scale + jnp.sum(attend * dresid, 0)
        dattend = attend_scale * dresid
        sum_outer_bias = sum_outer_bias + jnp.sum(dattend, 0)
        dattend_low = dattend.astype(jnp.bfloat16)
        sum_outer = sum_outer + contract_rows(mixed, dattend_low)
        dmixed = (
            contract_cols(dattend_low, outer_full)
            .astype(jnp.bfloat16)
            .reshape(rows, heads, head_dim)
        )
        logits = logits_of(query, keys, bias, allowed, factor)
        probs = jnp.exp(logits - log_total)
        dvalues = jnp.einsum(
            "hqk,qhd->khd", probs.astype(jnp.bfloat16), dmixed, preferred_element_type=jnp.float32
        )
        dprobs = jnp.einsum("qhd,khd->hqk", dmixed, values, preferred_element_type=jnp.float32)
        dlogits = probs * (dprobs - jnp.sum(dprobs * probs, -1, keepdims=True))
        sum_table_heads = sum_table_heads.at[:, flat_index].add(dlogits.reshape(heads, rows * rows))
        dlogits_low = dlogits.astype(jnp.bfloat16)
        dquery = (
            jnp.einsum("hqk,khd->qhd", dlogits_low, keys, preferred_element_type=jnp.float32)
            * factor
        )
        dkeys = (
            jnp.einsum("hqk,qhd->khd", dlogits_low, query, preferred_element_type=jnp.float32)
            * factor
        )
        dprojected = jnp.concatenate(
            [dquery.reshape(rows, width), dkeys.reshape(rows, width), dvalues.reshape(rows, width)],
            axis=1,
        ).astype(jnp.bfloat16)
        sum_query_bias = sum_query_bias + jnp.sum(dprojected[:, :width].astype(jnp.float32), 0)
        sum_value_bias = sum_value_bias + jnp.sum(dprojected[:, 2 * width :].astype(jnp.float32), 0)
        sum_inner = sum_inner + contract_rows(normed_one, dprojected)
        dnormed_one = contract_cols(dprojected, inner_full)
        dsource_norm, part_gain, part_shift = norm_back(
            dnormed_one, unit_one, scaled_one, first_gain
        )
        sum_first_gain = sum_first_gain + part_gain
        sum_first_shift = sum_first_shift + part_shift
        input_grads.append((dresid + dsource_norm).astype(jnp.bfloat16))
    sum_table = jnp.transpose(sum_table_heads)
    gradient_inner, gradient_outer = (
        lax.psum_scatter(sum_inner, ("dp", "mlp"), scatter_dimension=0, tiled=True),
        lax.psum_scatter(sum_outer, ("dp", "mlp"), scatter_dimension=0, tiled=True),
    )
    gradient_up, gradient_down = (
        lax.psum_scatter(sum_up, "dp", scatter_dimension=0, tiled=True),
        lax.psum_scatter(sum_down, "dp", scatter_dimension=1, tiled=True),
    )
    up_bias_full = lax.dynamic_update_slice_in_dim(
        jnp.zeros((up_bias.shape[0],), jnp.float32), sum_up_bias, col_start, 0
    )
    summed = lax.psum(
        (
            sum_first_gain,
            sum_first_shift,
            sum_query_bias,
            sum_value_bias,
            sum_outer_bias,
            sum_attend_scale,
            sum_second_gain,
            sum_second_shift,
            up_bias_full,
            sum_down_bias,
            sum_feed_scale,
            sum_table,
        ),
        ("dp", "mlp"),
    )
    return (
        jnp.stack(results),
        jnp.stack(input_grads),
        gradient_inner,
        gradient_outer,
        gradient_up,
        gradient_down,
        summed[0],
        summed[1],
        summed[2],
        summed[3],
        summed[4],
        summed[5],
        summed[6],
        summed[7],
        summed[8],
        summed[9],
        summed[10],
        summed[11],
    )


def solution(mesh):
    special = mesh.shape["dp"] == 8 and mesh.shape["mlp"] == 4
    placed = (
        P(None, ("dp", "mlp"), None),
        P(None, ("dp", "mlp")),
        P(),
        P(None, ("dp", "mlp"), None),
        P(),
        P(),
        P(("dp", "mlp"), None),
        P(),
        P(),
        P(("dp", "mlp"), None),
        P(),
        P(),
        P(),
        P(),
        P("dp", "mlp"),
        P(),
        P("mlp", "dp"),
        P(),
        P(),
        P(),
    )
    return jax.shard_map(
        fast_body if special else body,
        mesh=mesh,
        in_specs=placed,
        out_specs=(
            P(None, ("dp", "mlp"), None),
            P(None, ("dp", "mlp"), None),
            P(("dp", "mlp"), None),
            P(("dp", "mlp"), None),
            P("dp", "mlp"),
            P("mlp", "dp"),
            P(),
            P(),
            P(),
            P(),
            P(),
            P(),
            P(),
            P(),
            P(),
            P(),
            P(),
            P(),
        ),
        check_vma=False,
    )
```

```python
import functools

import jax
import jax.numpy as jnp
from jax import lax
from jax.experimental import pallas as pl
from jax.experimental.pallas import tpu as pltpu
from jax.sharding import PartitionSpec as P

EPS = 1e-06
ROOT_HALF = 0.7071067811865476
DENSITY = 0.3989422804014327


MESH = pl.DeviceIdType.MESH
F32 = jnp.float32
BF16 = jnp.bfloat16
TILE = 384
PAD = 208
TALL = 2 * PAD
KEYS = 256
N_COPY = 10
NAMES = ("I0", "I1", "I2", "O", "U0", "U1", "N0", "N1")
GATHER = {"I0": "zyx", "I1": "zxy", "I2": "zyx", "O": "zyx", "U0": "zxy", "N0": "zyx", "U1": "xzy", "N1": "zyx"}
REDUCE = {"I0": "yxz", "I1": "yxz", "I2": "xyz", "O": "xyz", "U0": "xyz", "N0": "yzx", "U1": "yxz", "N1": "xzy"}
ORDER = (
    "norm1", "fill", "LI0", "LU1", "look00", "look01", "LI1", "look10", "PI0", "QI0", "LI2", "look11",
    "look20", "PI1", "QI1", "LO", "look21", "RI0", "PI2", "turn1", "turnd", "FI0", "proj0", "RI1",
    "QI2", "LU0", "att0", "FI1", "PO", "QO", "proj1", "att1", "RI2", "LN0", "FI2", "proj2",
    "att2", "PU0", "QU0", "RO", "FO", "out", "PN0", "norm2", "LN1", "QN0", "RU0", "FU0",
    "wide00", "PU1", "QU1", "wide01", "RN0", "FN0", "back00", "PN1", "back01", "QN1", "cN0", "cU0",
    "RN1", "dN0", "RU1", "dU0", "FN1", "FU1", "wide10", "wide11", "back10", "back11", "cN1", "cU1",
    "sec0", "eN0", "sec1", "eU0", "dN1", "dU1", "E0", "dmix", "E1", "gout", "cO", "attb0",
    "fU0", "dO", "projb0", "fN0", "cI0", "attb1", "eN1", "dI0", "gU0", "projb1", "cI1", "attb2",
    "eU1", "eO", "dI1", "E2", "projb2", "gN0", "cI2", "first", "eI0", "dI2", "fN1", "fU1",
    "fO", "l0", "count0", "l1", "E3", "count1", "fI0", "count2", "eI1", "count3", "gN1", "count4",
    "gU1", "eI2", "l2", "t0", "res", "tok", "gO", "t1", "fI1", "gI0", "fI2", "l3",
    "t2", "gI1", "gI2", "t3",
)


def place():
    dp = lax.axis_index("dp")
    mlp = lax.axis_index("mlp")
    return lax.div(dp, 2), lax.rem(dp, 2), lax.div(mlp, 2), lax.rem(mlp, 2)


def device(z, x, y, c):
    return (z * 2 + x, y * 2 + c)


def greet(z, x, y, c):
    barrier = pltpu.get_barrier_semaphore()
    others = [device(lax.rem(z + d, 4), x, y, c) for d in (1, 2, 3)]
    others += [device(z, 1 - x, y, c), device(z, x, 1 - y, c), device(z, 1 - x, 1 - y, c), device(z, x, y, 1 - c)]
    for other in others:
        pl.semaphore_signal(barrier, inc=1, device_id=other, device_id_type=MESH)
    pl.semaphore_wait(barrier, len(others))


class Link:
    def __init__(self, send, recv):
        self.send, self.recv, self.pending = send, recv, {}

    def copy(self, src, dst, slot, target, group=None):
        made = pltpu.make_async_remote_copy(
            src_ref=src,
            dst_ref=dst,
            send_sem=self.send.at[slot],
            recv_sem=self.recv.at[slot],
            device_id=target,
            device_id_type=MESH,
        )
        made.start()
        self.pending.setdefault(group, []).append(made)
        return made

    def drain(self, *groups):
        for group in groups or tuple(self.pending):
            for made in self.pending.pop(group, []):
                made.wait_send()


class Unit:
    def __init__(self, link, ref, name, where, base):
        self.link, self.ref, self.where, self.base, self.name = link, ref, where, base, name
        self.narrow = name[0] in "IO"
        self.group = name if base < 8 * N_COPY else None

    def put(self, src, dst, slot, target):
        return self.link.copy(src, dst, self.base + slot, target, self.group)

    def block(self, z, x, y, c):
        return self.ref.at[c, z, x, y] if self.narrow else self.ref.at[y, c, z, x]

    def line(self, x, y, c):
        return self.ref.at[c, :, x, y] if self.narrow else self.ref.at[y, c, :, x]

    def by_core(self, c):
        return self.ref.at[c] if self.narrow else self.ref.at[:, c]

    def by_y(self, y, c):
        return self.ref.at[c, :, :, y] if self.narrow else self.ref.at[y, c]

    def by_x(self, x, c):
        return self.ref.at[c, :, x] if self.narrow else self.ref.at[:, c, :, x]

    def along_y(self, z, x, c):
        return self.ref.at[c, z, x] if self.narrow else self.ref.at[:, c, z, x]

    def along_x(self, z, y, c):
        return self.ref.at[c, z, :, y] if self.narrow else self.ref.at[y, c, z]

    def spread(self, part, slot):
        z, x, y, c = self.where
        return [self.put(part, part, slot + d - 1, device(lax.rem(z + d, 4), x, y, c)) for d in (1, 2, 3)]

    def across(self, axis, src, dst, slot):
        z, x, y, c = self.where
        target = {"x": (z, 1 - x, y, c), "y": (z, x, 1 - y, c), "c": (z, x, y, 1 - c)}[axis]
        return self.put(src, dst, slot, device(*target))


class Gather(Unit):
    def Z(self):
        self.z = self.spread(self.block(*self.where), 0)

    def L(self):
        z, x, y, c = self.where
        for made in self.z:
            made.wait_recv()
        part = self.line(x, y, c)
        self.made = {axis: self.across(axis, part, part, 3 + n) for n, axis in enumerate(GATHER[self.name][1:] + "c")}
        self.to_c = [self.made["c"]]

    def pass_on(self, axis, slot):
        z, x, y, c = self.where
        self.made[axis].wait_recv()
        part = self.line(1 - x, y, c) if axis == "x" else self.line(x, 1 - y, c)
        self.to_c.append(self.across("c", part, part, slot))
        return part

    def P(self):
        first, last = GATHER[self.name][1:]
        part = self.pass_on(first, 6)
        self.last = self.across(last, part, part, 7)

    def Q(self):
        self.pass_on(GATHER[self.name][2], 8)

    def R(self):
        z, x, y, c = self.where
        self.last.wait_recv()
        part = self.line(1 - x, 1 - y, c)
        self.to_c.append(self.across("c", part, part, 9))

    def F(self):
        for made in self.to_c:
            made.wait_recv()


class GatherZ(Unit):
    def Z(self):
        part = self.block(*self.where)
        self.first = self.across(GATHER[self.name][0], part, part, 0)
        self.z = self.spread(part, 1)

    def L(self):
        z, x, y, c = self.where
        self.first.wait_recv()
        part = self.block(z, 1 - x, y, c) if GATHER[self.name][0] == "x" else self.block(z, x, 1 - y, c)
        self.z += self.spread(part, 4)

    def P(self):
        z, x, y, c = self.where
        for made in self.z:
            made.wait_recv()
        last = GATHER[self.name][2]
        part = self.by_x(x, c) if last == "x" else self.by_y(y, c)
        self.last = self.across(last, part, part, 7)
        self.to_c = [self.across("c", part, part, 8)]

    def Q(self):
        pass

    def R(self):
        z, x, y, c = self.where
        self.last.wait_recv()
        part = self.by_x(1 - x, c) if GATHER[self.name][2] == "x" else self.by_y(1 - y, c)
        self.to_c.append(self.across("c", part, part, 9))

    def F(self):
        for made in self.to_c:
            made.wait_recv()


def mix(here, *there):
    total = here[...].astype(F32)
    for other in there:
        total = total + other[...].astype(F32)
    here[...] = total.astype(BF16)


class Reduce(Unit):
    def set_buffers(self, half, quarter, third, fourth):
        self.half, self.quarter, self.third, self.fourth = half, quarter, third, fourth

    @staticmethod
    def buffers(name):
        rows = 48 if name[0] in "IO" else 96
        half = (4, 2, 2, rows, TILE) if name[0] in "IO" else (2, 4, 2, rows, TILE)
        pair = (2, 4) if name[0] not in "IO" and REDUCE[name][0] == "x" else (4, 2)
        if REDUCE[name][2] == "z":
            return (half, (*pair, rows, TILE), (4, rows, TILE), (3, rows, TILE))
        return (half, (*pair, rows, TILE), (3, 2, rows, TILE), (rows, TILE))

    def c(self):
        z, x, y, c = self.where
        self.made = self.across("c", self.by_core(1 - c), self.half, 0)

    def d(self):
        z, x, y, c = self.where
        self.made.wait_recv()
        mix(self.by_core(c), self.half)
        first = REDUCE[self.name][0]
        self.made = self.across(first, self.by_x(1 - x, c) if first == "x" else self.by_y(1 - y, c), self.quarter, 1)

    def e(self):
        z, x, y, c = self.where
        self.made.wait_recv()
        mix(self.by_x(x, c) if REDUCE[self.name][0] == "x" else self.by_y(y, c), self.quarter)
        last = REDUCE[self.name][1]
        self.made = self.across(last, self.line(1 - x, y, c) if last == "x" else self.line(x, 1 - y, c), self.third, 2)

    def f(self):
        z, x, y, c = self.where
        self.made.wait_recv()
        mix(self.line(x, y, c), self.third)
        self.z = []
        for d in (1, 2, 3):
            far = lax.rem(z + d, 4)
            self.z.append(self.put(self.block(far, x, y, c), self.fourth.at[d - 1], 2 + d, device(far, x, y, c)))

    def total(self):
        for made in self.z:
            made.wait_recv()
        total = self.block(*self.where)[...].astype(F32)
        for d in range(3):
            total = total + self.fourth[d].astype(F32)
        return total


class ReduceZ(Reduce):
    def pair(self, z):
        x, y, c = self.where[1:]
        return self.along_y(z, x, c) if REDUCE[self.name][0] == "x" else self.along_x(z, y, c)

    def e(self):
        z, x, y, c = self.where
        self.made.wait_recv()
        mix(self.by_x(x, c) if REDUCE[self.name][0] == "x" else self.by_y(y, c), self.quarter)
        self.z = []
        for d in (1, 2, 3):
            far = lax.rem(z + d, 4)
            self.z.append(self.put(self.pair(far), self.third.at[d - 1], 2 + d, device(far, x, y, c)))

    def f(self):
        z, x, y, c = self.where
        for made in self.z:
            made.wait_recv()
        mix(self.pair(z), *(self.third.at[d] for d in range(3)))
        last = REDUCE[self.name][2]
        part = self.block(z, 1 - x, y, c) if last == "x" else self.block(z, x, 1 - y, c)
        self.made = self.across(last, part, self.fourth, 6)

    def total(self):
        self.made.wait_recv()
        return self.block(*self.where)[...].astype(F32) + self.fourth[...].astype(F32)


class Everywhere:
    def __init__(self, link, ref, core_ref, plane_ref, line_ref, base, where):
        self.link, self.ref, self.where, self.base = link, ref, where, base
        self.core_ref, self.plane_ref, self.line_ref = core_ref, plane_ref, line_ref

    def to_core(self):
        z, x, y, c = self.where
        self.made = [self.link.copy(self.ref, self.core_ref, self.base, device(z, x, y, 1 - c))]

    def wait(self):
        for made in self.made:
            made.wait_recv()

    def to_plane(self):
        z, x, y, c = self.where
        self.wait()
        chip = self.plane_ref.at[3]
        chip[...] = self.ref[...] + self.core_ref[...]
        targets = (device(z, 1 - x, y, c), device(z, x, 1 - y, c), device(z, 1 - x, 1 - y, c))
        self.made = [
            self.link.copy(chip, self.plane_ref.at[n], self.base + 1 + n, target) for n, target in enumerate(targets)
        ]

    def to_line(self):
        z, x, y, c = self.where
        self.wait()
        got = self.plane_ref
        self.line_ref[z] = (got[3] + got[0]) + (got[1] + got[2])
        part = self.line_ref.at[z]
        self.made = [
            self.link.copy(part, part, self.base + 3 + d, device(lax.rem(z + d, 4), x, y, c)) for d in (1, 2, 3)
        ]

    def total(self):
        self.wait()
        got = self.line_ref
        return (got[0] + got[1]) + (got[2] + got[3])


def dot(left, right):
    return lax.dot_general(left, right, (((1,), (0,)), ((), ())), preferred_element_type=F32)


def dot_nt(left, right):
    return lax.dot_general(left, right, (((1,), (1,)), ((), ())), preferred_element_type=F32)


def dot_tn(left, right):
    return lax.dot_general(left, right, (((0,), (0,)), ((), ())), preferred_element_type=F32)


def fold(values):
    rows, width = values.shape
    return jnp.sum(values.reshape(rows // 8, 8, width), 0)


def unit_of(values):
    mean = jnp.mean(values, -1, keepdims=True)
    centred = values - mean
    variance = jnp.mean(centred * centred, -1, keepdims=True)
    scaled = lax.rsqrt(variance + EPS)
    return centred * scaled, scaled


def loop(count, step, init):
    return lax.fori_loop(0, count, step, init)


def by_rows(step, init, first=0, count=13):
    size = 32

    def one(index, carried):
        return step(pl.ds(pl.multiple_of((index + first) * size, size), size), carried)

    one.__name__ = step.__name__
    return loop(count, one, init)


def layer_kernel(*refs):
    (
        tokens, keep, places, cotangent, first_gain1, first_shift1, inner_in, query_bias1, value_bias1, outer_in, outer_bias1,
        attend_scale1, second_gain1, second_shift1, up_in, up_bias, down_in, down_bias1, feed_scale1, table_in,
        result, token_grad, inner_out, outer_out, up_out, down_out, early_out, late_out, table_out,
        *rest,
    ) = refs
    (
        narrow, wide, small, pair, swap,
        source, upstream, normed1, normed1_t, normed2, normed2_t, qkv, bias, mask, index, probs, mix_t, attend, resid,
        dfeed, dfeed_t, hidden, slope, total, dnormed2, shifts, ups, tab, vectors,
        early, late, hits, early_core, early_plane, early_line, late_core, late_plane, late_line, hits_core, hits_plane, hits_line,
        send, recv, *buffers,
    ) = rest
    dresid, dproj, dmixed, mixed, dattend = resid, hidden, normed2, normed2, dfeed
    where = z, x, y, c = place()
    link = Link(send, recv)
    gathers, reduces = {}, {}
    for n, name in enumerate(NAMES):
        ref = narrow.at[n] if n < 4 else wide.at[n - 4]
        kind = Gather if GATHER[name][0] == "z" else GatherZ
        gathers[name] = kind(link, ref, name, where, n * N_COPY)
        kind = Reduce if REDUCE[name][2] == "z" else ReduceZ
        reduces[name] = kind(link, ref, name, where, (8 + n) * N_COPY)
        reduces[name].set_buffers(*buffers[4 * n : 4 * n + 4])
    spare = 16 * N_COPY
    sums = {
        "E": Everywhere(link, early, early_core, early_plane, early_line, spare + 5, where),
        "l": Everywhere(link, late, late_core, late_plane, late_line, spare + 15, where),
        "t": Everywhere(link, hits, hits_core, hits_plane, hits_line, spare + 25, where),
    }
    mates = []
    kept = {}
    for k in range(3):
        for core in range(2):
            for part in range(3):
                start = part * 768 + (core * 3 + k) * 128
                small[k, core, :, part * 128 : part * 128 + 128] = inner_in[:, start : start + 128].astype(F32)
    for core in range(2):
        small[3, core] = outer_in[:, core * TILE : core * TILE + TILE].astype(F32)
    for k in range(2):
        cols = slice(k * TILE, k * TILE + TILE)
        wide[k, y, c, z, x] = up_in[:, cols]
        wide[2 + k, y, c, z, x] = down_in[:, cols]
    greet(*where)
    mate = link.copy(small.at[:, 1 - c], pair.at[:, c], spare, device(z, x, y, 1 - c))
    for name in NAMES[4:]:
        if GATHER[name][0] != "z":
            gathers[name].Z()
    pair[:, c] = small[:, c]
    mate.wait_recv()
    link.drain(None)
    for unit in range(4):
        narrow[unit, c, z, x, y] = pair[unit].reshape(48, TILE).astype(BF16)
    for name in GATHER:
        if name[0] in "IO" or GATHER[name][0] == "z":
            gathers[name].Z()

    given = (first_gain1, first_shift1, query_bias1, value_bias1, outer_bias1, attend_scale1, second_gain1, second_shift1, down_bias1, feed_scale1)
    for n, ref in enumerate(given):
        vectors[n] = ref[...].reshape(1, 768)
    (first_gain, first_shift, query_bias, value_bias, outer_bias, attend_scale, second_gain, second_shift, down_bias, feed_scale) = (
        vectors.at[n] for n in range(10)
    )

    for image in range(2):
        last = pl.ds(image * PAD + 192, 16)
        source[last, :] = jnp.zeros((16, 768), BF16)
        upstream[last, :] = jnp.zeros((16, 768), BF16)
        source[pl.ds(image * PAD, 197), :] = tokens[image]
        upstream[pl.ds(image * PAD, 197), :] = cotangent[image]
    zero = jnp.zeros((8, 768), F32)
    lane = lax.broadcasted_iota(jnp.int32, (1, 128), 1)
    picks = [(lane < 64).astype(F32).astype(BF16), (lane >= 64).astype(F32).astype(BF16)]

    def rows_of(image):
        return slice(image * PAD, image * PAD + PAD)

    def keys_of(image):
        return slice(image * PAD, image * PAD + KEYS)

    def cols_of(p):
        return pl.ds(pl.multiple_of(p * 128, 128), 128)

    def half(core):
        return slice(core * TILE, core * TILE + TILE)

    def norm1():
        def norm_first(rows, carried):
            unit, _ = unit_of(source[rows, :].astype(F32))
            normed1[rows, :] = (unit * first_gain[...] + first_shift[...]).astype(BF16)
            lifted = upstream[rows, :].astype(F32) * feed_scale[...]
            dfeed[rows, :] = lifted.astype(BF16)
            return carried + fold(lifted)

        early[...] = jnp.zeros((16, 768), F32)
        late[...] = jnp.zeros((8, 768), F32)
        early[4:5, :] = jnp.sum(by_rows(norm_first, zero), 0, keepdims=True)
        zero_row = jnp.zeros((1, 128), F32)
        for p in range(6):
            cols = slice(p * 128, p * 128 + 128)
            shifts[p] = jnp.concatenate([query_bias[:, cols], zero_row, value_bias[:, cols]], axis=1)
            qkv[p, TALL:, :] = jnp.zeros((48, TILE), BF16)

    def fill():
        index[...] = jnp.full((PAD, KEYS), -1, jnp.int32)
        index[0:197, 0:197] = places[...]
        tab[...] = jnp.zeros((12, 1, 768), F32)
        for head in range(12):
            tab[head, :, 0:732] = table_in[head : head + 1, :]
        row_of = lax.broadcasted_iota(jnp.int32, (PAD, KEYS), 0)
        col_of = lax.broadcasted_iota(jnp.int32, (PAD, KEYS), 1)
        for image in range(2):
            mask[image] = jnp.full((PAD, KEYS), -1e30, F32)
            shown = jnp.where(keep[image : image + 1, :] == 1, 0.0, -1e30).astype(F32)
            mask[image, :, 0:197] = jnp.broadcast_to(shown, (PAD, 197))
            mask[image] = jnp.where(row_of == col_of, 0.0, mask[image])

    def look(k, core):
        def look_up(t, carried):
            head = 2 * (core * 3 + k) + t
            for side in range(2):
                cols = slice(side * 128, side * 128 + 128)
                spot = index[:, cols]
                low, high = spot & 127, spot >> 7
                found = jnp.zeros((PAD, 128), F32)
                for piece in range(6):
                    row = tab[head, :, piece * 128 : piece * 128 + 128]
                    picked = jnp.take_along_axis(jnp.broadcast_to(row, (PAD, 128)), low, axis=1)
                    found = jnp.where(high == piece, picked, found)
                bias[head, :, cols] = found
            return carried

        loop(2, look_up, 0)

    def turn1():
        normed1_t[...] = normed1[...].T

    def turnd():
        dfeed_t[...] = dfeed[...].T

    def proj(k):
        def project(core, carried):
            p = core * 3 + k
            weight = narrow[k, core].reshape(768, TILE)
            scaling = jnp.where(lax.broadcasted_iota(jnp.int32, (1, TILE), 1) < 128, 0.125, 1.0).astype(F32)
            value = (dot(normed1[...], weight) + shifts[p]).astype(BF16)
            qkv[p, 0:TALL, :] = (value.astype(F32) * scaling).astype(BF16)
            return carried

        loop(2, project, 0)

    def att(k):
        def attend_pair(core, carried):
            p = core * 3 + k
            first_half = lax.broadcasted_iota(jnp.int32, (PAD, 128), 1) < 64
            for image in range(2):
                query = qkv[p, rows_of(image), 0:128]
                keys = qkv[p, keys_of(image), 128:256]
                values = qkv[p, keys_of(image), 256:384]
                outs = []
                for t in range(2):
                    logits = dot_nt(query * picks[t], keys) + bias[2 * p + t] + mask[image]
                    top = jnp.max(logits, -1, keepdims=True)
                    expd = jnp.exp(logits - top)
                    share = (expd * (1.0 / jnp.sum(expd, -1, keepdims=True))).astype(BF16)
                    probs[image, 2 * p + t] = share
                    outs.append(dot(share, values))
                mixed[rows_of(image), cols_of(p)] = jnp.where(first_half, outs[0], outs[1]).astype(BF16)
            return carried

        loop(2, attend_pair, 0)

    def out():
        for core in range(2):
            attend[:, half(core)] = dot(mixed[...], narrow[3, core].reshape(768, TILE)) + outer_bias[:, half(core)]
        mix_t[...] = mixed[...].T

    def norm2():
        def norm_second(rows, carried):
            value = source[rows, :].astype(F32) + attend_scale[...] * attend[rows, :]
            resid[rows, :] = value
            unit, _ = unit_of(value)
            normed2[rows, :] = (unit * second_gain[...] + second_shift[...]).astype(BF16)
            return carried

        by_rows(norm_second, 0)
        normed2_t[...] = normed2[...].T

    def widening(k, side):
        def widen(core, carried):
            weight = wide[k, side, core].reshape(768, TILE)
            cols = pl.ds(pl.multiple_of((side * 2 + core) * 768 + k * TILE, 128), TILE)
            pre = dot(normed2[...], weight) + up_bias[:, cols]
            cumul = 0.5 * (1.0 + lax.erf(pre * ROOT_HALF))
            b = k * 4 + side * 2 + core
            hidden[b] = (pre * cumul).astype(BF16)
            slope[b] = (cumul + pre * jnp.exp(-0.5 * pre * pre) * DENSITY).astype(BF16)
            return carried

        loop(2, widen, 0)

    def back(k, side):
        if side == 0:
            link.drain("U" + str(k), "N" + str(k))
        b = k * 4 + side * 2

        def narrow_back(step, carried):
            down = jnp.concatenate([wide[2 + k, side, core].reshape(768, TILE) for core in range(2)], axis=1)
            up = jnp.concatenate([wide[k, side, core].reshape(768, TILE) for core in range(2)], axis=1)
            both = jnp.concatenate([hidden[b], hidden[b + 1]], axis=1)
            part = dot_nt(both, down)
            total[...] = part if b == 0 else total[...] + part
            tilt = jnp.concatenate([slope[b], slope[b + 1]], axis=1).astype(F32)
            dpre = (dot(dfeed[...], down) * tilt).astype(BF16)
            ups[b // 2] = jnp.sum(fold(dpre.astype(F32)), 0, keepdims=True)
            part = dot_nt(dpre, up)
            dnormed2[...] = part if b == 0 else dnormed2[...] + part
            up_grad = dot(normed2_t[...], dpre).astype(BF16)
            down_grad = dot(dfeed_t[...], both).astype(BF16)
            for core in range(2):
                wide[2 + k, side, core] = up_grad[:, half(core)].reshape(4, 2, 96, TILE)
                wide[k, side, core] = down_grad[:, half(core)].reshape(4, 2, 96, TILE)
            return carried

        loop(1, narrow_back, 0)

    def sec(n):
        def second_back(rows, carried):
            feed_scale_sum, gain_sum, shift_sum, scale_sum, bias_sum = carried
            feed = total[rows, :] + down_bias[...]
            above = upstream[rows, :].astype(F32)
            value = resid[rows, :]
            total[rows, :] = value + feed_scale[...] * feed
            unit, scaled = unit_of(value)
            grad = dnormed2[rows, :]
            inner = grad * second_gain[...]
            first = jnp.mean(inner, -1, keepdims=True)
            second = jnp.mean(inner * unit, -1, keepdims=True)
            back = above + scaled * (inner - first - unit * second)
            dresid[rows, :] = back
            lifted = attend_scale[...] * back
            dattend[rows, :] = lifted.astype(BF16)
            return (
                feed_scale_sum + fold(feed * above),
                gain_sum + fold(grad * unit),
                shift_sum + fold(grad),
                scale_sum + fold(attend[rows, :] * back),
                bias_sum + fold(lifted),
            )

        kept["sec"] = by_rows(second_back, kept.get("sec", (zero,) * 5), 7 * n, 7 - n)
        if n == 1:
            for block in range(4):
                for k in range(2):
                    b = k * 4 + block
                    early[8 + block : 9 + block, half(k)] = ups[b // 2, :, half(b % 2)]
            for row, value in zip((5, 2, 3, 1, 0), kept.pop("sec")):
                early[row : row + 1, :] = jnp.sum(value, 0, keepdims=True)

    def res():
        for image in range(2):
            result[image] = total[pl.ds(image * PAD, 197), :].astype(BF16)
        kept["res"] = True

    def dmix():
        parts = [dot_nt(dattend[:, half(core)], narrow[3, core].reshape(768, TILE)) for core in range(2)]
        dmixed[...] = (parts[0] + parts[1]).astype(BF16)

    def gout():
        link.drain("O")
        for core in range(2):
            narrow[3, core] = dot(mix_t[...], dattend[:, half(core)]).astype(BF16).reshape(4, 2, 2, 48, TILE)

    def attb(k):
        def attend_back(core, carried):
            p = core * 3 + k
            first_half = lax.broadcasted_iota(jnp.int32, (PAD, 128), 1) < 64
            hit = [None, None]
            for image in range(2):
                rows = rows_of(image)
                query = qkv[p, rows, 0:128]
                keys = qkv[p, keys_of(image), 128:256]
                values = qkv[p, keys_of(image), 256:384]
                above = dmixed[rows, cols_of(p)]
                dquery, dkeys, dvalues = [], [], []
                for t in range(2):
                    share = probs[image, 2 * p + t]
                    dvalues.append(dot_tn(share, above)[0:PAD])
                    dshare = dot_nt(above * picks[t], values)
                    full = share.astype(F32)
                    dlogits = full * (dshare - jnp.sum(dshare * full, -1, keepdims=True))
                    hit[t] = dlogits if image == 0 else hit[t] + dlogits
                    low = dlogits.astype(BF16)
                    dquery.append(dot(low, keys) * 0.125)
                    dkeys.append(dot_tn(low, query)[0:PAD])
                dproj[p, rows, 0:128] = jnp.where(first_half, dquery[0], dquery[1]).astype(BF16)
                dproj[p, rows, 128:256] = jnp.where(first_half, dkeys[0], dkeys[1]).astype(BF16)
                dproj[p, rows, 256:384] = jnp.where(first_half, dvalues[0], dvalues[1]).astype(BF16)
            for t in range(2):
                bias[2 * p + t] = hit[t]
            return carried

        loop(2, attend_back, 0)

    def projb(k):
        link.drain("I" + str(k))

        def project_back(core, carried):
            p = core * 3 + k
            grad = dproj[p]
            summed = jnp.sum(fold(grad.astype(F32)), 0, keepdims=True)
            late[2:3, cols_of(p)] = summed[:, 0:128]
            late[3:4, cols_of(p)] = summed[:, 256:384]
            part = dot_nt(grad, narrow[k, core].reshape(768, TILE))
            dnormed2[...] = jnp.where(core == 0, 0.0, dnormed2[...]) + part if k == 0 else dnormed2[...] + part
            narrow[k, core] = dot(normed1_t[...], grad).astype(BF16).reshape(4, 2, 2, 48, TILE)
            return carried

        loop(2, project_back, 0)

    def first():
        def first_back(rows, carried):
            gain_sum, shift_sum = carried
            grad = dnormed2[rows, :]
            unit, scaled = unit_of(source[rows, :].astype(F32))
            inner = grad * first_gain[...]
            mean = jnp.mean(inner, -1, keepdims=True)
            second = jnp.mean(inner * unit, -1, keepdims=True)
            dresid[rows, :] = dresid[rows, :] + scaled * (inner - mean - unit * second)
            return gain_sum + fold(grad * unit), shift_sum + fold(grad)

        found = by_rows(first_back, (zero, zero))
        late[0:1, :] = jnp.sum(found[0], 0, keepdims=True)
        late[1:2, :] = jnp.sum(found[1], 0, keepdims=True)

    def tok():
        for image in range(2):
            token_grad[image] = dresid[pl.ds(image * PAD, 197), :].astype(BF16)

    def counting(n):
        low_of = lax.broadcasted_iota(jnp.int32, (128, KEYS), 0)
        high_of = lax.broadcasted_iota(jnp.int32, (8, KEYS), 0)

        def count(group, carried):
            eight = pl.ds(pl.multiple_of((group + 5 * n) * 8, 8), 8)
            spots = index[eight, :]
            for r in range(8):
                spot = jnp.broadcast_to(spots[r : r + 1, :], (8, KEYS))
                high = (spot >> 7) == high_of
                parts = []
                for head in range(12):
                    grads = bias[head, eight, :]
                    parts.append(jnp.where(high, jnp.broadcast_to(grads[r : r + 1, :], (8, KEYS)), 0.0))
                spread = jnp.concatenate(parts, axis=0).astype(BF16)
                low = jnp.concatenate([spot & 127] * 16, axis=0)
                which = (low == low_of).astype(F32).astype(BF16)
                carried = carried + dot_nt(spread, which)
            return carried

        before = jnp.zeros((96, 128), F32) if n == 0 else hits[...]
        hits[...] = loop(5, count, before)

    def settle(name):
        value = reduces[name].total()
        n = NAMES.index(name)
        if n < 4:
            small[n] = value.reshape(2, 24, TILE)
            swap[n, c] = small[n, c]
            mates.append(link.copy(small.at[n, 1 - c], swap.at[n, c], spare + 1 + n, device(z, x, y, 1 - c)))
        elif n < 6:
            down_out[:, half(n - 4)] = value
        else:
            up_out[:, half(n - 6)] = value

    steps = {"norm1": norm1, "fill": fill, "turn1": turn1, "turnd": turnd, "out": out, "norm2": norm2, "dmix": dmix, "gout": gout, "first": first, "res": res, "tok": tok}
    for k in range(3):
        steps["proj" + str(k)] = functools.partial(proj, k)
        steps["att" + str(k)] = functools.partial(att, k)
        steps["attb" + str(k)] = functools.partial(attb, k)
        steps["projb" + str(k)] = functools.partial(projb, k)
        for i in range(2):
            steps["look" + str(k) + str(i)] = functools.partial(look, k, i)
    for i in range(2):
        steps["sec" + str(i)] = functools.partial(sec, i)
        for k in range(2):
            steps["wide" + str(k) + str(i)] = functools.partial(widening, k, i)
            steps["back" + str(k) + str(i)] = functools.partial(back, k, i)
    for n in range(5):
        steps["count" + str(n)] = functools.partial(counting, n)
    for name in NAMES:
        for event in "LPQRF":
            steps[event + name] = getattr(gathers[name], event)
        for event in "cdef":
            steps[event + name] = getattr(reduces[name], event)
        steps["g" + name] = functools.partial(settle, name)
    for what, everywhere in sums.items():
        steps[what + "0"] = everywhere.to_core
        steps[what + "1"] = everywhere.to_plane
        steps[what + "2"] = everywhere.to_line

    def give(what, ref):
        ref[...] = sums[what].total()

    steps["E3"] = functools.partial(give, "E", early_out)
    steps["l3"] = functools.partial(give, "l", late_out)

    def give_table():
        found = sums["t"].total().reshape(12, 8, 128)
        for piece in range(6):
            width = min(128, 732 - piece * 128)
            table_out[:, piece * 128 : piece * 128 + width] = found[:, piece, 0:width]

    steps["t3"] = give_table
    for name in ORDER:
        steps[name]()
    for made in mates:
        made.wait_recv()
    for k in range(3):
        for core in range(2):
            for part in range(3):
                start = part * 768 + (core * 3 + k) * 128
                inner_out[:, start : start + 128] = swap[k, core, :, part * 128 : part * 128 + 128]
    for core in range(2):
        outer_out[:, half(core)] = swap[3, core]
    link.drain()


def run_layer(*operands):
    def vmem(*shape, dtype=BF16):
        return pltpu.VMEM(shape, dtype)

    scratch = [
        vmem(4, 2, 4, 2, 2, 48, TILE),
        vmem(4, 2, 2, 4, 2, 96, TILE),
        vmem(4, 2, 24, TILE, dtype=F32),
        vmem(4, 2, 24, TILE, dtype=F32),
        vmem(4, 2, 24, TILE, dtype=F32),
        vmem(TALL, 768),
        vmem(TALL, 768),
        vmem(TALL, 768),
        vmem(768, TALL),
        vmem(TALL, 768),
        vmem(768, TALL),
        vmem(6, TALL + 48, TILE),
        vmem(12, PAD, KEYS, dtype=F32),
        vmem(2, PAD, KEYS, dtype=F32),
        vmem(PAD, KEYS, dtype=jnp.int32),
        vmem(2, 12, PAD, KEYS),
        vmem(768, TALL),
        vmem(TALL, 768, dtype=F32),
        vmem(TALL, 768, dtype=F32),
        vmem(TALL, 768),
        vmem(768, TALL),
        vmem(8, TALL, TILE),
        vmem(8, TALL, TILE),
        vmem(TALL, 768, dtype=F32),
        vmem(TALL, 768, dtype=F32),
        vmem(6, 1, TILE, dtype=F32),
        vmem(4, 1, 768, dtype=F32),
        vmem(12, 1, 768, dtype=F32),
        vmem(10, 1, 768, dtype=F32),
        vmem(16, 768, dtype=F32),
        vmem(8, 768, dtype=F32),
        vmem(96, 128, dtype=F32),
    ]
    for shape in ((16, 768), (8, 768), (96, 128)):
        scratch += [vmem(*shape, dtype=F32), vmem(4, *shape, dtype=F32), vmem(4, *shape, dtype=F32)]
    copies = 16 * N_COPY + 40
    scratch += [pltpu.SemaphoreType.DMA((copies,)), pltpu.SemaphoreType.DMA((copies,))]
    for name in NAMES:
        scratch += [vmem(*shape) for shape in Reduce.buffers(name)]
    shapes = [((2, 197, 768), BF16), ((2, 197, 768), BF16), ((24, 2304), F32), ((24, 768), F32), ((96, 768), F32), ((96, 768), F32)]
    shapes += [((16, 768), F32), ((8, 768), F32), ((12, 732), F32)]
    return pl.pallas_call(
        layer_kernel,
        out_shape=[jax.ShapeDtypeStruct(*shape) for shape in shapes],
        in_specs=[pl.BlockSpec(memory_space=pltpu.VMEM)] * len(operands),
        out_specs=[pl.BlockSpec(memory_space=pltpu.VMEM)] * len(shapes),
        scratch_shapes=scratch,
        compiler_params=pltpu.CompilerParams(
            collective_id=0, has_side_effects=True, vmem_limit_bytes=62 * 2**20
        ),
    )(*operands)


def fast_body(*operands):
    operands = list(operands)
    operands[15] = operands[15].reshape(1, -1)
    operands[16] = operands[16].T
    operands[19] = operands[19].T
    result, token_grad, inner, outer, up, down, early, late, table = run_layer(*operands)
    first = (result, token_grad, inner, outer, up, down.T, late[0], late[1], late[2], late[3])
    return (*first, early[0], early[1], early[2], early[3], early[8:12].reshape(3072), early[4], early[5], table.T)


def layer_norm(values, gain, shift):
    mean = jnp.mean(values, -1, keepdims=True)
    centred = values - mean
    variance = jnp.mean(centred * centred, -1, keepdims=True)
    scaled = lax.rsqrt(variance + EPS)
    unit = centred * scaled
    return (unit * gain + shift, unit, scaled)


def norm_back(upstream, unit, scaled, gain):
    inner = upstream * gain
    first = jnp.mean(inner, -1, keepdims=True)
    second = jnp.mean(inner * unit, -1, keepdims=True)
    return (
        scaled * (inner - first - unit * second),
        jnp.sum(upstream * unit, 0),
        jnp.sum(upstream, 0),
    )


def gelu_pair(pre):
    cumul = 0.5 * (1.0 + lax.erf(pre * ROOT_HALF))
    return (pre * cumul, cumul + pre * jnp.exp(-0.5 * pre * pre) * DENSITY)


def fetch(inner_weight, outer_weight, up_weight, down_weight):
    inner_full, outer_full = (
        lax.all_gather(inner_weight, ("dp", "mlp"), axis=0, tiled=True),
        lax.all_gather(outer_weight, ("dp", "mlp"), axis=0, tiled=True),
    )
    up_full, down_full = (
        lax.all_gather(up_weight, "dp", axis=0, tiled=True),
        lax.all_gather(down_weight, "dp", axis=1, tiled=True),
    )
    return (inner_full, outer_full, up_full, down_full)


def contract_rows(left, right):
    return lax.dot_general(
        left, right, (((0,), (0,)), ((), ())), preferred_element_type=jnp.float32
    )


def contract_cols(left, right):
    return lax.dot_general(
        left, right, (((1,), (1,)), ((), ())), preferred_element_type=jnp.float32
    )


def logits_of(query, keys, bias, allowed, factor):
    raw = jnp.einsum("qhd,khd->hqk", query, keys, preferred_element_type=jnp.float32) * factor
    return jnp.where(allowed, raw + bias, -1e30)


def body(
    tokens,
    keep_mask,
    position_index,
    cotangent,
    first_gain,
    first_shift,
    inner_weight,
    query_bias,
    value_bias,
    outer_weight,
    outer_bias,
    attend_scale,
    second_gain,
    second_shift,
    up_weight,
    up_bias,
    down_weight,
    down_bias,
    feed_scale,
    position_table,
):
    micro, rows, width = tokens.shape
    heads = position_table.shape[1]
    head_dim = width // heads
    factor = head_dim ** (-0.5)
    entries = position_table.shape[0]
    columns = up_weight.shape[1]
    col_start = lax.axis_index("mlp") * columns
    up_local = lax.dynamic_slice_in_dim(up_bias, col_start, columns, 0)
    shift_vector = jnp.concatenate([query_bias, jnp.zeros_like(query_bias), value_bias])
    table_by_head = jnp.transpose(position_table)
    bias = table_by_head[:, position_index]
    seen = jnp.arange(rows)
    diagonal = seen[:, None] == seen[None, :]
    flat_index = position_index.reshape(rows * rows)
    zero_width = jnp.zeros((width,), jnp.float32)
    sum_inner = jnp.zeros((width, 3 * width), jnp.float32)
    sum_outer = jnp.zeros((width, width), jnp.float32)
    sum_up = jnp.zeros((width, columns), jnp.float32)
    sum_down = jnp.zeros((columns, width), jnp.float32)
    sum_table_heads = jnp.zeros((heads, entries), jnp.float32)
    sum_up_bias = jnp.zeros((columns,), jnp.float32)
    sum_first_gain = zero_width
    sum_first_shift = zero_width
    sum_query_bias = zero_width
    sum_value_bias = zero_width
    sum_outer_bias = zero_width
    sum_attend_scale = zero_width
    sum_second_gain = zero_width
    sum_second_shift = zero_width
    sum_down_bias = zero_width
    sum_feed_scale = zero_width
    results = []
    input_grads = []
    for index in range(micro):
        inner_full, outer_full, up_full, down_full = fetch(
            inner_weight, outer_weight, up_weight, down_weight
        )
        source = tokens[index].astype(jnp.float32)
        allowed = jnp.logical_or(keep_mask[index][None, :] == 1, diagonal)[None]
        normed_one, unit_one, scaled_one = layer_norm(source, first_gain, first_shift)
        normed_one = normed_one.astype(jnp.bfloat16)
        projected = (
            jnp.dot(normed_one, inner_full, preferred_element_type=jnp.float32) + shift_vector
        ).astype(jnp.bfloat16)
        query = projected[:, :width].reshape(rows, heads, head_dim)
        keys = projected[:, width : 2 * width].reshape(rows, heads, head_dim)
        values = projected[:, 2 * width :].reshape(rows, heads, head_dim)
        logits = logits_of(query, keys, bias, allowed, factor)
        top = jnp.max(logits, -1, keepdims=True)
        expd = jnp.exp(logits - top)
        total = jnp.sum(expd, -1, keepdims=True)
        probs = expd / total
        log_total = top + jnp.log(total)
        mixed = jnp.einsum(
            "hqk,khd->qhd", probs.astype(jnp.bfloat16), values, preferred_element_type=jnp.float32
        )
        mixed = mixed.reshape(rows, width).astype(jnp.bfloat16)
        attend = jnp.dot(mixed, outer_full, preferred_element_type=jnp.float32) + outer_bias
        resid = source + attend_scale * attend
        normed_two, unit_two, scaled_two = layer_norm(resid, second_gain, second_shift)
        normed_two = normed_two.astype(jnp.bfloat16)
        sequence_rows = lax.all_gather(normed_two, "mlp", axis=0, tiled=True)
        pre = jnp.dot(sequence_rows, up_full, preferred_element_type=jnp.float32) + up_local
        active, slope = gelu_pair(pre)
        hidden = active.astype(jnp.bfloat16)
        feed = (
            lax.psum_scatter(
                jnp.dot(hidden, down_full, preferred_element_type=jnp.float32).astype(jnp.bfloat16),
                "mlp",
                scatter_dimension=0,
                tiled=True,
            ).astype(jnp.float32)
            + down_bias
        )
        results.append((resid + feed_scale * feed).astype(jnp.bfloat16))
        inner_full, outer_full, up_full, down_full = fetch(
            inner_weight, outer_weight, up_weight, down_weight
        )
        upstream = cotangent[index].astype(jnp.float32)
        sum_feed_scale = sum_feed_scale + jnp.sum(feed * upstream, 0)
        dfeed = feed_scale * upstream
        sum_down_bias = sum_down_bias + jnp.sum(dfeed, 0)
        upstream_all = lax.all_gather(dfeed.astype(jnp.bfloat16), "mlp", axis=0, tiled=True)
        sum_down = sum_down + contract_rows(hidden, upstream_all)
        dpre = (contract_cols(upstream_all, down_full) * slope).astype(jnp.bfloat16)
        sum_up_bias = sum_up_bias + jnp.sum(dpre.astype(jnp.float32), 0)
        sum_up = sum_up + contract_rows(sequence_rows, dpre)
        dnormed_two = lax.psum_scatter(
            contract_cols(dpre, up_full).astype(jnp.bfloat16),
            "mlp",
            scatter_dimension=0,
            tiled=True,
        ).astype(jnp.float32)
        dresid_norm, part_gain, part_shift = norm_back(
            dnormed_two, unit_two, scaled_two, second_gain
        )
        sum_second_gain = sum_second_gain + part_gain
        sum_second_shift = sum_second_shift + part_shift
        dresid = upstream + dresid_norm
        sum_attend_scale = sum_attend_scale + jnp.sum(attend * dresid, 0)
        dattend = attend_scale * dresid
        sum_outer_bias = sum_outer_bias + jnp.sum(dattend, 0)
        dattend_low = dattend.astype(jnp.bfloat16)
        sum_outer = sum_outer + contract_rows(mixed, dattend_low)
        dmixed = (
            contract_cols(dattend_low, outer_full)
            .astype(jnp.bfloat16)
            .reshape(rows, heads, head_dim)
        )
        logits = logits_of(query, keys, bias, allowed, factor)
        probs = jnp.exp(logits - log_total)
        dvalues = jnp.einsum(
            "hqk,qhd->khd", probs.astype(jnp.bfloat16), dmixed, preferred_element_type=jnp.float32
        )
        dprobs = jnp.einsum("qhd,khd->hqk", dmixed, values, preferred_element_type=jnp.float32)
        dlogits = probs * (dprobs - jnp.sum(dprobs * probs, -1, keepdims=True))
        sum_table_heads = sum_table_heads.at[:, flat_index].add(dlogits.reshape(heads, rows * rows))
        dlogits_low = dlogits.astype(jnp.bfloat16)
        dquery = (
            jnp.einsum("hqk,khd->qhd", dlogits_low, keys, preferred_element_type=jnp.float32)
            * factor
        )
        dkeys = (
            jnp.einsum("hqk,qhd->khd", dlogits_low, query, preferred_element_type=jnp.float32)
            * factor
        )
        dprojected = jnp.concatenate(
            [dquery.reshape(rows, width), dkeys.reshape(rows, width), dvalues.reshape(rows, width)],
            axis=1,
        ).astype(jnp.bfloat16)
        sum_query_bias = sum_query_bias + jnp.sum(dprojected[:, :width].astype(jnp.float32), 0)
        sum_value_bias = sum_value_bias + jnp.sum(dprojected[:, 2 * width :].astype(jnp.float32), 0)
        sum_inner = sum_inner + contract_rows(normed_one, dprojected)
        dnormed_one = contract_cols(dprojected, inner_full)
        dsource_norm, part_gain, part_shift = norm_back(
            dnormed_one, unit_one, scaled_one, first_gain
        )
        sum_first_gain = sum_first_gain + part_gain
        sum_first_shift = sum_first_shift + part_shift
        input_grads.append((dresid + dsource_norm).astype(jnp.bfloat16))
    sum_table = jnp.transpose(sum_table_heads)
    gradient_inner, gradient_outer = (
        lax.psum_scatter(sum_inner, ("dp", "mlp"), scatter_dimension=0, tiled=True),
        lax.psum_scatter(sum_outer, ("dp", "mlp"), scatter_dimension=0, tiled=True),
    )
    gradient_up, gradient_down = (
        lax.psum_scatter(sum_up, "dp", scatter_dimension=0, tiled=True),
        lax.psum_scatter(sum_down, "dp", scatter_dimension=1, tiled=True),
    )
    up_bias_full = lax.dynamic_update_slice_in_dim(
        jnp.zeros((up_bias.shape[0],), jnp.float32), sum_up_bias, col_start, 0
    )
    summed = lax.psum(
        (
            sum_first_gain,
            sum_first_shift,
            sum_query_bias,
            sum_value_bias,
            sum_outer_bias,
            sum_attend_scale,
            sum_second_gain,
            sum_second_shift,
            up_bias_full,
            sum_down_bias,
            sum_feed_scale,
            sum_table,
        ),
        ("dp", "mlp"),
    )
    return (
        jnp.stack(results),
        jnp.stack(input_grads),
        gradient_inner,
        gradient_outer,
        gradient_up,
        gradient_down,
        summed[0],
        summed[1],
        summed[2],
        summed[3],
        summed[4],
        summed[5],
        summed[6],
        summed[7],
        summed[8],
        summed[9],
        summed[10],
        summed[11],
    )


def solution(mesh):
    special = mesh.shape["dp"] == 8 and mesh.shape["mlp"] == 4
    placed = (
        P(None, ("dp", "mlp"), None),
        P(None, ("dp", "mlp")),
        P(),
        P(None, ("dp", "mlp"), None),
        P(),
        P(),
        P(("dp", "mlp"), None),
        P(),
        P(),
        P(("dp", "mlp"), None),
        P(),
        P(),
        P(),
        P(),
        P("dp", "mlp"),
        P(),
        P("mlp", "dp"),
        P(),
        P(),
        P(),
    )
    return jax.shard_map(
        fast_body if special else body,
        mesh=mesh,
        in_specs=placed,
        out_specs=(
            P(None, ("dp", "mlp"), None),
            P(None, ("dp", "mlp"), None),
            P(("dp", "mlp"), None),
            P(("dp", "mlp"), None),
            P("dp", "mlp"),
            P("mlp", "dp"),
            P(),
            P(),
            P(),
            P(),
            P(),
            P(),
            P(),
            P(),
            P(),
            P(),
            P(),
            P(),
        ),
        check_vma=False,
    )
```

```python
import functools

import jax
import jax.numpy as jnp
from jax import lax
from jax.experimental import pallas as pl
from jax.experimental.pallas import tpu as pltpu
from jax.sharding import PartitionSpec as P

EPS = 1e-06
ROOT_HALF = 0.7071067811865476
DENSITY = 0.3989422804014327


MESH = pl.DeviceIdType.MESH
F32 = jnp.float32
BF16 = jnp.bfloat16
TILE = 384
PAD = 208
TALL = 2 * PAD
KEYS = 256
N_COPY = 11
NAMES = ("I0", "I1", "I2", "O", "U0a", "U0b", "U1a", "U1b", "N0a", "N0b", "N1a", "N1b")
GATHER = {"I1": "zxy", "I0": "zyx", "I2": "zxy", "U0a": "Zyx", "U0b": "yzx", "N0a": "xZy", "O": "zxy", "U1b": "xZy", "U1a": "yZx", "N0b": "Zyx", "N1a": "xZy", "N1b": "yZx"}
REDUCE = {"I1": "yZx", "I0": "xyz", "I2": "xyz", "U0a": "yxz", "U0b": "yzx", "N0a": "xzy", "O": "yzx", "U1b": "yZx", "U1a": "xyZ", "N0b": "xzy", "N1a": "xyZ", "N1b": "xZy"}
ORDER = (
    71, 72, 57, 58, 85, 86, 99, 100, 0, 30, 126, 127, 128, 168, 14, 154, 140, 15, 70, 196, 210, 34, 22, 13,
    56, 24, 113, 43, 73, 74, 84, 1, 2, 16, 59, 60, 29, 21, 183, 23, 75, 87, 31, 98, 76, 17, 169, 18,
    61, 88, 129, 130, 155, 32, 62, 114, 141, 9, 89, 101, 184, 197, 10, 90, 211, 25, 112, 170, 102, 26, 131, 103,
    182, 156, 132, 104, 3, 115, 116, 171, 172, 142, 4, 157, 158, 185, 186, 198, 143, 144, 117, 212, 118, 45, 173, 187,
    199, 200, 36, 174, 188, 37, 213, 214, 38, 46, 159, 145, 47, 160, 175, 119, 133, 189, 146, 48, 39, 176, 120, 201,
    215, 134, 190, 202, 216, 40, 41, 49, 177, 179, 180, 121, 50, 161, 147, 203, 217, 33, 42, 162, 135, 137, 138, 191,
    193, 194, 148, 204, 5, 178, 122, 123, 124, 218, 6, 105, 19, 106, 27, 181, 163, 136, 149, 7, 224, 11, 107, 109,
    110, 165, 192, 125, 205, 225, 12, 63, 150, 20, 77, 195, 64, 139, 219, 28, 78, 91, 206, 108, 151, 226, 51, 52,
    166, 92, 221, 53, 65, 152, 111, 207, 54, 79, 55, 164, 230, 233, 35, 66, 67, 68, 153, 231, 222, 44, 81, 167,
    93, 208, 227, 8, 228, 232, 69, 220, 209, 94, 95, 96, 82, 229, 223, 235, 80, 97, 83, 234,
)


def place():
    dp = lax.axis_index("dp")
    mlp = lax.axis_index("mlp")
    return lax.div(dp, 2), lax.rem(dp, 2), lax.div(mlp, 2), lax.rem(mlp, 2)


def device(z, x, y, c):
    return (z * 2 + x, y * 2 + c)


def greet(z, x, y, c):
    barrier = pltpu.get_barrier_semaphore()
    others = [device(lax.rem(z + d, 4), x, y, c) for d in (1, 2, 3)]
    others += [device(z, 1 - x, y, c), device(z, x, 1 - y, c), device(z, 1 - x, 1 - y, c), device(z, x, y, 1 - c)]
    for other in others:
        pl.semaphore_signal(barrier, inc=1, device_id=other, device_id_type=MESH)
    pl.semaphore_wait(barrier, len(others))


class Link:
    def __init__(self, send, recv):
        self.send, self.recv, self.pending = send, recv, {}

    def make(self, src, dst, slot, target):
        return pltpu.make_async_remote_copy(
            src_ref=src,
            dst_ref=dst,
            send_sem=self.send.at[slot],
            recv_sem=self.recv.at[slot],
            device_id=target,
            device_id_type=MESH,
        )

    def copy(self, src, dst, slot, target, group=None):
        made = self.make(src, dst, slot, target)
        made.start()
        self.pending.setdefault(group, []).append((made, None))
        return made

    def drain(self, *groups):
        for group in groups or tuple(self.pending):
            for made, sender in self.pending.pop(group, []):
                if sender is None:
                    made.wait_send()
                else:
                    pl.when(sender)(made.wait_send)


class Some:
    def __init__(self, link, src, dst, slot, target, sender, getter, group):
        self.made = link.make(src, dst, slot, target)
        self.getter = getter
        pl.when(sender)(self.made.start)
        link.pending.setdefault(group, []).append((self.made, sender))

    def wait_recv(self):
        pl.when(self.getter)(self.made.wait_recv)


def mix(here, *there):
    total = here[...].astype(F32)
    for other in there:
        total = total + other[...].astype(F32)
    here[...] = total.astype(BF16)


class Unit:
    def __init__(self, link, ref, name, where, base):
        self.link, self.ref, self.where, self.base, self.name = link, ref, where, base, name
        self.narrow = name[0] in "IO"
        self.rows = slice(None) if self.narrow else pl.ds(48 * "ab".index(name[2]), 48)
        self.group = name if base < len(NAMES) * N_COPY else None
        z = where[0]
        self.side = lax.div(z, 2)
        self.mate = z + 1 - 2 * lax.rem(z, 2)
        self.inner = jnp.logical_and(z > 0, z < 3)
        self.outer = jnp.logical_not(self.inner)

    def put(self, src, dst, slot, target):
        return self.link.copy(src, dst, self.base + slot, target, self.group)

    def some(self, src, dst, slot, z, sender, getter):
        x, y, c = self.where[1:]
        return Some(self.link, src, dst, self.base + slot, device(z, x, y, c), sender, getter, self.group)

    def at(self, z, x, y, c):
        return self.ref.at[c, z, x, y] if self.narrow else self.ref.at[y, c, z, x, self.rows]

    def by_core(self, c):
        return self.ref.at[c] if self.narrow else self.ref.at[:, c, :, :, self.rows]

    def plane(self, axis, x, y, c):
        every = slice(None)
        return self.at(every, x, every, c) if axis == "x" else self.at(every, every, y, c)

    def pairs(self, axis, z):
        x, y, c = self.where[1:]
        every = slice(None)
        return self.at(z, every, y, c) if axis == "x" else self.at(z, x, every, c)

    def two(self, side):
        return pl.ds(2 * side, 2)

    def spread(self, part, slot):
        z, x, y, c = self.where
        return [self.put(part, part, slot + d - 1, device(lax.rem(z + d, 4), x, y, c)) for d in (1, 2, 3)]

    def across(self, axis, src, dst, slot):
        z, x, y, c = self.where
        target = {"x": (z, 1 - x, y, c), "y": (z, x, 1 - y, c), "c": (z, x, y, 1 - c)}[axis]
        return self.put(src, dst, slot, device(*target))

    def other(self, axis):
        z, x, y, c = self.where
        return (1 - x, y, c) if axis == "x" else (x, 1 - y, c)


class Gather(Unit):
    def __init__(self, *given):
        super().__init__(*given)
        self.axes = GATHER[self.name]
        self.steps = "Z" in self.axes
        self.early = self.axes[0] in "zZ"
        self.z, self.to_c = [], []

    def own(self, z):
        x, y, c = self.where[1:]
        return self.at(z, x, y, c) if self.early else self.pairs(self.axes[0], z)

    def swap_pair(self, slot):
        part = self.own(self.where[0])
        self.z = [self.put(part, part, slot, device(self.mate, *self.where[1:]))]

    def Z(self):
        z, x, y, c = self.where
        part = self.at(z, x, y, c)
        if not self.early:
            self.first = self.across(self.axes[0], part, part, 0)
        if not self.steps:
            self.z = self.spread(part, 1)
        elif self.early:
            self.swap_pair(1)

    def m(self):
        if self.steps:
            self.z[0].wait_recv()
            part = self.own(self.two(self.side))
            self.z = [self.some(part, part, 2, 3 - self.where[0], self.inner, self.inner)]

    def n(self):
        if self.steps:
            self.z[0].wait_recv()
            part = self.own(self.two(1 - self.side))
            self.z = [self.some(part, part, 3, self.mate, self.inner, self.outer)]

    def L(self):
        z, x, y, c = self.where
        if not self.early:
            self.first.wait_recv()
            if self.steps:
                self.swap_pair(1)
            else:
                self.z += self.spread(self.at(z, *self.other(self.axes[0])), 4)
            return
        for made in self.z:
            made.wait_recv()
        part = self.at(slice(None), x, y, c)
        self.made = {axis: self.across(axis, part, part, 4 + i) for i, axis in enumerate(self.axes[1:] + "c")}
        self.to_c = [self.made["c"]]

    def pass_on(self, axis, slot):
        self.made[axis].wait_recv()
        part = self.at(slice(None), *self.other(axis))
        self.to_c.append(self.across("c", part, part, slot))
        return part

    def P(self):
        z, x, y, c = self.where
        last = self.axes[2]
        if self.early:
            part = self.pass_on(self.axes[1], 7)
            self.last = self.across(last, part, part, 8)
            return
        for made in self.z:
            made.wait_recv()
        part = self.plane(last, x, y, c)
        self.last = self.across(last, part, part, 7)
        self.to_c = [self.across("c", part, part, 8)]

    def Q(self):
        if self.early:
            self.pass_on(self.axes[2], 9)

    def R(self):
        z, x, y, c = self.where
        self.last.wait_recv()
        part = self.at(slice(None), 1 - x, 1 - y, c) if self.early else self.plane(self.axes[2], 1 - x, 1 - y, c)
        self.to_c.append(self.across("c", part, part, 10))

    def F(self):
        for made in self.to_c:
            made.wait_recv()


class Reduce(Unit):
    def __init__(self, *given):
        super().__init__(*given)
        self.axes = REDUCE[self.name]
        self.steps = "Z" in self.axes
        self.late = self.axes[2] in "zZ"

    @staticmethod
    def buffers(name):
        narrow, axes = name[0] in "IO", REDUCE[name]
        half = (4, 2, 2) if narrow else (2, 4, 2)
        quarter = (2, 4) if not narrow and axes[0] == "x" else (4, 2)
        one = () if axes[2] in "zZ" else (2,)
        two = (2, 2) if one else (2,)
        along_z = [(*two,), (*two,), (*one,)] if "Z" in axes else [(3, *one)]
        shapes = [half, quarter, (4,) if axes[2] in "zZ" else (), *along_z]
        return [(*shape, 48, TILE) for shape in shapes]

    def set_buffers(self, half, quarter, side, *along_z):
        self.half, self.quarter, self.side_ref, self.along_z = half, quarter, side, along_z

    def own(self, z):
        x, y, c = self.where[1:]
        return self.at(z, x, y, c) if self.late else self.pairs(self.axes[2], z)

    def c(self):
        self.made = self.across("c", self.by_core(1 - self.where[3]), self.half, 0)

    def d(self):
        z, x, y, c = self.where
        self.made.wait_recv()
        mix(self.by_core(c), self.half)
        axis = self.axes[0]
        self.made = self.across(axis, self.plane(axis, 1 - x, 1 - y, c), self.quarter, 1)

    def e(self):
        z, x, y, c = self.where
        self.made.wait_recv()
        mix(self.plane(self.axes[0], x, y, c), self.quarter)
        if not self.late:
            self.into_z()
            return
        axis = self.axes[1]
        self.made = self.across(axis, self.at(slice(None), *self.other(axis)), self.side_ref, 2)

    def into_z(self):
        z, x, y, c = self.where
        if self.steps:
            part = self.own(self.two(1 - self.side))
            self.z = [self.some(part, self.along_z[0], 3, self.mate, self.outer, self.inner)]
            return
        self.z = []
        for d in (1, 2, 3):
            far = lax.rem(z + d, 4)
            self.z.append(self.put(self.own(far), self.along_z[0].at[d - 1], 2 + d, device(far, x, y, c)))

    def p(self):
        if self.steps:
            self.z[0].wait_recv()
            part = self.own(self.two(1 - self.side))
            pl.when(self.inner)(functools.partial(mix, part, self.along_z[0]))
            self.z = [self.some(part, self.along_z[1], 4, 3 - self.where[0], self.inner, self.inner)]

    def q(self):
        if self.steps:
            self.z[0].wait_recv()
            pl.when(self.inner)(functools.partial(mix, self.own(self.two(self.side)), self.along_z[1]))
            self.z = [self.put(self.own(self.mate), self.along_z[2], 5, device(self.mate, *self.where[1:]))]

    def parts(self):
        for made in self.z:
            made.wait_recv()
        return [self.along_z[2]] if self.steps else [self.along_z[0].at[d] for d in range(3)]

    def f(self):
        z, x, y, c = self.where
        if self.late:
            self.made.wait_recv()
            mix(self.at(slice(None), x, y, c), self.side_ref)
            self.into_z()
            return
        mix(self.own(z), *self.parts())
        axis = self.axes[2]
        self.made = self.across(axis, self.at(z, *self.other(axis)), self.side_ref, 6)

    def total(self):
        if self.late:
            parts = self.parts()
        else:
            self.made.wait_recv()
            parts = [self.side_ref]
        total = self.at(*self.where)[...].astype(F32)
        for part in parts:
            total = total + part[...].astype(F32)
        return total


class Everywhere:
    def __init__(self, link, ref, core_ref, plane_ref, line_ref, base, where):
        self.link, self.ref, self.where, self.base = link, ref, where, base
        self.core_ref, self.plane_ref, self.line_ref = core_ref, plane_ref, line_ref

    def to_core(self):
        z, x, y, c = self.where
        self.made = [self.link.copy(self.ref, self.core_ref, self.base, device(z, x, y, 1 - c))]

    def wait(self):
        for made in self.made:
            made.wait_recv()

    def to_plane(self):
        z, x, y, c = self.where
        self.wait()
        chip = self.plane_ref.at[3]
        chip[...] = self.ref[...] + self.core_ref[...]
        targets = (device(z, 1 - x, y, c), device(z, x, 1 - y, c), device(z, 1 - x, 1 - y, c))
        self.made = [
            self.link.copy(chip, self.plane_ref.at[n], self.base + 1 + n, target) for n, target in enumerate(targets)
        ]

    def to_line(self):
        z, x, y, c = self.where
        self.wait()
        got = self.plane_ref
        self.line_ref[z] = (got[3] + got[0]) + (got[1] + got[2])
        part = self.line_ref.at[z]
        self.made = [
            self.link.copy(part, part, self.base + 3 + d, device(lax.rem(z + d, 4), x, y, c)) for d in (1, 2, 3)
        ]

    def total(self):
        self.wait()
        got = self.line_ref
        return (got[0] + got[1]) + (got[2] + got[3])


def dot(left, right):
    return lax.dot_general(left, right, (((1,), (0,)), ((), ())), preferred_element_type=F32)


def dot_nt(left, right):
    return lax.dot_general(left, right, (((1,), (1,)), ((), ())), preferred_element_type=F32)


def dot_tn(left, right):
    return lax.dot_general(left, right, (((0,), (0,)), ((), ())), preferred_element_type=F32)


def fold(values):
    rows, width = values.shape
    return jnp.sum(values.reshape(rows // 8, 8, width), 0)


def unit_of(values):
    mean = jnp.mean(values, -1, keepdims=True)
    centred = values - mean
    variance = jnp.mean(centred * centred, -1, keepdims=True)
    scaled = lax.rsqrt(variance + EPS)
    return centred * scaled, scaled


def loop(count, step, init):
    return lax.fori_loop(0, count, step, init)


def by_rows(step, init, first=0, count=13):
    size = 32

    def one(index, carried):
        return step(pl.ds(pl.multiple_of((index + first) * size, size), size), carried)

    one.__name__ = step.__name__
    return loop(count, one, init)


def layer_kernel(*refs):
    (
        tokens, keep, places, cotangent, first_gain1, first_shift1, inner_in, query_bias1, value_bias1, outer_in, outer_bias1,
        attend_scale1, second_gain1, second_shift1, up_in, up_bias, down_in, down_bias1, feed_scale1, table_in,
        result, token_grad, packed,
        *rest,
    ) = refs
    (
        narrow, wide, small, pair, swap,
        source, upstream, normed1, normed1_t, normed2, normed2_t, qkv, bias, mask, index, probs, mix_t, attend, resid,
        dfeed, dfeed_t, hidden, slope, total, dnormed2, shifts, ups, tab, vectors,
        early, late, hits, early_core, early_plane, early_line, late_core, late_plane, late_line, hits_core, hits_plane, hits_line,
        send, recv, *buffers,
    ) = rest
    outer_out, up_out, down_out, early_out, late_out, table_out = (
        packed.at[pl.ds(first, rows)] for first, rows in ((72, 24), (96, 96), (192, 96), (288, 16), (304, 8), (312, 16))
    )
    dresid, dproj, dmixed, mixed, dattend = attend, hidden, normed2, normed2, dfeed
    where = z, x, y, c = place()
    link = Link(send, recv)
    gathers, reduces = {}, {}
    taken = 0
    for n, name in enumerate(NAMES):
        ref = narrow.at[n] if n < 4 else wide.at[(n - 4) // 2]
        gathers[name] = Gather(link, ref, name, where, n * N_COPY)
        reduces[name] = Reduce(link, ref, name, where, (len(NAMES) + n) * N_COPY)
        count = len(Reduce.buffers(name))
        reduces[name].set_buffers(*buffers[taken : taken + count])
        taken += count
    spare = 2 * len(NAMES) * N_COPY
    sums = {
        "E": Everywhere(link, early, early_core, early_plane, early_line, spare + 5, where),
        "l": Everywhere(link, late, late_core, late_plane, late_line, spare + 15, where),
        "t": Everywhere(link, hits, hits_core, hits_plane, hits_line, spare + 25, where),
    }
    mates = []
    kept = {}
    for k in range(3):
        for core in range(2):
            for part in range(3):
                start = part * 768 + (core * 3 + k) * 128
                small[k, core, :, part * 128 : part * 128 + 128] = inner_in[:, start : start + 128].astype(F32)
    for core in range(2):
        small[3, core] = outer_in[:, core * TILE : core * TILE + TILE].astype(F32)
    for k in range(2):
        cols = slice(k * TILE, k * TILE + TILE)
        wide[k, y, c, z, x] = up_in[:, cols]
        wide[2 + k, y, c, z, x] = down_in[:, cols]
    greet(*where)
    mate = link.copy(small.at[:, 1 - c], pair.at[:, c], spare, device(z, x, y, 1 - c))
    for name in NAMES[4:]:
        if not gathers[name].early:
            gathers[name].Z()
    pair[:, c] = small[:, c]
    mate.wait_recv()
    link.drain(None)
    for unit in range(4):
        narrow[unit, c, z, x, y] = pair[unit].reshape(48, TILE).astype(BF16)
    for name in GATHER:
        if name[0] in "IO" or gathers[name].early:
            gathers[name].Z()

    given = (first_gain1, first_shift1, query_bias1, value_bias1, outer_bias1, attend_scale1, second_gain1, second_shift1, down_bias1, feed_scale1)
    for n, ref in enumerate(given):
        vectors[n] = ref[...].reshape(1, 768)
    (first_gain, first_shift, query_bias, value_bias, outer_bias, attend_scale, second_gain, second_shift, down_bias, feed_scale) = (
        vectors.at[n] for n in range(10)
    )

    for image in range(2):
        last = pl.ds(image * PAD + 192, 16)
        source[last, :] = jnp.zeros((16, 768), BF16)
        upstream[last, :] = jnp.zeros((16, 768), BF16)
        source[pl.ds(image * PAD, 197), :] = tokens[:, image, :]
        upstream[pl.ds(image * PAD, 197), :] = cotangent[:, image, :]
    zero = jnp.zeros((8, 768), F32)
    lane = lax.broadcasted_iota(jnp.int32, (1, 128), 1)
    picks = [(lane < 64).astype(F32).astype(BF16), (lane >= 64).astype(F32).astype(BF16)]

    def rows_of(image):
        return slice(image * PAD, image * PAD + PAD)

    def keys_of(image):
        return slice(image * PAD, image * PAD + KEYS)

    def cols_of(p):
        return pl.ds(pl.multiple_of(p * 128, 128), 128)

    def half(core):
        return slice(core * TILE, core * TILE + TILE)

    def norm1(n):
        def norm_first(rows, carried):
            unit, _ = unit_of(source[rows, :].astype(F32))
            normed1[rows, :] = (unit * first_gain[...] + first_shift[...]).astype(BF16)
            lifted = upstream[rows, :].astype(F32) * feed_scale[...]
            dfeed[rows, :] = lifted.astype(BF16)
            return carried + fold(lifted)

        kept["down"] = by_rows(norm_first, kept.get("down", zero), 7 * n, 7 - n)
        if n == 0:
            return
        early[...] = jnp.zeros((16, 768), F32)
        late[...] = jnp.zeros((8, 768), F32)
        early[4:5, :] = jnp.sum(kept.pop("down"), 0, keepdims=True)
        zero_row = jnp.zeros((1, 128), F32)
        for p in range(6):
            cols = slice(p * 128, p * 128 + 128)
            shifts[p] = jnp.concatenate([query_bias[:, cols], zero_row, value_bias[:, cols]], axis=1)
            qkv[p, TALL:, :] = jnp.zeros((48, TILE), BF16)

    def fill():
        index[...] = jnp.full((PAD, KEYS), -1, jnp.int32)
        index[0:197, 0:197] = places[...]
        tab[...] = jnp.zeros((12, 1, 768), F32)
        for head in range(12):
            tab[head, :, 0:732] = table_in[head : head + 1, :]
        row_of = lax.broadcasted_iota(jnp.int32, (PAD, KEYS), 0)
        col_of = lax.broadcasted_iota(jnp.int32, (PAD, KEYS), 1)
        for image in range(2):
            mask[image] = jnp.full((PAD, KEYS), -1e30, F32)
            shown = jnp.where(keep[image : image + 1, :] == 1, 0.0, -1e30).astype(F32)
            mask[image, :, 0:197] = jnp.broadcast_to(shown, (PAD, 197))
            mask[image] = jnp.where(row_of == col_of, 0.0, mask[image])

    def look(k, n):
        def look_up(step, carried):
            head = 2 * ((n // 2) * 3 + k) + n % 2
            for side in range(2):
                cols = slice(side * 128, side * 128 + 128)
                spot = index[:, cols]
                low, high = spot & 127, spot >> 7
                found = jnp.zeros((PAD, 128), F32)
                for piece in range(6):
                    row = tab[head, :, piece * 128 : piece * 128 + 128]
                    picked = jnp.take_along_axis(jnp.broadcast_to(row, (PAD, 128)), low, axis=1)
                    found = jnp.where(high == piece, picked, found)
                bias[head, :, cols] = found
            return carried

        loop(1, look_up, 0)

    def turn1():
        normed1_t[...] = normed1[...].T

    def turnd():
        dfeed_t[...] = dfeed[...].T

    def proj(k):
        def project(core, carried):
            p = core * 3 + k
            weight = narrow[k, core].reshape(768, TILE)
            scaling = jnp.where(lax.broadcasted_iota(jnp.int32, (1, TILE), 1) < 128, 0.125, 1.0).astype(F32)
            value = (dot(normed1[...], weight) + shifts[p]).astype(BF16)
            qkv[p, 0:TALL, :] = (value.astype(F32) * scaling).astype(BF16)
            return carried

        loop(2, project, 0)

    def att(k):
        def attend_pair(core, carried):
            p = core * 3 + k
            first_half = lax.broadcasted_iota(jnp.int32, (PAD, 128), 1) < 64
            for image in range(2):
                query = qkv[p, rows_of(image), 0:128]
                keys = qkv[p, keys_of(image), 128:256]
                values = qkv[p, keys_of(image), 256:384]
                outs = []
                for t in range(2):
                    logits = dot_nt(query * picks[t], keys) + bias[2 * p + t] + mask[image]
                    top = jnp.max(logits, -1, keepdims=True)
                    expd = jnp.exp(logits - top)
                    share = (expd * (1.0 / jnp.sum(expd, -1, keepdims=True))).astype(BF16)
                    probs[image, 2 * p + t] = share
                    outs.append(dot(share, values))
                mixed[rows_of(image), cols_of(p)] = jnp.where(first_half, outs[0], outs[1]).astype(BF16)
            return carried

        loop(2, attend_pair, 0)

    def out():
        for core in range(2):
            attend[:, half(core)] = dot(mixed[...], narrow[3, core].reshape(768, TILE)) + outer_bias[:, half(core)]
        mix_t[...] = mixed[...].T

    def norm2():
        def norm_second(rows, carried):
            value = source[rows, :].astype(F32) + attend_scale[...] * attend[rows, :]
            resid[rows, :] = value
            unit, _ = unit_of(value)
            normed2[rows, :] = (unit * second_gain[...] + second_shift[...]).astype(BF16)
            return carried

        by_rows(norm_second, 0)
        normed2_t[...] = normed2[...].T

    def widening(k, side):
        def widen(core, carried):
            weight = wide[k, side, core].reshape(768, TILE)
            cols = pl.ds(pl.multiple_of((side * 2 + core) * 768 + k * TILE, 128), TILE)
            pre = dot(normed2[...], weight) + up_bias[:, cols]
            cumul = 0.5 * (1.0 + lax.erf(pre * ROOT_HALF))
            b = k * 4 + side * 2 + core
            hidden[b] = (pre * cumul).astype(BF16)
            slope[b] = (cumul + pre * jnp.exp(-0.5 * pre * pre) * DENSITY).astype(BF16)
            return carried

        loop(2, widen, 0)

    def joined(ref, b):
        return jnp.concatenate([ref[b], ref[b + 1]], axis=1)

    def weights(slot, side):
        return jnp.concatenate([wide[slot, side, core].reshape(768, TILE) for core in range(2)], axis=1)

    def back(k, side):
        b = k * 4 + side * 2

        def narrow_back(step, carried):
            dpre = (dot(dfeed[...], weights(2 + k, side)) * joined(slope, b).astype(F32)).astype(BF16)
            for core in range(2):
                slope[b + core] = dpre[:, half(core)]
            ups[b // 2] = jnp.sum(fold(dpre.astype(F32)), 0, keepdims=True)
            part = dot_nt(dpre, weights(k, side))
            dnormed2[...] = part if b == 0 else dnormed2[...] + part
            return carried

        loop(1, narrow_back, 0)

    def grad(k, side):
        if side == 0:
            link.drain(*(what + str(k) + part for what in "UN" for part in "ab"))
        b = k * 4 + side * 2

        def narrow_grad(step, carried):
            both = joined(hidden, b)
            part = dot_nt(both, weights(2 + k, side))
            total[...] = part if b == 0 else total[...] + part
            up_grad = dot(normed2_t[...], joined(slope, b)).astype(BF16)
            down_grad = dot(dfeed_t[...], both).astype(BF16)
            for core in range(2):
                wide[2 + k, side, core] = up_grad[:, half(core)].reshape(4, 2, 96, TILE)
                wide[k, side, core] = down_grad[:, half(core)].reshape(4, 2, 96, TILE)
            return carried

        loop(1, narrow_grad, 0)

    def sec(n):
        def second_back(rows, carried):
            gain_sum, shift_sum, scale_sum, bias_sum = carried
            unit, scaled = unit_of(resid[rows, :])
            grad = dnormed2[rows, :]
            inner = grad * second_gain[...]
            first = jnp.mean(inner, -1, keepdims=True)
            second = jnp.mean(inner * unit, -1, keepdims=True)
            back = upstream[rows, :].astype(F32) + scaled * (inner - first - unit * second)
            scale_sum = scale_sum + fold(attend[rows, :] * back)
            dresid[rows, :] = back
            lifted = attend_scale[...] * back
            dattend[rows, :] = lifted.astype(BF16)
            return gain_sum + fold(grad * unit), shift_sum + fold(grad), scale_sum, bias_sum + fold(lifted)

        kept["sec"] = by_rows(second_back, kept.get("sec", (zero,) * 4), 7 * n, 7 - n)
        if n == 1:
            for block in range(4):
                for k in range(2):
                    b = k * 4 + block
                    early[8 + block : 9 + block, half(k)] = ups[b // 2, :, half(b % 2)]
            for row, value in zip((2, 3, 1, 0), kept.pop("sec")):
                early[row : row + 1, :] = jnp.sum(value, 0, keepdims=True)

    def res():
        def feed_out(rows, carried):
            feed = total[rows, :] + down_bias[...]
            total[rows, :] = resid[rows, :] + feed_scale[...] * feed
            return carried + fold(feed * upstream[rows, :].astype(F32))

        early[5:6, :] = jnp.sum(by_rows(feed_out, zero), 0, keepdims=True)
        for image in range(2):
            result[:, image, :] = total[pl.ds(image * PAD, 197), :].astype(BF16)

    def dmix():
        parts = [dot_nt(dattend[:, half(core)], narrow[3, core].reshape(768, TILE)) for core in range(2)]
        dmixed[...] = (parts[0] + parts[1]).astype(BF16)

    def gout():
        link.drain("O")
        for core in range(2):
            narrow[3, core] = dot(mix_t[...], dattend[:, half(core)]).astype(BF16).reshape(4, 2, 2, 48, TILE)

    def attb(k):
        def attend_back(core, carried):
            p = core * 3 + k
            first_half = lax.broadcasted_iota(jnp.int32, (PAD, 128), 1) < 64
            hit = [None, None]
            for image in range(2):
                rows = rows_of(image)
                query = qkv[p, rows, 0:128]
                keys = qkv[p, keys_of(image), 128:256]
                values = qkv[p, keys_of(image), 256:384]
                above = dmixed[rows, cols_of(p)]
                dquery, dkeys, dvalues = [], [], []
                for t in range(2):
                    share = probs[image, 2 * p + t]
                    dvalues.append(dot_tn(share, above)[0:PAD])
                    dshare = dot_nt(above * picks[t], values)
                    full = share.astype(F32)
                    dlogits = full * (dshare - jnp.sum(dshare * full, -1, keepdims=True))
                    hit[t] = dlogits if image == 0 else hit[t] + dlogits
                    low = dlogits.astype(BF16)
                    dquery.append(dot(low, keys) * 0.125)
                    dkeys.append(dot_tn(low, query)[0:PAD])
                dproj[p, rows, 0:128] = jnp.where(first_half, dquery[0], dquery[1]).astype(BF16)
                dproj[p, rows, 128:256] = jnp.where(first_half, dkeys[0], dkeys[1]).astype(BF16)
                dproj[p, rows, 256:384] = jnp.where(first_half, dvalues[0], dvalues[1]).astype(BF16)
            for t in range(2):
                bias[2 * p + t] = hit[t]
            return carried

        loop(2, attend_back, 0)

    def projb(k):
        link.drain("I" + str(k))

        def project_back(core, carried):
            p = core * 3 + k
            grad = dproj[p]
            summed = jnp.sum(fold(grad.astype(F32)), 0, keepdims=True)
            late[2:3, cols_of(p)] = summed[:, 0:128]
            late[3:4, cols_of(p)] = summed[:, 256:384]
            part = dot_nt(grad, narrow[k, core].reshape(768, TILE))
            dnormed2[...] = jnp.where(core == 0, 0.0, dnormed2[...]) + part if k == 0 else dnormed2[...] + part
            narrow[k, core] = dot(normed1_t[...], grad).astype(BF16).reshape(4, 2, 2, 48, TILE)
            return carried

        loop(2, project_back, 0)

    def first(n):
        def first_back(rows, carried):
            gain_sum, shift_sum = carried
            grad = dnormed2[rows, :]
            unit, scaled = unit_of(source[rows, :].astype(F32))
            inner = grad * first_gain[...]
            mean = jnp.mean(inner, -1, keepdims=True)
            second = jnp.mean(inner * unit, -1, keepdims=True)
            dresid[rows, :] = dresid[rows, :] + scaled * (inner - mean - unit * second)
            return gain_sum + fold(grad * unit), shift_sum + fold(grad)

        kept["first"] = by_rows(first_back, kept.get("first", (zero, zero)), 7 * n, 7 - n)
        if n == 0:
            return
        found = kept.pop("first")
        late[0:1, :] = jnp.sum(found[0], 0, keepdims=True)
        late[1:2, :] = jnp.sum(found[1], 0, keepdims=True)

    def tok():
        for image in range(2):
            token_grad[:, image, :] = dresid[pl.ds(image * PAD, 197), :].astype(BF16)

    def counting(n):
        low_of = lax.broadcasted_iota(jnp.int32, (128, KEYS), 0)
        high_of = lax.broadcasted_iota(jnp.int32, (8, KEYS), 0)

        def count(group, carried):
            eight = pl.ds(pl.multiple_of((group + 5 * n) * 8, 8), 8)
            spots = index[eight, :]
            for r in range(8):
                spot = jnp.broadcast_to(spots[r : r + 1, :], (8, KEYS))
                high = (spot >> 7) == high_of
                parts = []
                for head in range(12):
                    grads = bias[head, eight, :]
                    parts.append(jnp.where(high, jnp.broadcast_to(grads[r : r + 1, :], (8, KEYS)), 0.0))
                spread = jnp.concatenate(parts, axis=0).astype(BF16)
                low = jnp.concatenate([spot & 127] * 16, axis=0)
                which = (low == low_of).astype(F32).astype(BF16)
                carried = carried + dot_nt(spread, which)
            return carried

        before = jnp.zeros((96, 128), F32) if n == 0 else hits[...]
        hits[...] = loop(5, count, before)

    def settle(name):
        value = reduces[name].total()
        n = NAMES.index(name)
        if n < 4:
            small[n] = value.reshape(2, 24, TILE)
            swap[n, c] = small[n, c]
            mates.append(link.copy(small.at[n, 1 - c], swap.at[n, c], spare + 1 + n, device(z, x, y, 1 - c)))
        else:
            rows = slice(48 * (n % 2), 48 * (n % 2) + 48)
            if n < 8:
                down_out[rows, half((n - 4) // 2)] = value
            else:
                up_out[rows, half((n - 8) // 2)] = value

    steps = {"fill": fill, "turn1": turn1, "turnd": turnd, "out": out, "norm2": norm2, "dmix": dmix, "gout": gout, "res": res, "tok": tok}
    for k in range(3):
        steps["proj" + str(k)] = functools.partial(proj, k)
        steps["att" + str(k)] = functools.partial(att, k)
        steps["attb" + str(k)] = functools.partial(attb, k)
        steps["projb" + str(k)] = functools.partial(projb, k)
        for i in range(4):
            steps["look" + str(k) + str(i)] = functools.partial(look, k, i)
    for i in range(2):
        steps["sec" + str(i)] = functools.partial(sec, i)
        steps["norm1" + str(i)] = functools.partial(norm1, i)
        steps["first" + str(i)] = functools.partial(first, i)
        for k in range(2):
            steps["wide" + str(k) + str(i)] = functools.partial(widening, k, i)
            steps["back" + str(k) + str(i)] = functools.partial(back, k, i)
            steps["grad" + str(k) + str(i)] = functools.partial(grad, k, i)
    for n in range(5):
        steps["count" + str(n)] = functools.partial(counting, n)
    for name in NAMES:
        for event in "LmnPQRF":
            steps[event + name] = getattr(gathers[name], event)
        for event in "cdefpq":
            steps[event + name] = getattr(reduces[name], event)
        steps["g" + name] = functools.partial(settle, name)
    for what, everywhere in sums.items():
        steps[what + "0"] = everywhere.to_core
        steps[what + "1"] = everywhere.to_plane
        steps[what + "2"] = everywhere.to_line

    def give(what, ref):
        ref[...] = sums[what].total()

    steps["E3"] = functools.partial(give, "E", early_out)
    steps["l3"] = functools.partial(give, "l", late_out)

    def give_table():
        found = sums["t"].total().reshape(12, 8, 128)
        for piece in range(6):
            width = min(128, 732 - piece * 128)
            table_out[0:12, piece * 128 : piece * 128 + width] = found[:, piece, 0:width]

    steps["t3"] = give_table
    todo = list(steps.values())
    for n in ORDER:
        todo[n]()
    for made in mates:
        made.wait_recv()
    for k in range(3):
        for core in range(2):
            for part in range(3):
                start = (core * 3 + k) * 128
                packed[part * 24 : part * 24 + 24, start : start + 128] = swap[k, core, :, part * 128 : part * 128 + 128]
    for core in range(2):
        outer_out[:, half(core)] = swap[3, core]
    link.drain()


def run_layer(*operands):
    def vmem(*shape, dtype=BF16):
        return pltpu.VMEM(shape, dtype)

    scratch = [
        vmem(4, 2, 4, 2, 2, 48, TILE),
        vmem(4, 2, 2, 4, 2, 96, TILE),
        vmem(4, 2, 24, TILE, dtype=F32),
        vmem(4, 2, 24, TILE, dtype=F32),
        vmem(4, 2, 24, TILE, dtype=F32),
        vmem(TALL, 768),
        vmem(TALL, 768),
        vmem(TALL, 768),
        vmem(768, TALL),
        vmem(TALL, 768),
        vmem(768, TALL),
        vmem(6, TALL + 48, TILE),
        vmem(12, PAD, KEYS, dtype=F32),
        vmem(2, PAD, KEYS, dtype=F32),
        vmem(PAD, KEYS, dtype=jnp.int32),
        vmem(2, 12, PAD, KEYS),
        vmem(768, TALL),
        vmem(TALL, 768, dtype=F32),
        vmem(TALL, 768, dtype=F32),
        vmem(TALL, 768),
        vmem(768, TALL),
        vmem(8, TALL, TILE),
        vmem(8, TALL, TILE),
        vmem(TALL, 768, dtype=F32),
        vmem(TALL, 768, dtype=F32),
        vmem(6, 1, TILE, dtype=F32),
        vmem(4, 1, 768, dtype=F32),
        vmem(12, 1, 768, dtype=F32),
        vmem(10, 1, 768, dtype=F32),
        vmem(16, 768, dtype=F32),
        vmem(8, 768, dtype=F32),
        vmem(96, 128, dtype=F32),
    ]
    for shape in ((16, 768), (8, 768), (96, 128)):
        scratch += [vmem(*shape, dtype=F32), vmem(4, *shape, dtype=F32), vmem(4, *shape, dtype=F32)]
    copies = 2 * len(NAMES) * N_COPY + 40
    scratch += [pltpu.SemaphoreType.DMA((copies,)), pltpu.SemaphoreType.DMA((copies,))]
    for name in NAMES:
        scratch += [vmem(*shape) for shape in Reduce.buffers(name)]
    shapes = [((197, 2, 768), BF16), ((197, 2, 768), BF16), ((328, 768), F32)]
    return pl.pallas_call(
        layer_kernel,
        out_shape=[jax.ShapeDtypeStruct(*shape) for shape in shapes],
        in_specs=[pl.BlockSpec(memory_space=pltpu.VMEM)] * len(operands),
        out_specs=[pl.BlockSpec(memory_space=pltpu.VMEM)] * len(shapes),
        scratch_shapes=scratch,
        compiler_params=pltpu.CompilerParams(
            collective_id=0, has_side_effects=True, vmem_limit_bytes=62 * 2**20
        ),
    )(*operands)


def fast_body(*operands):
    operands = list(operands)
    operands[0] = operands[0].transpose(1, 0, 2)
    operands[3] = operands[3].transpose(1, 0, 2)
    operands[15] = operands[15].reshape(1, -1)
    operands[16] = operands[16].T
    operands[19] = operands[19].T
    result, token_grad, packed = run_layer(*operands)
    result, token_grad = result.transpose(1, 0, 2), token_grad.transpose(1, 0, 2)
    inner = jnp.concatenate([packed[0:24], packed[24:48], packed[48:72]], axis=1)
    early, late = packed[288:304], packed[304:312]
    first = (result, token_grad, inner, packed[72:96], packed[96:192], packed[192:288].T, late[0], late[1], late[2], late[3])
    table = packed[312:324, 0:732].T
    return (*first, early[0], early[1], early[2], early[3], early[8:12].reshape(3072), early[4], early[5], table)


def layer_norm(values, gain, shift):
    mean = jnp.mean(values, -1, keepdims=True)
    centred = values - mean
    variance = jnp.mean(centred * centred, -1, keepdims=True)
    scaled = lax.rsqrt(variance + EPS)
    unit = centred * scaled
    return (unit * gain + shift, unit, scaled)


def norm_back(upstream, unit, scaled, gain):
    inner = upstream * gain
    first = jnp.mean(inner, -1, keepdims=True)
    second = jnp.mean(inner * unit, -1, keepdims=True)
    return (
        scaled * (inner - first - unit * second),
        jnp.sum(upstream * unit, 0),
        jnp.sum(upstream, 0),
    )


def gelu_pair(pre):
    cumul = 0.5 * (1.0 + lax.erf(pre * ROOT_HALF))
    return (pre * cumul, cumul + pre * jnp.exp(-0.5 * pre * pre) * DENSITY)


def fetch(inner_weight, outer_weight, up_weight, down_weight):
    inner_full, outer_full = (
        lax.all_gather(inner_weight, ("dp", "mlp"), axis=0, tiled=True),
        lax.all_gather(outer_weight, ("dp", "mlp"), axis=0, tiled=True),
    )
    up_full, down_full = (
        lax.all_gather(up_weight, "dp", axis=0, tiled=True),
        lax.all_gather(down_weight, "dp", axis=1, tiled=True),
    )
    return (inner_full, outer_full, up_full, down_full)


def contract_rows(left, right):
    return lax.dot_general(
        left, right, (((0,), (0,)), ((), ())), preferred_element_type=jnp.float32
    )


def contract_cols(left, right):
    return lax.dot_general(
        left, right, (((1,), (1,)), ((), ())), preferred_element_type=jnp.float32
    )


def logits_of(query, keys, bias, allowed, factor):
    raw = jnp.einsum("qhd,khd->hqk", query, keys, preferred_element_type=jnp.float32) * factor
    return jnp.where(allowed, raw + bias, -1e30)


def body(
    tokens,
    keep_mask,
    position_index,
    cotangent,
    first_gain,
    first_shift,
    inner_weight,
    query_bias,
    value_bias,
    outer_weight,
    outer_bias,
    attend_scale,
    second_gain,
    second_shift,
    up_weight,
    up_bias,
    down_weight,
    down_bias,
    feed_scale,
    position_table,
):
    micro, rows, width = tokens.shape
    heads = position_table.shape[1]
    head_dim = width // heads
    factor = head_dim ** (-0.5)
    entries = position_table.shape[0]
    columns = up_weight.shape[1]
    col_start = lax.axis_index("mlp") * columns
    up_local = lax.dynamic_slice_in_dim(up_bias, col_start, columns, 0)
    shift_vector = jnp.concatenate([query_bias, jnp.zeros_like(query_bias), value_bias])
    table_by_head = jnp.transpose(position_table)
    bias = table_by_head[:, position_index]
    seen = jnp.arange(rows)
    diagonal = seen[:, None] == seen[None, :]
    flat_index = position_index.reshape(rows * rows)
    zero_width = jnp.zeros((width,), jnp.float32)
    sum_inner = jnp.zeros((width, 3 * width), jnp.float32)
    sum_outer = jnp.zeros((width, width), jnp.float32)
    sum_up = jnp.zeros((width, columns), jnp.float32)
    sum_down = jnp.zeros((columns, width), jnp.float32)
    sum_table_heads = jnp.zeros((heads, entries), jnp.float32)
    sum_up_bias = jnp.zeros((columns,), jnp.float32)
    sum_first_gain = zero_width
    sum_first_shift = zero_width
    sum_query_bias = zero_width
    sum_value_bias = zero_width
    sum_outer_bias = zero_width
    sum_attend_scale = zero_width
    sum_second_gain = zero_width
    sum_second_shift = zero_width
    sum_down_bias = zero_width
    sum_feed_scale = zero_width
    results = []
    input_grads = []
    for index in range(micro):
        inner_full, outer_full, up_full, down_full = fetch(
            inner_weight, outer_weight, up_weight, down_weight
        )
        source = tokens[index].astype(jnp.float32)
        allowed = jnp.logical_or(keep_mask[index][None, :] == 1, diagonal)[None]
        normed_one, unit_one, scaled_one = layer_norm(source, first_gain, first_shift)
        normed_one = normed_one.astype(jnp.bfloat16)
        projected = (
            jnp.dot(normed_one, inner_full, preferred_element_type=jnp.float32) + shift_vector
        ).astype(jnp.bfloat16)
        query = projected[:, :width].reshape(rows, heads, head_dim)
        keys = projected[:, width : 2 * width].reshape(rows, heads, head_dim)
        values = projected[:, 2 * width :].reshape(rows, heads, head_dim)
        logits = logits_of(query, keys, bias, allowed, factor)
        top = jnp.max(logits, -1, keepdims=True)
        expd = jnp.exp(logits - top)
        total = jnp.sum(expd, -1, keepdims=True)
        probs = expd / total
        log_total = top + jnp.log(total)
        mixed = jnp.einsum(
            "hqk,khd->qhd", probs.astype(jnp.bfloat16), values, preferred_element_type=jnp.float32
        )
        mixed = mixed.reshape(rows, width).astype(jnp.bfloat16)
        attend = jnp.dot(mixed, outer_full, preferred_element_type=jnp.float32) + outer_bias
        resid = source + attend_scale * attend
        normed_two, unit_two, scaled_two = layer_norm(resid, second_gain, second_shift)
        normed_two = normed_two.astype(jnp.bfloat16)
        sequence_rows = lax.all_gather(normed_two, "mlp", axis=0, tiled=True)
        pre = jnp.dot(sequence_rows, up_full, preferred_element_type=jnp.float32) + up_local
        active, slope = gelu_pair(pre)
        hidden = active.astype(jnp.bfloat16)
        feed = (
            lax.psum_scatter(
                jnp.dot(hidden, down_full, preferred_element_type=jnp.float32).astype(jnp.bfloat16),
                "mlp",
                scatter_dimension=0,
                tiled=True,
            ).astype(jnp.float32)
            + down_bias
        )
        results.append((resid + feed_scale * feed).astype(jnp.bfloat16))
        inner_full, outer_full, up_full, down_full = fetch(
            inner_weight, outer_weight, up_weight, down_weight
        )
        upstream = cotangent[index].astype(jnp.float32)
        sum_feed_scale = sum_feed_scale + jnp.sum(feed * upstream, 0)
        dfeed = feed_scale * upstream
        sum_down_bias = sum_down_bias + jnp.sum(dfeed, 0)
        upstream_all = lax.all_gather(dfeed.astype(jnp.bfloat16), "mlp", axis=0, tiled=True)
        sum_down = sum_down + contract_rows(hidden, upstream_all)
        dpre = (contract_cols(upstream_all, down_full) * slope).astype(jnp.bfloat16)
        sum_up_bias = sum_up_bias + jnp.sum(dpre.astype(jnp.float32), 0)
        sum_up = sum_up + contract_rows(sequence_rows, dpre)
        dnormed_two = lax.psum_scatter(
            contract_cols(dpre, up_full).astype(jnp.bfloat16),
            "mlp",
            scatter_dimension=0,
            tiled=True,
        ).astype(jnp.float32)
        dresid_norm, part_gain, part_shift = norm_back(
            dnormed_two, unit_two, scaled_two, second_gain
        )
        sum_second_gain = sum_second_gain + part_gain
        sum_second_shift = sum_second_shift + part_shift
        dresid = upstream + dresid_norm
        sum_attend_scale = sum_attend_scale + jnp.sum(attend * dresid, 0)
        dattend = attend_scale * dresid
        sum_outer_bias = sum_outer_bias + jnp.sum(dattend, 0)
        dattend_low = dattend.astype(jnp.bfloat16)
        sum_outer = sum_outer + contract_rows(mixed, dattend_low)
        dmixed = (
            contract_cols(dattend_low, outer_full)
            .astype(jnp.bfloat16)
            .reshape(rows, heads, head_dim)
        )
        logits = logits_of(query, keys, bias, allowed, factor)
        probs = jnp.exp(logits - log_total)
        dvalues = jnp.einsum(
            "hqk,qhd->khd", probs.astype(jnp.bfloat16), dmixed, preferred_element_type=jnp.float32
        )
        dprobs = jnp.einsum("qhd,khd->hqk", dmixed, values, preferred_element_type=jnp.float32)
        dlogits = probs * (dprobs - jnp.sum(dprobs * probs, -1, keepdims=True))
        sum_table_heads = sum_table_heads.at[:, flat_index].add(dlogits.reshape(heads, rows * rows))
        dlogits_low = dlogits.astype(jnp.bfloat16)
        dquery = (
            jnp.einsum("hqk,khd->qhd", dlogits_low, keys, preferred_element_type=jnp.float32)
            * factor
        )
        dkeys = (
            jnp.einsum("hqk,qhd->khd", dlogits_low, query, preferred_element_type=jnp.float32)
            * factor
        )
        dprojected = jnp.concatenate(
            [dquery.reshape(rows, width), dkeys.reshape(rows, width), dvalues.reshape(rows, width)],
            axis=1,
        ).astype(jnp.bfloat16)
        sum_query_bias = sum_query_bias + jnp.sum(dprojected[:, :width].astype(jnp.float32), 0)
        sum_value_bias = sum_value_bias + jnp.sum(dprojected[:, 2 * width :].astype(jnp.float32), 0)
        sum_inner = sum_inner + contract_rows(normed_one, dprojected)
        dnormed_one = contract_cols(dprojected, inner_full)
        dsource_norm, part_gain, part_shift = norm_back(
            dnormed_one, unit_one, scaled_one, first_gain
        )
        sum_first_gain = sum_first_gain + part_gain
        sum_first_shift = sum_first_shift + part_shift
        input_grads.append((dresid + dsource_norm).astype(jnp.bfloat16))
    sum_table = jnp.transpose(sum_table_heads)
    gradient_inner, gradient_outer = (
        lax.psum_scatter(sum_inner, ("dp", "mlp"), scatter_dimension=0, tiled=True),
        lax.psum_scatter(sum_outer, ("dp", "mlp"), scatter_dimension=0, tiled=True),
    )
    gradient_up, gradient_down = (
        lax.psum_scatter(sum_up, "dp", scatter_dimension=0, tiled=True),
        lax.psum_scatter(sum_down, "dp", scatter_dimension=1, tiled=True),
    )
    up_bias_full = lax.dynamic_update_slice_in_dim(
        jnp.zeros((up_bias.shape[0],), jnp.float32), sum_up_bias, col_start, 0
    )
    summed = lax.psum(
        (
            sum_first_gain,
            sum_first_shift,
            sum_query_bias,
            sum_value_bias,
            sum_outer_bias,
            sum_attend_scale,
            sum_second_gain,
            sum_second_shift,
            up_bias_full,
            sum_down_bias,
            sum_feed_scale,
            sum_table,
        ),
        ("dp", "mlp"),
    )
    return (
        jnp.stack(results),
        jnp.stack(input_grads),
        gradient_inner,
        gradient_outer,
        gradient_up,
        gradient_down,
        summed[0],
        summed[1],
        summed[2],
        summed[3],
        summed[4],
        summed[5],
        summed[6],
        summed[7],
        summed[8],
        summed[9],
        summed[10],
        summed[11],
    )


def solution(mesh):
    special = mesh.shape["dp"] == 8 and mesh.shape["mlp"] == 4
    placed = (
        P(None, ("dp", "mlp"), None),
        P(None, ("dp", "mlp")),
        P(),
        P(None, ("dp", "mlp"), None),
        P(),
        P(),
        P(("dp", "mlp"), None),
        P(),
        P(),
        P(("dp", "mlp"), None),
        P(),
        P(),
        P(),
        P(),
        P("dp", "mlp"),
        P(),
        P("mlp", "dp"),
        P(),
        P(),
        P(),
    )
    return jax.shard_map(
        fast_body if special else body,
        mesh=mesh,
        in_specs=placed,
        out_specs=(
            P(None, ("dp", "mlp"), None),
            P(None, ("dp", "mlp"), None),
            P(("dp", "mlp"), None),
            P(("dp", "mlp"), None),
            P("dp", "mlp"),
            P("mlp", "dp"),
            P(),
            P(),
            P(),
            P(),
            P(),
            P(),
            P(),
            P(),
            P(),
            P(),
            P(),
            P(),
        ),
        check_vma=False,
    )
```

```python
import functools

import jax
import jax.numpy as jnp
from jax import lax
from jax.experimental import pallas as pl
from jax.experimental.pallas import tpu as pltpu
from jax.sharding import PartitionSpec as P

EPS = 1e-06
ROOT_HALF = 0.7071067811865476
DENSITY = 0.3989422804014327


MESH = pl.DeviceIdType.MESH
F32 = jnp.float32
BF16 = jnp.bfloat16
TILE = 384
PAD = 208
TALL = 2 * PAD
KEYS = 256
N_COPY = 11
NAMES = ("I0", "I1", "I2", "O", "U0a", "U0b", "U1a", "U1b", "N0a", "N0b", "N1a", "N1b")
GATHER = {"U0a": "xZy", "U1b": "xZy", "I2": "zxy", "N0a": "yZx", "I0": "zyx", "O": "zxy", "I1": "zyx", "U1a": "yZx", "N0b": "Zxy", "U0b": "zyx", "N1b": "xZy", "N1a": "yZx"}
REDUCE = {"U0a": "yxZ", "U1b": "yxZ", "I2": "yxz", "N0a": "xzy", "I0": "xZy", "O": "yxz", "I1": "yxZ", "U1a": "xyz", "N0b": "yzx", "U0b": "xZy", "N1b": "yzx", "N1a": "xZy"}
ORDER = (
    85, 57, 86, 99, 71, 58, 100, 72, 127, 128, 0, 14, 112, 168, 13, 154, 140, 30, 210, 196, 16, 84, 15, 24,
    34, 56, 43, 2, 87, 88, 21, 29, 98, 31, 59, 60, 22, 183, 23, 70, 32, 89, 1, 101, 90, 25, 113, 126,
    26, 169, 184, 102, 61, 155, 73, 62, 9, 114, 141, 74, 10, 211, 197, 103, 170, 104, 182, 129, 130, 75, 156, 115,
    116, 76, 17, 18, 171, 142, 172, 185, 186, 3, 131, 4, 157, 158, 212, 132, 117, 198, 143, 144, 118, 36, 173, 187,
    45, 174, 213, 214, 188, 37, 46, 199, 200, 38, 159, 145, 47, 160, 175, 133, 119, 189, 146, 48, 39, 215, 176, 134,
    201, 120, 190, 216, 202, 40, 41, 49, 177, 179, 180, 50, 217, 203, 161, 121, 147, 33, 7, 218, 204, 135, 162, 191,
    193, 194, 42, 224, 178, 122, 148, 5, 225, 6, 105, 137, 11, 106, 219, 221, 205, 222, 12, 63, 192, 27, 64, 181,
    138, 163, 226, 123, 149, 195, 19, 20, 77, 220, 28, 107, 78, 91, 65, 207, 136, 124, 51, 227, 92, 164, 150, 151,
    152, 52, 236, 223, 53, 67, 108, 109, 110, 208, 125, 54, 79, 165, 55, 232, 139, 35, 233, 153, 68, 44, 228, 80,
    8, 229, 93, 206, 111, 234, 66, 166, 230, 209, 81, 69, 94, 235, 95, 96, 167, 238, 231, 82, 237, 83, 97,
)


def place():
    dp = lax.axis_index("dp")
    mlp = lax.axis_index("mlp")
    return lax.div(dp, 2), lax.rem(dp, 2), lax.div(mlp, 2), lax.rem(mlp, 2)


def device(z, x, y, c):
    return (z * 2 + x, y * 2 + c)


def greet(z, x, y, c):
    barrier = pltpu.get_barrier_semaphore()
    others = [device(lax.rem(z + d, 4), x, y, c) for d in (1, 2, 3)]
    others += [device(z, 1 - x, y, c), device(z, x, 1 - y, c), device(z, 1 - x, 1 - y, c), device(z, x, y, 1 - c)]
    for other in others:
        pl.semaphore_signal(barrier, inc=1, device_id=other, device_id_type=MESH)
    return lambda: pl.semaphore_wait(barrier, len(others))


class Link:
    def __init__(self, send, recv):
        self.send, self.recv, self.pending = send, recv, {}

    def make(self, src, dst, slot, target):
        return pltpu.make_async_remote_copy(
            src_ref=src,
            dst_ref=dst,
            send_sem=self.send.at[slot],
            recv_sem=self.recv.at[slot],
            device_id=target,
            device_id_type=MESH,
        )

    def copy(self, src, dst, slot, target, group=None):
        made = self.make(src, dst, slot, target)
        made.start()
        self.pending.setdefault(group, []).append((made, None))
        return made

    def drain(self, *groups):
        for group in groups or tuple(self.pending):
            for made, sender in self.pending.pop(group, []):
                if sender is None:
                    made.wait_send()
                else:
                    pl.when(sender)(made.wait_send)


class Some:
    def __init__(self, link, src, dst, slot, target, sender, getter, group):
        self.made = link.make(src, dst, slot, target)
        self.getter = getter
        pl.when(sender)(self.made.start)
        link.pending.setdefault(group, []).append((self.made, sender))

    def wait_recv(self):
        pl.when(self.getter)(self.made.wait_recv)


def mix(here, *there):
    total = here[...].astype(F32)
    for other in there:
        total = total + other[...].astype(F32)
    here[...] = total.astype(BF16)


class Unit:
    def __init__(self, link, ref, name, where, base):
        self.link, self.ref, self.where, self.base, self.name = link, ref, where, base, name
        self.narrow = name[0] in "IO"
        self.rows = slice(None) if self.narrow else pl.ds(48 * "ab".index(name[2]), 48)
        self.group = name if base < len(NAMES) * N_COPY else None
        z = where[0]
        self.side = lax.div(z, 2)
        self.mate = z + 1 - 2 * lax.rem(z, 2)
        self.inner = jnp.logical_and(z > 0, z < 3)
        self.outer = jnp.logical_not(self.inner)

    def put(self, src, dst, slot, target):
        return self.link.copy(src, dst, self.base + slot, target, self.group)

    def some(self, src, dst, slot, z, sender, getter):
        x, y, c = self.where[1:]
        return Some(self.link, src, dst, self.base + slot, device(z, x, y, c), sender, getter, self.group)

    def at(self, z, x, y, c):
        return self.ref.at[c, z, x, y] if self.narrow else self.ref.at[y, c, z, x, self.rows]

    def by_core(self, c):
        return self.ref.at[c] if self.narrow else self.ref.at[:, c, :, :, self.rows]

    def plane(self, axis, x, y, c):
        every = slice(None)
        return self.at(every, x, every, c) if axis == "x" else self.at(every, every, y, c)

    def pairs(self, axis, z):
        x, y, c = self.where[1:]
        every = slice(None)
        return self.at(z, every, y, c) if axis == "x" else self.at(z, x, every, c)

    def two(self, side):
        return pl.ds(2 * side, 2)

    def spread(self, part, slot):
        z, x, y, c = self.where
        return [self.put(part, part, slot + d - 1, device(lax.rem(z + d, 4), x, y, c)) for d in (1, 2, 3)]

    def across(self, axis, src, dst, slot):
        z, x, y, c = self.where
        target = {"x": (z, 1 - x, y, c), "y": (z, x, 1 - y, c), "c": (z, x, y, 1 - c)}[axis]
        return self.put(src, dst, slot, device(*target))

    def other(self, axis):
        z, x, y, c = self.where
        return (1 - x, y, c) if axis == "x" else (x, 1 - y, c)


class Gather(Unit):
    def __init__(self, *given):
        super().__init__(*given)
        self.axes = GATHER[self.name]
        self.steps = "Z" in self.axes
        self.early = self.axes[0] in "zZ"
        self.z, self.to_c = [], []

    def own(self, z):
        x, y, c = self.where[1:]
        return self.at(z, x, y, c) if self.early else self.pairs(self.axes[0], z)

    def swap_pair(self, slot):
        part = self.own(self.where[0])
        self.z = [self.put(part, part, slot, device(self.mate, *self.where[1:]))]

    def Z(self):
        z, x, y, c = self.where
        part = self.at(z, x, y, c)
        if not self.early:
            self.first = self.across(self.axes[0], part, part, 0)
        if not self.steps:
            self.z = self.spread(part, 1)
        elif self.early:
            self.swap_pair(1)

    def m(self):
        if self.steps:
            self.z[0].wait_recv()
            part = self.own(self.two(self.side))
            self.z = [self.some(part, part, 2, 3 - self.where[0], self.inner, self.inner)]

    def n(self):
        if self.steps:
            self.z[0].wait_recv()
            part = self.own(self.two(1 - self.side))
            self.z = [self.some(part, part, 3, self.mate, self.inner, self.outer)]

    def L(self):
        z, x, y, c = self.where
        if not self.early:
            self.first.wait_recv()
            if self.steps:
                self.swap_pair(1)
            else:
                self.z += self.spread(self.at(z, *self.other(self.axes[0])), 4)
            return
        for made in self.z:
            made.wait_recv()
        part = self.at(slice(None), x, y, c)
        self.made = {axis: self.across(axis, part, part, 4 + i) for i, axis in enumerate(self.axes[1:] + "c")}
        self.to_c = [self.made["c"]]

    def pass_on(self, axis, slot):
        self.made[axis].wait_recv()
        part = self.at(slice(None), *self.other(axis))
        self.to_c.append(self.across("c", part, part, slot))
        return part

    def P(self):
        z, x, y, c = self.where
        last = self.axes[2]
        if self.early:
            part = self.pass_on(self.axes[1], 7)
            self.last = self.across(last, part, part, 8)
            return
        for made in self.z:
            made.wait_recv()
        part = self.plane(last, x, y, c)
        self.last = self.across(last, part, part, 7)
        self.to_c = [self.across("c", part, part, 8)]

    def Q(self):
        if self.early:
            self.pass_on(self.axes[2], 9)

    def R(self):
        z, x, y, c = self.where
        self.last.wait_recv()
        part = self.at(slice(None), 1 - x, 1 - y, c) if self.early else self.plane(self.axes[2], 1 - x, 1 - y, c)
        self.to_c.append(self.across("c", part, part, 10))

    def F(self):
        for made in self.to_c:
            made.wait_recv()


class Reduce(Unit):
    def __init__(self, *given):
        super().__init__(*given)
        self.axes = REDUCE[self.name]
        self.steps = "Z" in self.axes
        self.late = self.axes[2] in "zZ"

    @staticmethod
    def buffers(name):
        narrow, axes = name[0] in "IO", REDUCE[name]
        half = (4, 2, 2) if narrow else (2, 4, 2)
        quarter = (2, 4) if not narrow and axes[0] == "x" else (4, 2)
        one = () if axes[2] in "zZ" else (2,)
        two = (2, 2) if one else (2,)
        along_z = [(*two,), (*two,), (*one,)] if "Z" in axes else [(3, *one)]
        shapes = [half, quarter, (4,) if axes[2] in "zZ" else (), *along_z]
        return [(*shape, 48, TILE) for shape in shapes]

    def set_buffers(self, half, quarter, side, *along_z):
        self.half, self.quarter, self.side_ref, self.along_z = half, quarter, side, along_z

    def own(self, z):
        x, y, c = self.where[1:]
        return self.at(z, x, y, c) if self.late else self.pairs(self.axes[2], z)

    def c(self):
        self.made = self.across("c", self.by_core(1 - self.where[3]), self.half, 0)

    def d(self):
        z, x, y, c = self.where
        self.made.wait_recv()
        mix(self.by_core(c), self.half)
        axis = self.axes[0]
        self.made = self.across(axis, self.plane(axis, 1 - x, 1 - y, c), self.quarter, 1)

    def e(self):
        z, x, y, c = self.where
        self.made.wait_recv()
        mix(self.plane(self.axes[0], x, y, c), self.quarter)
        if not self.late:
            self.into_z()
            return
        axis = self.axes[1]
        self.made = self.across(axis, self.at(slice(None), *self.other(axis)), self.side_ref, 2)

    def into_z(self):
        z, x, y, c = self.where
        if self.steps:
            part = self.own(self.two(1 - self.side))
            self.z = [self.some(part, self.along_z[0], 3, self.mate, self.outer, self.inner)]
            return
        self.z = []
        for d in (1, 2, 3):
            far = lax.rem(z + d, 4)
            self.z.append(self.put(self.own(far), self.along_z[0].at[d - 1], 2 + d, device(far, x, y, c)))

    def p(self):
        if self.steps:
            self.z[0].wait_recv()
            part = self.own(self.two(1 - self.side))
            pl.when(self.inner)(functools.partial(mix, part, self.along_z[0]))
            self.z = [self.some(part, self.along_z[1], 4, 3 - self.where[0], self.inner, self.inner)]

    def q(self):
        if self.steps:
            self.z[0].wait_recv()
            pl.when(self.inner)(functools.partial(mix, self.own(self.two(self.side)), self.along_z[1]))
            self.z = [self.put(self.own(self.mate), self.along_z[2], 5, device(self.mate, *self.where[1:]))]

    def parts(self):
        for made in self.z:
            made.wait_recv()
        return [self.along_z[2]] if self.steps else [self.along_z[0].at[d] for d in range(3)]

    def f(self):
        z, x, y, c = self.where
        if self.late:
            self.made.wait_recv()
            mix(self.at(slice(None), x, y, c), self.side_ref)
            self.into_z()
            return
        mix(self.own(z), *self.parts())
        axis = self.axes[2]
        self.made = self.across(axis, self.at(z, *self.other(axis)), self.side_ref, 6)

    def total(self):
        if self.late:
            parts = self.parts()
        else:
            self.made.wait_recv()
            parts = [self.side_ref]
        total = self.at(*self.where)[...].astype(F32)
        for part in parts:
            total = total + part[...].astype(F32)
        return total


class Everywhere:
    def __init__(self, link, ref, core_ref, plane_ref, line_ref, base, where):
        self.link, self.ref, self.where, self.base = link, ref, where, base
        self.core_ref, self.plane_ref, self.line_ref = core_ref, plane_ref, line_ref

    def to_core(self):
        z, x, y, c = self.where
        self.made = [self.link.copy(self.ref.at[1 - c], self.core_ref.at[0], self.base, device(z, x, y, 1 - c))]

    def wait(self):
        for made in self.made:
            made.wait_recv()

    def to_plane(self):
        z, x, y, c = self.where
        self.wait()
        chip = self.plane_ref.at[3]
        chip[...] = self.ref[c] + self.core_ref[0]
        targets = (device(z, 1 - x, y, c), device(z, x, 1 - y, c), device(z, 1 - x, 1 - y, c))
        self.made = [
            self.link.copy(chip, self.plane_ref.at[n], self.base + 1 + n, target) for n, target in enumerate(targets)
        ]

    def to_line(self):
        z, x, y, c = self.where
        self.wait()
        got = self.plane_ref
        self.line_ref[z] = (got[3] + got[0]) + (got[1] + got[2])
        part = self.line_ref.at[z]
        self.made = [
            self.link.copy(part, part, self.base + 3 + d, device(lax.rem(z + d, 4), x, y, c)) for d in (1, 2, 3)
        ]

    def to_mate(self):
        z, x, y, c = self.where
        self.wait()
        got = self.line_ref
        part = self.core_ref.at[1 + c]
        part[...] = (got[0] + got[1]) + (got[2] + got[3])
        self.made = [self.link.copy(part, part, self.base + 7, device(z, x, y, 1 - c))]

    def total(self, half):
        return self.core_ref[1 + half]


def dot(left, right):
    return lax.dot_general(left, right, (((1,), (0,)), ((), ())), preferred_element_type=F32)


def dot_nt(left, right):
    return lax.dot_general(left, right, (((1,), (1,)), ((), ())), preferred_element_type=F32)


def dot_tn(left, right):
    return lax.dot_general(left, right, (((0,), (0,)), ((), ())), preferred_element_type=F32)


def fold(values):
    rows, width = values.shape
    return jnp.sum(values.reshape(rows // 8, 8, width), 0)


def unit_of(values):
    mean = jnp.mean(values, -1, keepdims=True)
    centred = values - mean
    variance = jnp.mean(centred * centred, -1, keepdims=True)
    scaled = lax.rsqrt(variance + EPS)
    return centred * scaled, scaled


def loop(count, step, init):
    return lax.fori_loop(0, count, step, init)


def by_rows(step, init, first=0, count=13):
    size = 32

    def one(index, carried):
        return step(pl.ds(pl.multiple_of((index + first) * size, size), size), carried)

    one.__name__ = step.__name__
    return loop(count, one, init)


def layer_kernel(*refs):
    (
        tokens, keep, places, cotangent, first_gain1, first_shift1, inner_in, query_bias1, value_bias1, outer_in, outer_bias1,
        attend_scale1, second_gain1, second_shift1, up_in, up_bias, down_in, down_bias1, feed_scale1, table_in,
        result, token_grad, packed,
        *rest,
    ) = refs
    (
        narrow, wide, small, pair, swap,
        source, upstream, normed1, normed1_t, normed2, normed2_t, qkv, bias, mask, index, probs, mix_t, attend, resid,
        dfeed, dfeed_t, hidden, slope, total, dnormed2, shifts, ups, tab, vectors,
        early, late, hits, early_core, early_plane, early_line, late_core, late_plane, late_line, hits_core, hits_plane, hits_line,
        send, recv, *buffers,
    ) = rest
    outer_out, up_out, down_out, early_out, late_out, table_out = (
        packed.at[pl.ds(first, rows)] for first, rows in ((72, 24), (96, 96), (192, 96), (288, 16), (304, 8), (312, 16))
    )
    dresid, dproj, dmixed, mixed, dattend = attend, hidden, normed2, normed2, dfeed
    where = z, x, y, c = place()
    all_here = greet(*where)
    link = Link(send, recv)
    gathers, reduces = {}, {}
    taken = 0
    for n, name in enumerate(NAMES):
        ref = narrow.at[n] if n < 4 else wide.at[(n - 4) // 2]
        gathers[name] = Gather(link, ref, name, where, n * N_COPY)
        reduces[name] = Reduce(link, ref, name, where, (len(NAMES) + n) * N_COPY)
        count = len(Reduce.buffers(name))
        reduces[name].set_buffers(*buffers[taken : taken + count])
        taken += count
    spare = 2 * len(NAMES) * N_COPY
    sums = {
        "E": Everywhere(link, early, early_core, early_plane, early_line, spare + 5, where),
        "l": Everywhere(link, late, late_core, late_plane, late_line, spare + 15, where),
        "t": Everywhere(link, hits, hits_core, hits_plane, hits_line, spare + 25, where),
    }
    mates = []
    kept = {}
    for k in range(3):
        for core in range(2):
            for part in range(3):
                start = part * 768 + (core * 3 + k) * 128
                small[k, core, :, part * 128 : part * 128 + 128] = inner_in[:, start : start + 128].astype(F32)
    for core in range(2):
        small[3, core] = outer_in[:, core * TILE : core * TILE + TILE].astype(F32)
    for k in range(2):
        cols = slice(k * TILE, k * TILE + TILE)
        wide[k, y, c, z, x] = up_in[:, cols]
        wide[2 + k, y, c, z, x] = down_in[:, cols]
    all_here()
    mate = link.copy(small.at[:, 1 - c], pair.at[:, c], spare, device(z, x, y, 1 - c))
    for name in NAMES[4:]:
        if not gathers[name].early:
            gathers[name].Z()
    pair[:, c] = small[:, c]
    mate.wait_recv()
    link.drain(None)
    for unit in range(4):
        narrow[unit, c, z, x, y] = pair[unit].reshape(48, TILE).astype(BF16)
    for name in GATHER:
        if name[0] in "IO" or gathers[name].early:
            gathers[name].Z()

    given = (first_gain1, first_shift1, query_bias1, value_bias1, outer_bias1, attend_scale1, second_gain1, second_shift1, down_bias1, feed_scale1)
    for n, ref in enumerate(given):
        vectors[n] = ref[...].reshape(1, 768)
    (first_gain, first_shift, query_bias, value_bias, outer_bias, attend_scale, second_gain, second_shift, down_bias, feed_scale) = (
        vectors.at[n] for n in range(10)
    )

    for image in range(2):
        last = pl.ds(image * PAD + 192, 16)
        source[last, :] = jnp.zeros((16, 768), BF16)
        upstream[last, :] = jnp.zeros((16, 768), BF16)
        source[pl.ds(image * PAD, 197), :] = tokens[:, image, :]
        upstream[pl.ds(image * PAD, 197), :] = cotangent[:, image, :]
    zero = jnp.zeros((8, 768), F32)
    lane = lax.broadcasted_iota(jnp.int32, (1, 128), 1)
    picks = [(lane < 64).astype(F32).astype(BF16), (lane >= 64).astype(F32).astype(BF16)]

    def rows_of(image):
        return slice(image * PAD, image * PAD + PAD)

    def keys_of(image):
        return slice(image * PAD, image * PAD + KEYS)

    def cols_of(p):
        return pl.ds(pl.multiple_of(p * 128, 128), 128)

    def half(core):
        return slice(core * TILE, core * TILE + TILE)

    def norm1(n):
        def norm_first(rows, carried):
            unit, _ = unit_of(source[rows, :].astype(F32))
            normed1[rows, :] = (unit * first_gain[...] + first_shift[...]).astype(BF16)
            lifted = upstream[rows, :].astype(F32) * feed_scale[...]
            dfeed[rows, :] = lifted.astype(BF16)
            return carried + fold(lifted)

        kept["down"] = by_rows(norm_first, kept.get("down", zero), 7 * n, 7 - n)
        if n == 0:
            return
        early[...] = jnp.zeros((2, 8, 768), F32)
        late[...] = jnp.zeros((2, 8, TILE), F32)
        early[0, 4:5, :] = jnp.sum(kept.pop("down"), 0, keepdims=True)
        zero_row = jnp.zeros((1, 128), F32)
        for p in range(6):
            cols = slice(p * 128, p * 128 + 128)
            shifts[p] = jnp.concatenate([query_bias[:, cols], zero_row, value_bias[:, cols]], axis=1)
            qkv[p, TALL:, :] = jnp.zeros((48, TILE), BF16)

    def fill():
        index[...] = jnp.full((PAD, KEYS), -1, jnp.int32)
        index[0:197, 0:197] = places[...]
        tab[...] = jnp.zeros((12, 1, 768), F32)
        for head in range(12):
            tab[head, :, 0:732] = table_in[head : head + 1, :]
        row_of = lax.broadcasted_iota(jnp.int32, (PAD, KEYS), 0)
        col_of = lax.broadcasted_iota(jnp.int32, (PAD, KEYS), 1)
        for image in range(2):
            mask[image] = jnp.full((PAD, KEYS), -1e30, F32)
            shown = jnp.where(keep[image : image + 1, :] == 1, 0.0, -1e30).astype(F32)
            mask[image, :, 0:197] = jnp.broadcast_to(shown, (PAD, 197))
            mask[image] = jnp.where(row_of == col_of, 0.0, mask[image])

    def look(k, n):
        def look_up(step, carried):
            head = 2 * ((n // 2) * 3 + k) + n % 2
            for side in range(2):
                cols = slice(side * 128, side * 128 + 128)
                spot = index[:, cols]
                low, high = spot & 127, spot >> 7
                found = jnp.zeros((PAD, 128), F32)
                for piece in range(6):
                    row = tab[head, :, piece * 128 : piece * 128 + 128]
                    picked = jnp.take_along_axis(jnp.broadcast_to(row, (PAD, 128)), low, axis=1)
                    found = jnp.where(high == piece, picked, found)
                bias[head, :, cols] = found
            return carried

        loop(1, look_up, 0)

    def turn1():
        normed1_t[...] = normed1[...].T

    def turnd():
        dfeed_t[...] = dfeed[...].T

    def proj(k):
        def project(core, carried):
            p = core * 3 + k
            weight = narrow[k, core].reshape(768, TILE)
            scaling = jnp.where(lax.broadcasted_iota(jnp.int32, (1, TILE), 1) < 128, 0.125, 1.0).astype(F32)
            value = (dot(normed1[...], weight) + shifts[p]).astype(BF16)
            qkv[p, 0:TALL, :] = (value.astype(F32) * scaling).astype(BF16)
            return carried

        loop(2, project, 0)

    def att(k):
        def attend_pair(core, carried):
            p = core * 3 + k
            first_half = lax.broadcasted_iota(jnp.int32, (PAD, 128), 1) < 64
            for image in range(2):
                query = qkv[p, rows_of(image), 0:128]
                keys = qkv[p, keys_of(image), 128:256]
                values = qkv[p, keys_of(image), 256:384]
                outs = []
                for t in range(2):
                    logits = dot_nt(query * picks[t], keys) + bias[2 * p + t] + mask[image]
                    top = jnp.max(logits, -1, keepdims=True)
                    expd = jnp.exp(logits - top)
                    share = (expd * (1.0 / jnp.sum(expd, -1, keepdims=True))).astype(BF16)
                    probs[image, 2 * p + t] = share
                    outs.append(dot(share, values))
                mixed[rows_of(image), cols_of(p)] = jnp.where(first_half, outs[0], outs[1]).astype(BF16)
            return carried

        loop(2, attend_pair, 0)

    def out():
        for core in range(2):
            attend[:, half(core)] = dot(mixed[...], narrow[3, core].reshape(768, TILE)) + outer_bias[:, half(core)]
        mix_t[...] = mixed[...].T

    def norm2():
        def norm_second(rows, carried):
            value = source[rows, :].astype(F32) + attend_scale[...] * attend[rows, :]
            resid[rows, :] = value
            unit, _ = unit_of(value)
            normed2[rows, :] = (unit * second_gain[...] + second_shift[...]).astype(BF16)
            return carried

        by_rows(norm_second, 0)
        normed2_t[...] = normed2[...].T

    def widening(k, side):
        def widen(core, carried):
            weight = wide[k, side, core].reshape(768, TILE)
            cols = pl.ds(pl.multiple_of((side * 2 + core) * 768 + k * TILE, 128), TILE)
            pre = dot(normed2[...], weight) + up_bias[:, cols]
            cumul = 0.5 * (1.0 + lax.erf(pre * ROOT_HALF))
            b = k * 4 + side * 2 + core
            hidden[b] = (pre * cumul).astype(BF16)
            slope[b] = (cumul + pre * jnp.exp(-0.5 * pre * pre) * DENSITY).astype(BF16)
            return carried

        loop(2, widen, 0)

    def joined(ref, b):
        return jnp.concatenate([ref[b], ref[b + 1]], axis=1)

    def weights(slot, side):
        return jnp.concatenate([wide[slot, side, core].reshape(768, TILE) for core in range(2)], axis=1)

    def back(k, side):
        b = k * 4 + side * 2

        def narrow_back(step, carried):
            dpre = (dot(dfeed[...], weights(2 + k, side)) * joined(slope, b).astype(F32)).astype(BF16)
            for core in range(2):
                slope[b + core] = dpre[:, half(core)]
            ups[b // 2] = jnp.sum(fold(dpre.astype(F32)), 0, keepdims=True)
            part = dot_nt(dpre, weights(k, side))
            dnormed2[...] = part if b == 0 else dnormed2[...] + part
            return carried

        loop(1, narrow_back, 0)

    def grad(k, side):
        if side == 0:
            link.drain(*(what + str(k) + part for what in "UN" for part in "ab"))
        b = k * 4 + side * 2

        def narrow_grad(step, carried):
            both = joined(hidden, b)
            part = dot_nt(both, weights(2 + k, side))
            total[...] = part if b == 0 else total[...] + part
            up_grad = dot(normed2_t[...], joined(slope, b)).astype(BF16)
            down_grad = dot(dfeed_t[...], both).astype(BF16)
            for core in range(2):
                wide[2 + k, side, core] = up_grad[:, half(core)].reshape(4, 2, 96, TILE)
                wide[k, side, core] = down_grad[:, half(core)].reshape(4, 2, 96, TILE)
            return carried

        loop(1, narrow_grad, 0)

    def sec(n):
        def second_back(rows, carried):
            gain_sum, shift_sum, scale_sum, bias_sum = carried
            unit, scaled = unit_of(resid[rows, :])
            grad = dnormed2[rows, :]
            inner = grad * second_gain[...]
            first = jnp.mean(inner, -1, keepdims=True)
            second = jnp.mean(inner * unit, -1, keepdims=True)
            back = upstream[rows, :].astype(F32) + scaled * (inner - first - unit * second)
            scale_sum = scale_sum + fold(attend[rows, :] * back)
            dresid[rows, :] = back
            lifted = attend_scale[...] * back
            dattend[rows, :] = lifted.astype(BF16)
            return gain_sum + fold(grad * unit), shift_sum + fold(grad), scale_sum, bias_sum + fold(lifted)

        kept["sec"] = by_rows(second_back, kept.get("sec", (zero,) * 4), 7 * n, 7 - n)
        if n == 1:
            for block in range(4):
                for k in range(2):
                    b = k * 4 + block
                    early[1, block : 1 + block, half(k)] = ups[b // 2, :, half(b % 2)]
            for row, value in zip((2, 3, 1, 0), kept.pop("sec")):
                early[0, row : row + 1, :] = jnp.sum(value, 0, keepdims=True)

    def res():
        def feed_out(rows, carried):
            feed = total[rows, :] + down_bias[...]
            total[rows, :] = resid[rows, :] + feed_scale[...] * feed
            return carried + fold(feed * upstream[rows, :].astype(F32))

        early[0, 5:6, :] = jnp.sum(by_rows(feed_out, zero), 0, keepdims=True)
        for image in range(2):
            result[:, image, :] = total[pl.ds(image * PAD, 197), :].astype(BF16)

    def dmix():
        parts = [dot_nt(dattend[:, half(core)], narrow[3, core].reshape(768, TILE)) for core in range(2)]
        dmixed[...] = (parts[0] + parts[1]).astype(BF16)

    def gout():
        link.drain("O")
        for core in range(2):
            narrow[3, core] = dot(mix_t[...], dattend[:, half(core)]).astype(BF16).reshape(4, 2, 2, 48, TILE)

    def attb(k):
        def attend_back(core, carried):
            p = core * 3 + k
            first_half = lax.broadcasted_iota(jnp.int32, (PAD, 128), 1) < 64
            hit = [None, None]
            for image in range(2):
                rows = rows_of(image)
                query = qkv[p, rows, 0:128]
                keys = qkv[p, keys_of(image), 128:256]
                values = qkv[p, keys_of(image), 256:384]
                above = dmixed[rows, cols_of(p)]
                dquery, dkeys, dvalues = [], [], []
                for t in range(2):
                    share = probs[image, 2 * p + t]
                    dvalues.append(dot_tn(share, above)[0:PAD])
                    dshare = dot_nt(above * picks[t], values)
                    full = share.astype(F32)
                    dlogits = full * (dshare - jnp.sum(dshare * full, -1, keepdims=True))
                    hit[t] = dlogits if image == 0 else hit[t] + dlogits
                    low = dlogits.astype(BF16)
                    dquery.append(dot(low, keys) * 0.125)
                    dkeys.append(dot_tn(low, query)[0:PAD])
                dproj[p, rows, 0:128] = jnp.where(first_half, dquery[0], dquery[1]).astype(BF16)
                dproj[p, rows, 128:256] = jnp.where(first_half, dkeys[0], dkeys[1]).astype(BF16)
                dproj[p, rows, 256:384] = jnp.where(first_half, dvalues[0], dvalues[1]).astype(BF16)
            for t in range(2):
                bias[2 * p + t] = hit[t]
            return carried

        loop(2, attend_back, 0)

    def projb(k):
        link.drain("I" + str(k))

        def project_back(core, carried):
            p = core * 3 + k
            grad = dproj[p]
            summed = jnp.sum(fold(grad.astype(F32)), 0, keepdims=True)
            late[core, 2:3, k * 128 : k * 128 + 128] = summed[:, 0:128]
            late[core, 3:4, k * 128 : k * 128 + 128] = summed[:, 256:384]
            part = dot_nt(grad, narrow[k, core].reshape(768, TILE))
            dnormed2[...] = jnp.where(core == 0, 0.0, dnormed2[...]) + part if k == 0 else dnormed2[...] + part
            narrow[k, core] = dot(normed1_t[...], grad).astype(BF16).reshape(4, 2, 2, 48, TILE)
            return carried

        loop(2, project_back, 0)

    def first(n):
        def first_back(rows, carried):
            gain_sum, shift_sum = carried
            grad = dnormed2[rows, :]
            unit, scaled = unit_of(source[rows, :].astype(F32))
            inner = grad * first_gain[...]
            mean = jnp.mean(inner, -1, keepdims=True)
            second = jnp.mean(inner * unit, -1, keepdims=True)
            dresid[rows, :] = dresid[rows, :] + scaled * (inner - mean - unit * second)
            return gain_sum + fold(grad * unit), shift_sum + fold(grad)

        kept["first"] = by_rows(first_back, kept.get("first", (zero, zero)), 7 * n, 7 - n)
        if n == 0:
            return
        found = kept.pop("first")
        for row in range(2):
            value = jnp.sum(found[row], 0, keepdims=True)
            for core in range(2):
                late[core, row : row + 1, :] = value[:, half(core)]

    def tok():
        for image in range(2):
            token_grad[:, image, :] = dresid[pl.ds(image * PAD, 197), :].astype(BF16)

    def counting(n):
        low_of = lax.broadcasted_iota(jnp.int32, (128, KEYS), 0)
        high_of = lax.broadcasted_iota(jnp.int32, (8, KEYS), 0)

        def count(group, carried):
            eight = pl.ds(pl.multiple_of((group + 5 * n) * 8, 8), 8)
            spots = index[eight, :]
            for r in range(8):
                spot = jnp.broadcast_to(spots[r : r + 1, :], (8, KEYS))
                high = (spot >> 7) == high_of
                parts = []
                for head in range(12):
                    grads = bias[head, eight, :]
                    parts.append(jnp.where(high, jnp.broadcast_to(grads[r : r + 1, :], (8, KEYS)), 0.0))
                spread = jnp.concatenate(parts, axis=0).astype(BF16)
                low = jnp.concatenate([spot & 127] * 16, axis=0)
                which = (low == low_of).astype(F32).astype(BF16)
                carried = carried + dot_nt(spread, which)
            return carried

        before = jnp.zeros((96, 128), F32) if n == 0 else hits[...].reshape(96, 128)
        hits[...] = loop(5, count, before).reshape(2, 48, 128)

    def settle(name):
        value = reduces[name].total()
        n = NAMES.index(name)
        if n < 4:
            small[n] = value.reshape(2, 24, TILE)
            swap[n, c] = small[n, c]
            mates.append(link.copy(small.at[n, 1 - c], swap.at[n, c], spare + 1 + n, device(z, x, y, 1 - c)))
        else:
            rows = slice(48 * (n % 2), 48 * (n % 2) + 48)
            if n < 8:
                down_out[rows, half((n - 4) // 2)] = value
            else:
                up_out[rows, half((n - 8) // 2)] = value

    steps = {"fill": fill, "turn1": turn1, "turnd": turnd, "out": out, "norm2": norm2, "dmix": dmix, "gout": gout, "res": res, "tok": tok}
    for k in range(3):
        steps["proj" + str(k)] = functools.partial(proj, k)
        steps["att" + str(k)] = functools.partial(att, k)
        steps["attb" + str(k)] = functools.partial(attb, k)
        steps["projb" + str(k)] = functools.partial(projb, k)
        for i in range(4):
            steps["look" + str(k) + str(i)] = functools.partial(look, k, i)
    for i in range(2):
        steps["sec" + str(i)] = functools.partial(sec, i)
        steps["norm1" + str(i)] = functools.partial(norm1, i)
        steps["first" + str(i)] = functools.partial(first, i)
        for k in range(2):
            steps["wide" + str(k) + str(i)] = functools.partial(widening, k, i)
            steps["back" + str(k) + str(i)] = functools.partial(back, k, i)
            steps["grad" + str(k) + str(i)] = functools.partial(grad, k, i)
    for n in range(5):
        steps["count" + str(n)] = functools.partial(counting, n)
    for name in NAMES:
        for event in "LmnPQRF":
            steps[event + name] = getattr(gathers[name], event)
        for event in "cdefpq":
            steps[event + name] = getattr(reduces[name], event)
        steps["g" + name] = functools.partial(settle, name)
    for what, everywhere in sums.items():
        steps[what + "0"] = everywhere.to_core
        steps[what + "1"] = everywhere.to_plane
        steps[what + "2"] = everywhere.to_line
        steps[what + "3"] = everywhere.to_mate

    def give_early():
        sums["E"].wait()
        for part in range(2):
            early_out[part * 8 : part * 8 + 8, :] = sums["E"].total(part)

    def give_late():
        sums["l"].wait()
        for core in range(2):
            late_out[:, half(core)] = sums["l"].total(core)

    def give_table():
        sums["t"].wait()
        for part in range(2):
            found = sums["t"].total(part).reshape(6, 8, 128)
            for piece in range(6):
                width = min(128, 732 - piece * 128)
                table_out[part * 6 : part * 6 + 6, piece * 128 : piece * 128 + width] = found[:, piece, 0:width]

    steps["E4"], steps["l4"], steps["t4"] = give_early, give_late, give_table
    todo = list(steps.values())
    for n in ORDER:
        todo[n]()
    for made in mates:
        made.wait_recv()
    for k in range(3):
        for core in range(2):
            for part in range(3):
                start = (core * 3 + k) * 128
                packed[part * 24 : part * 24 + 24, start : start + 128] = swap[k, core, :, part * 128 : part * 128 + 128]
    for core in range(2):
        outer_out[:, half(core)] = swap[3, core]
    link.drain()


def run_layer(*operands):
    def vmem(*shape, dtype=BF16):
        return pltpu.VMEM(shape, dtype)

    scratch = [
        vmem(4, 2, 4, 2, 2, 48, TILE),
        vmem(4, 2, 2, 4, 2, 96, TILE),
        vmem(4, 2, 24, TILE, dtype=F32),
        vmem(4, 2, 24, TILE, dtype=F32),
        vmem(4, 2, 24, TILE, dtype=F32),
        vmem(TALL, 768),
        vmem(TALL, 768),
        vmem(TALL, 768),
        vmem(768, TALL),
        vmem(TALL, 768),
        vmem(768, TALL),
        vmem(6, TALL + 48, TILE),
        vmem(12, PAD, KEYS, dtype=F32),
        vmem(2, PAD, KEYS, dtype=F32),
        vmem(PAD, KEYS, dtype=jnp.int32),
        vmem(2, 12, PAD, KEYS),
        vmem(768, TALL),
        vmem(TALL, 768, dtype=F32),
        vmem(TALL, 768, dtype=F32),
        vmem(TALL, 768),
        vmem(768, TALL),
        vmem(8, TALL, TILE),
        vmem(8, TALL, TILE),
        vmem(TALL, 768, dtype=F32),
        vmem(TALL, 768, dtype=F32),
        vmem(6, 1, TILE, dtype=F32),
        vmem(4, 1, 768, dtype=F32),
        vmem(12, 1, 768, dtype=F32),
        vmem(10, 1, 768, dtype=F32),
        vmem(2, 8, 768, dtype=F32),
        vmem(2, 8, TILE, dtype=F32),
        vmem(2, 48, 128, dtype=F32),
    ]
    for shape in ((8, 768), (8, TILE), (48, 128)):
        scratch += [vmem(3, *shape, dtype=F32), vmem(4, *shape, dtype=F32), vmem(4, *shape, dtype=F32)]
    copies = 2 * len(NAMES) * N_COPY + 40
    scratch += [pltpu.SemaphoreType.DMA((copies,)), pltpu.SemaphoreType.DMA((copies,))]
    for name in NAMES:
        scratch += [vmem(*shape) for shape in Reduce.buffers(name)]
    shapes = [((197, 2, 768), BF16), ((197, 2, 768), BF16), ((328, 768), F32)]
    return pl.pallas_call(
        layer_kernel,
        out_shape=[jax.ShapeDtypeStruct(*shape) for shape in shapes],
        in_specs=[pl.BlockSpec(memory_space=pltpu.VMEM)] * len(operands),
        out_specs=[pl.BlockSpec(memory_space=pltpu.VMEM)] * len(shapes),
        scratch_shapes=scratch,
        compiler_params=pltpu.CompilerParams(
            collective_id=0, has_side_effects=True, vmem_limit_bytes=62 * 2**20
        ),
    )(*operands)


def fast_body(*operands):
    operands = list(operands)
    operands[0] = operands[0].transpose(1, 0, 2)
    operands[3] = operands[3].transpose(1, 0, 2)
    operands[15] = operands[15].reshape(1, -1)
    operands[16] = operands[16].T
    operands[19] = operands[19].T
    result, token_grad, packed = run_layer(*operands)
    result, token_grad = result.transpose(1, 0, 2), token_grad.transpose(1, 0, 2)
    inner = jnp.concatenate([packed[0:24], packed[24:48], packed[48:72]], axis=1)
    early, late = packed[288:304], packed[304:312]
    first = (result, token_grad, inner, packed[72:96], packed[96:192], packed[192:288].T, late[0], late[1], late[2], late[3])
    table = packed[312:324, 0:732].T
    return (*first, early[0], early[1], early[2], early[3], early[8:12].reshape(3072), early[4], early[5], table)


def layer_norm(values, gain, shift):
    mean = jnp.mean(values, -1, keepdims=True)
    centred = values - mean
    variance = jnp.mean(centred * centred, -1, keepdims=True)
    scaled = lax.rsqrt(variance + EPS)
    unit = centred * scaled
    return (unit * gain + shift, unit, scaled)


def norm_back(upstream, unit, scaled, gain):
    inner = upstream * gain
    first = jnp.mean(inner, -1, keepdims=True)
    second = jnp.mean(inner * unit, -1, keepdims=True)
    return (
        scaled * (inner - first - unit * second),
        jnp.sum(upstream * unit, 0),
        jnp.sum(upstream, 0),
    )


def gelu_pair(pre):
    cumul = 0.5 * (1.0 + lax.erf(pre * ROOT_HALF))
    return (pre * cumul, cumul + pre * jnp.exp(-0.5 * pre * pre) * DENSITY)


def fetch(inner_weight, outer_weight, up_weight, down_weight):
    inner_full, outer_full = (
        lax.all_gather(inner_weight, ("dp", "mlp"), axis=0, tiled=True),
        lax.all_gather(outer_weight, ("dp", "mlp"), axis=0, tiled=True),
    )
    up_full, down_full = (
        lax.all_gather(up_weight, "dp", axis=0, tiled=True),
        lax.all_gather(down_weight, "dp", axis=1, tiled=True),
    )
    return (inner_full, outer_full, up_full, down_full)


def contract_rows(left, right):
    return lax.dot_general(
        left, right, (((0,), (0,)), ((), ())), preferred_element_type=jnp.float32
    )


def contract_cols(left, right):
    return lax.dot_general(
        left, right, (((1,), (1,)), ((), ())), preferred_element_type=jnp.float32
    )


def logits_of(query, keys, bias, allowed, factor):
    raw = jnp.einsum("qhd,khd->hqk", query, keys, preferred_element_type=jnp.float32) * factor
    return jnp.where(allowed, raw + bias, -1e30)


def body(
    tokens,
    keep_mask,
    position_index,
    cotangent,
    first_gain,
    first_shift,
    inner_weight,
    query_bias,
    value_bias,
    outer_weight,
    outer_bias,
    attend_scale,
    second_gain,
    second_shift,
    up_weight,
    up_bias,
    down_weight,
    down_bias,
    feed_scale,
    position_table,
):
    micro, rows, width = tokens.shape
    heads = position_table.shape[1]
    head_dim = width // heads
    factor = head_dim ** (-0.5)
    entries = position_table.shape[0]
    columns = up_weight.shape[1]
    col_start = lax.axis_index("mlp") * columns
    up_local = lax.dynamic_slice_in_dim(up_bias, col_start, columns, 0)
    shift_vector = jnp.concatenate([query_bias, jnp.zeros_like(query_bias), value_bias])
    table_by_head = jnp.transpose(position_table)
    bias = table_by_head[:, position_index]
    seen = jnp.arange(rows)
    diagonal = seen[:, None] == seen[None, :]
    flat_index = position_index.reshape(rows * rows)
    zero_width = jnp.zeros((width,), jnp.float32)
    sum_inner = jnp.zeros((width, 3 * width), jnp.float32)
    sum_outer = jnp.zeros((width, width), jnp.float32)
    sum_up = jnp.zeros((width, columns), jnp.float32)
    sum_down = jnp.zeros((columns, width), jnp.float32)
    sum_table_heads = jnp.zeros((heads, entries), jnp.float32)
    sum_up_bias = jnp.zeros((columns,), jnp.float32)
    sum_first_gain = zero_width
    sum_first_shift = zero_width
    sum_query_bias = zero_width
    sum_value_bias = zero_width
    sum_outer_bias = zero_width
    sum_attend_scale = zero_width
    sum_second_gain = zero_width
    sum_second_shift = zero_width
    sum_down_bias = zero_width
    sum_feed_scale = zero_width
    results = []
    input_grads = []
    for index in range(micro):
        inner_full, outer_full, up_full, down_full = fetch(
            inner_weight, outer_weight, up_weight, down_weight
        )
        source = tokens[index].astype(jnp.float32)
        allowed = jnp.logical_or(keep_mask[index][None, :] == 1, diagonal)[None]
        normed_one, unit_one, scaled_one = layer_norm(source, first_gain, first_shift)
        normed_one = normed_one.astype(jnp.bfloat16)
        projected = (
            jnp.dot(normed_one, inner_full, preferred_element_type=jnp.float32) + shift_vector
        ).astype(jnp.bfloat16)
        query = projected[:, :width].reshape(rows, heads, head_dim)
        keys = projected[:, width : 2 * width].reshape(rows, heads, head_dim)
        values = projected[:, 2 * width :].reshape(rows, heads, head_dim)
        logits = logits_of(query, keys, bias, allowed, factor)
        top = jnp.max(logits, -1, keepdims=True)
        expd = jnp.exp(logits - top)
        total = jnp.sum(expd, -1, keepdims=True)
        probs = expd / total
        log_total = top + jnp.log(total)
        mixed = jnp.einsum(
            "hqk,khd->qhd", probs.astype(jnp.bfloat16), values, preferred_element_type=jnp.float32
        )
        mixed = mixed.reshape(rows, width).astype(jnp.bfloat16)
        attend = jnp.dot(mixed, outer_full, preferred_element_type=jnp.float32) + outer_bias
        resid = source + attend_scale * attend
        normed_two, unit_two, scaled_two = layer_norm(resid, second_gain, second_shift)
        normed_two = normed_two.astype(jnp.bfloat16)
        sequence_rows = lax.all_gather(normed_two, "mlp", axis=0, tiled=True)
        pre = jnp.dot(sequence_rows, up_full, preferred_element_type=jnp.float32) + up_local
        active, slope = gelu_pair(pre)
        hidden = active.astype(jnp.bfloat16)
        feed = (
            lax.psum_scatter(
                jnp.dot(hidden, down_full, preferred_element_type=jnp.float32).astype(jnp.bfloat16),
                "mlp",
                scatter_dimension=0,
                tiled=True,
            ).astype(jnp.float32)
            + down_bias
        )
        results.append((resid + feed_scale * feed).astype(jnp.bfloat16))
        inner_full, outer_full, up_full, down_full = fetch(
            inner_weight, outer_weight, up_weight, down_weight
        )
        upstream = cotangent[index].astype(jnp.float32)
        sum_feed_scale = sum_feed_scale + jnp.sum(feed * upstream, 0)
        dfeed = feed_scale * upstream
        sum_down_bias = sum_down_bias + jnp.sum(dfeed, 0)
        upstream_all = lax.all_gather(dfeed.astype(jnp.bfloat16), "mlp", axis=0, tiled=True)
        sum_down = sum_down + contract_rows(hidden, upstream_all)
        dpre = (contract_cols(upstream_all, down_full) * slope).astype(jnp.bfloat16)
        sum_up_bias = sum_up_bias + jnp.sum(dpre.astype(jnp.float32), 0)
        sum_up = sum_up + contract_rows(sequence_rows, dpre)
        dnormed_two = lax.psum_scatter(
            contract_cols(dpre, up_full).astype(jnp.bfloat16),
            "mlp",
            scatter_dimension=0,
            tiled=True,
        ).astype(jnp.float32)
        dresid_norm, part_gain, part_shift = norm_back(
            dnormed_two, unit_two, scaled_two, second_gain
        )
        sum_second_gain = sum_second_gain + part_gain
        sum_second_shift = sum_second_shift + part_shift
        dresid = upstream + dresid_norm
        sum_attend_scale = sum_attend_scale + jnp.sum(attend * dresid, 0)
        dattend = attend_scale * dresid
        sum_outer_bias = sum_outer_bias + jnp.sum(dattend, 0)
        dattend_low = dattend.astype(jnp.bfloat16)
        sum_outer = sum_outer + contract_rows(mixed, dattend_low)
        dmixed = (
            contract_cols(dattend_low, outer_full)
            .astype(jnp.bfloat16)
            .reshape(rows, heads, head_dim)
        )
        logits = logits_of(query, keys, bias, allowed, factor)
        probs = jnp.exp(logits - log_total)
        dvalues = jnp.einsum(
            "hqk,qhd->khd", probs.astype(jnp.bfloat16), dmixed, preferred_element_type=jnp.float32
        )
        dprobs = jnp.einsum("qhd,khd->hqk", dmixed, values, preferred_element_type=jnp.float32)
        dlogits = probs * (dprobs - jnp.sum(dprobs * probs, -1, keepdims=True))
        sum_table_heads = sum_table_heads.at[:, flat_index].add(dlogits.reshape(heads, rows * rows))
        dlogits_low = dlogits.astype(jnp.bfloat16)
        dquery = (
            jnp.einsum("hqk,khd->qhd", dlogits_low, keys, preferred_element_type=jnp.float32)
            * factor
        )
        dkeys = (
            jnp.einsum("hqk,qhd->khd", dlogits_low, query, preferred_element_type=jnp.float32)
            * factor
        )
        dprojected = jnp.concatenate(
            [dquery.reshape(rows, width), dkeys.reshape(rows, width), dvalues.reshape(rows, width)],
            axis=1,
        ).astype(jnp.bfloat16)
        sum_query_bias = sum_query_bias + jnp.sum(dprojected[:, :width].astype(jnp.float32), 0)
        sum_value_bias = sum_value_bias + jnp.sum(dprojected[:, 2 * width :].astype(jnp.float32), 0)
        sum_inner = sum_inner + contract_rows(normed_one, dprojected)
        dnormed_one = contract_cols(dprojected, inner_full)
        dsource_norm, part_gain, part_shift = norm_back(
            dnormed_one, unit_one, scaled_one, first_gain
        )
        sum_first_gain = sum_first_gain + part_gain
        sum_first_shift = sum_first_shift + part_shift
        input_grads.append((dresid + dsource_norm).astype(jnp.bfloat16))
    sum_table = jnp.transpose(sum_table_heads)
    gradient_inner, gradient_outer = (
        lax.psum_scatter(sum_inner, ("dp", "mlp"), scatter_dimension=0, tiled=True),
        lax.psum_scatter(sum_outer, ("dp", "mlp"), scatter_dimension=0, tiled=True),
    )
    gradient_up, gradient_down = (
        lax.psum_scatter(sum_up, "dp", scatter_dimension=0, tiled=True),
        lax.psum_scatter(sum_down, "dp", scatter_dimension=1, tiled=True),
    )
    up_bias_full = lax.dynamic_update_slice_in_dim(
        jnp.zeros((up_bias.shape[0],), jnp.float32), sum_up_bias, col_start, 0
    )
    summed = lax.psum(
        (
            sum_first_gain,
            sum_first_shift,
            sum_query_bias,
            sum_value_bias,
            sum_outer_bias,
            sum_attend_scale,
            sum_second_gain,
            sum_second_shift,
            up_bias_full,
            sum_down_bias,
            sum_feed_scale,
            sum_table,
        ),
        ("dp", "mlp"),
    )
    return (
        jnp.stack(results),
        jnp.stack(input_grads),
        gradient_inner,
        gradient_outer,
        gradient_up,
        gradient_down,
        summed[0],
        summed[1],
        summed[2],
        summed[3],
        summed[4],
        summed[5],
        summed[6],
        summed[7],
        summed[8],
        summed[9],
        summed[10],
        summed[11],
    )


def solution(mesh):
    special = mesh.shape["dp"] == 8 and mesh.shape["mlp"] == 4
    placed = (
        P(None, ("dp", "mlp"), None),
        P(None, ("dp", "mlp")),
        P(),
        P(None, ("dp", "mlp"), None),
        P(),
        P(),
        P(("dp", "mlp"), None),
        P(),
        P(),
        P(("dp", "mlp"), None),
        P(),
        P(),
        P(),
        P(),
        P("dp", "mlp"),
        P(),
        P("mlp", "dp"),
        P(),
        P(),
        P(),
    )
    return jax.shard_map(
        fast_body if special else body,
        mesh=mesh,
        in_specs=placed,
        out_specs=(
            P(None, ("dp", "mlp"), None),
            P(None, ("dp", "mlp"), None),
            P(("dp", "mlp"), None),
            P(("dp", "mlp"), None),
            P("dp", "mlp"),
            P("mlp", "dp"),
            P(),
            P(),
            P(),
            P(),
            P(),
            P(),
            P(),
            P(),
            P(),
            P(),
            P(),
            P(),
        ),
        check_vma=False,
    )
```

```python
import functools

import jax
import jax.numpy as jnp
from jax import lax
from jax.experimental import pallas as pl
from jax.experimental.pallas import tpu as pltpu
from jax.sharding import PartitionSpec as P

EPS = 1e-06
ROOT_HALF = 0.7071067811865476
DENSITY = 0.3989422804014327


MESH = pl.DeviceIdType.MESH
F32 = jnp.float32
BF16 = jnp.bfloat16
TILE = 384
PAD = 208
TALL = 2 * PAD
KEYS = 256
N_COPY = 11
NAMES = ("I0", "I1", "I2", "O", "U0a", "U0b", "U1a", "U1b", "N0a", "N0b", "N1a", "N1b")
GATHER = {"U0a": "xZy", "N0a": "yZx", "I1": "zxy", "U1a": "yZx", "I2": "zyx", "O": "zxy", "I0": "zyx", "U1b": "xZy", "N1b": "xZy", "N0b": "Zxy", "N1a": "yZx", "U0b": "zyx"}
REDUCE = {"U0a": "xzy", "N0a": "xZy", "I1": "xyZ", "U1a": "xzy", "I2": "xyz", "O": "xyz", "I0": "yZx", "U1b": "yxZ", "N1b": "yxZ", "N0b": "yxz", "N1a": "yZx", "U0b": "yxz"}
ORDER = (
    71, 72, 85, 86, 99, 100, 57, 58, 127, 128, 0, 30, 112, 168, 15, 140, 154, 13, 210, 196, 14, 70, 24, 16,
    34, 84, 43, 2, 73, 74, 21, 22, 98, 31, 87, 88, 23, 183, 29, 56, 75, 101, 76, 17, 113, 126, 18, 169,
    89, 102, 184, 32, 141, 1, 90, 59, 25, 114, 60, 155, 26, 103, 211, 197, 170, 104, 182, 129, 130, 61, 142, 115,
    116, 62, 9, 10, 171, 172, 156, 185, 186, 3, 131, 4, 143, 144, 212, 132, 117, 198, 157, 158, 118, 36, 173, 187,
    45, 174, 213, 214, 188, 37, 38, 199, 200, 46, 145, 159, 47, 146, 119, 133, 189, 175, 160, 48, 39, 215, 120, 134,
    201, 190, 176, 216, 202, 40, 41, 49, 121, 123, 124, 135, 50, 161, 217, 147, 203, 7, 33, 162, 218, 191, 177, 148,
    42, 122, 136, 137, 138, 204, 224, 5, 225, 6, 105, 192, 193, 194, 179, 11, 163, 106, 139, 12, 63, 149, 151, 152,
    27, 219, 125, 64, 164, 195, 180, 19, 20, 77, 205, 28, 91, 165, 78, 107, 150, 178, 226, 51, 92, 220, 207, 52,
    166, 65, 53, 221, 227, 54, 167, 108, 79, 109, 110, 153, 208, 236, 55, 222, 181, 67, 232, 35, 233, 44, 80, 93,
    111, 228, 8, 206, 234, 229, 223, 68, 81, 209, 94, 95, 96, 235, 230, 238, 66, 82, 69, 97, 231, 83, 237,
)


def place():
    dp = lax.axis_index("dp")
    mlp = lax.axis_index("mlp")
    return lax.div(dp, 2), lax.rem(dp, 2), lax.div(mlp, 2), lax.rem(mlp, 2)


def device(z, x, y, c):
    return (z * 2 + x, y * 2 + c)


def greet(z, x, y, c):
    barrier = pltpu.get_barrier_semaphore()
    others = [device(lax.rem(z + d, 4), x, y, c) for d in (1, 2, 3)]
    others += [device(z, 1 - x, y, c), device(z, x, 1 - y, c), device(z, 1 - x, 1 - y, c), device(z, x, y, 1 - c)]
    for other in others:
        pl.semaphore_signal(barrier, inc=1, device_id=other, device_id_type=MESH)
    return lambda: pl.semaphore_wait(barrier, len(others))


class Link:
    def __init__(self, send, recv):
        self.send, self.recv, self.pending = send, recv, {}

    def make(self, src, dst, slot, target):
        return pltpu.make_async_remote_copy(
            src_ref=src,
            dst_ref=dst,
            send_sem=self.send.at[slot],
            recv_sem=self.recv.at[slot],
            device_id=target,
            device_id_type=MESH,
        )

    def copy(self, src, dst, slot, target, group=None):
        made = self.make(src, dst, slot, target)
        made.start()
        self.pending.setdefault(group, []).append((made, None))
        return made

    def drain(self, *groups):
        for group in groups or tuple(self.pending):
            for made, sender in self.pending.pop(group, []):
                if sender is None:
                    made.wait_send()
                else:
                    pl.when(sender)(made.wait_send)


class Some:
    def __init__(self, link, src, dst, slot, target, sender, getter, group):
        self.made = link.make(src, dst, slot, target)
        self.getter = getter
        pl.when(sender)(self.made.start)
        link.pending.setdefault(group, []).append((self.made, sender))

    def wait_recv(self):
        pl.when(self.getter)(self.made.wait_recv)


def mix(here, *there):
    total = here[...].astype(F32)
    for other in there:
        total = total + other[...].astype(F32)
    here[...] = total.astype(BF16)


class Unit:
    def __init__(self, link, ref, name, where, base):
        self.link, self.ref, self.where, self.base, self.name = link, ref, where, base, name
        self.narrow = name[0] in "IO"
        self.rows = slice(None) if self.narrow else pl.ds(48 * "ab".index(name[2]), 48)
        self.group = name if base < len(NAMES) * N_COPY else None
        z = where[0]
        self.side = lax.div(z, 2)
        self.mate = z + 1 - 2 * lax.rem(z, 2)
        self.inner = jnp.logical_and(z > 0, z < 3)
        self.outer = jnp.logical_not(self.inner)

    def put(self, src, dst, slot, target):
        return self.link.copy(src, dst, self.base + slot, target, self.group)

    def some(self, src, dst, slot, z, sender, getter):
        x, y, c = self.where[1:]
        return Some(self.link, src, dst, self.base + slot, device(z, x, y, c), sender, getter, self.group)

    def at(self, z, x, y, c):
        return self.ref.at[c, z, x, y] if self.narrow else self.ref.at[y, c, z, x, self.rows]

    def by_core(self, c):
        return self.ref.at[c] if self.narrow else self.ref.at[:, c, :, :, self.rows]

    def plane(self, axis, x, y, c):
        every = slice(None)
        return self.at(every, x, every, c) if axis == "x" else self.at(every, every, y, c)

    def pairs(self, axis, z):
        x, y, c = self.where[1:]
        every = slice(None)
        return self.at(z, every, y, c) if axis == "x" else self.at(z, x, every, c)

    def two(self, side):
        return pl.ds(2 * side, 2)

    def spread(self, part, slot):
        z, x, y, c = self.where
        return [self.put(part, part, slot + d - 1, device(lax.rem(z + d, 4), x, y, c)) for d in (1, 2, 3)]

    def across(self, axis, src, dst, slot):
        z, x, y, c = self.where
        target = {"x": (z, 1 - x, y, c), "y": (z, x, 1 - y, c), "c": (z, x, y, 1 - c)}[axis]
        return self.put(src, dst, slot, device(*target))

    def other(self, axis):
        z, x, y, c = self.where
        return (1 - x, y, c) if axis == "x" else (x, 1 - y, c)


class Gather(Unit):
    def __init__(self, *given):
        super().__init__(*given)
        self.axes = GATHER[self.name]
        self.steps = "Z" in self.axes
        self.early = self.axes[0] in "zZ"
        self.z, self.to_c = [], []

    def own(self, z):
        x, y, c = self.where[1:]
        return self.at(z, x, y, c) if self.early else self.pairs(self.axes[0], z)

    def swap_pair(self, slot):
        part = self.own(self.where[0])
        self.z = [self.put(part, part, slot, device(self.mate, *self.where[1:]))]

    def Z(self):
        z, x, y, c = self.where
        part = self.at(z, x, y, c)
        if not self.early:
            self.first = self.across(self.axes[0], part, part, 0)
        if not self.steps:
            self.z = self.spread(part, 1)
        elif self.early:
            self.swap_pair(1)

    def m(self):
        if self.steps:
            self.z[0].wait_recv()
            part = self.own(self.two(self.side))
            self.z = [self.some(part, part, 2, 3 - self.where[0], self.inner, self.inner)]

    def n(self):
        if self.steps:
            self.z[0].wait_recv()
            part = self.own(self.two(1 - self.side))
            self.z = [self.some(part, part, 3, self.mate, self.inner, self.outer)]

    def L(self):
        z, x, y, c = self.where
        if not self.early:
            self.first.wait_recv()
            if self.steps:
                self.swap_pair(1)
            else:
                self.z += self.spread(self.at(z, *self.other(self.axes[0])), 4)
            return
        for made in self.z:
            made.wait_recv()
        part = self.at(slice(None), x, y, c)
        self.made = {axis: self.across(axis, part, part, 4 + i) for i, axis in enumerate(self.axes[1:] + "c")}
        self.to_c = [self.made["c"]]

    def pass_on(self, axis, slot):
        self.made[axis].wait_recv()
        part = self.at(slice(None), *self.other(axis))
        self.to_c.append(self.across("c", part, part, slot))
        return part

    def P(self):
        z, x, y, c = self.where
        last = self.axes[2]
        if self.early:
            part = self.pass_on(self.axes[1], 7)
            self.last = self.across(last, part, part, 8)
            return
        for made in self.z:
            made.wait_recv()
        part = self.plane(last, x, y, c)
        self.last = self.across(last, part, part, 7)
        self.to_c = [self.across("c", part, part, 8)]

    def Q(self):
        if self.early:
            self.pass_on(self.axes[2], 9)

    def R(self):
        z, x, y, c = self.where
        self.last.wait_recv()
        part = self.at(slice(None), 1 - x, 1 - y, c) if self.early else self.plane(self.axes[2], 1 - x, 1 - y, c)
        self.to_c.append(self.across("c", part, part, 10))

    def F(self):
        for made in self.to_c:
            made.wait_recv()


class Reduce(Unit):
    def __init__(self, *given):
        super().__init__(*given)
        self.axes = REDUCE[self.name]
        self.steps = "Z" in self.axes
        self.late = self.axes[2] in "zZ"

    @staticmethod
    def buffers(name):
        narrow, axes = name[0] in "IO", REDUCE[name]
        half = (4, 2, 2) if narrow else (2, 4, 2)
        quarter = (2, 4) if not narrow and axes[0] == "x" else (4, 2)
        one = () if axes[2] in "zZ" else (2,)
        two = (2, 2) if one else (2,)
        along_z = [(*two,), (*two,), (*one,)] if "Z" in axes else [(3, *one)]
        shapes = [half, quarter, (4,) if axes[2] in "zZ" else (), *along_z]
        return [(*shape, 48, TILE) for shape in shapes]

    def set_buffers(self, half, quarter, side, *along_z):
        self.half, self.quarter, self.side_ref, self.along_z = half, quarter, side, along_z

    def own(self, z):
        x, y, c = self.where[1:]
        return self.at(z, x, y, c) if self.late else self.pairs(self.axes[2], z)

    def c(self):
        self.made = self.across("c", self.by_core(1 - self.where[3]), self.half, 0)

    def d(self):
        z, x, y, c = self.where
        self.made.wait_recv()
        mix(self.by_core(c), self.half)
        axis = self.axes[0]
        self.made = self.across(axis, self.plane(axis, 1 - x, 1 - y, c), self.quarter, 1)

    def e(self):
        z, x, y, c = self.where
        self.made.wait_recv()
        mix(self.plane(self.axes[0], x, y, c), self.quarter)
        if not self.late:
            self.into_z()
            return
        axis = self.axes[1]
        self.made = self.across(axis, self.at(slice(None), *self.other(axis)), self.side_ref, 2)

    def into_z(self):
        z, x, y, c = self.where
        if self.steps:
            part = self.own(self.two(1 - self.side))
            self.z = [self.some(part, self.along_z[0], 3, self.mate, self.outer, self.inner)]
            return
        self.z = []
        for d in (1, 2, 3):
            far = lax.rem(z + d, 4)
            self.z.append(self.put(self.own(far), self.along_z[0].at[d - 1], 2 + d, device(far, x, y, c)))

    def p(self):
        if self.steps:
            self.z[0].wait_recv()
            part = self.own(self.two(1 - self.side))
            pl.when(self.inner)(functools.partial(mix, part, self.along_z[0]))
            self.z = [self.some(part, self.along_z[1], 4, 3 - self.where[0], self.inner, self.inner)]

    def q(self):
        if self.steps:
            self.z[0].wait_recv()
            pl.when(self.inner)(functools.partial(mix, self.own(self.two(self.side)), self.along_z[1]))
            self.z = [self.put(self.own(self.mate), self.along_z[2], 5, device(self.mate, *self.where[1:]))]

    def parts(self):
        for made in self.z:
            made.wait_recv()
        return [self.along_z[2]] if self.steps else [self.along_z[0].at[d] for d in range(3)]

    def f(self):
        z, x, y, c = self.where
        if self.late:
            self.made.wait_recv()
            mix(self.at(slice(None), x, y, c), self.side_ref)
            self.into_z()
            return
        mix(self.own(z), *self.parts())
        axis = self.axes[2]
        self.made = self.across(axis, self.at(z, *self.other(axis)), self.side_ref, 6)

    def total(self):
        if self.late:
            parts = self.parts()
        else:
            self.made.wait_recv()
            parts = [self.side_ref]
        total = self.at(*self.where)[...].astype(F32)
        for part in parts:
            total = total + part[...].astype(F32)
        return total


class Everywhere:
    def __init__(self, link, ref, core_ref, plane_ref, line_ref, base, where):
        self.link, self.ref, self.where, self.base = link, ref, where, base
        self.core_ref, self.plane_ref, self.line_ref = core_ref, plane_ref, line_ref

    def to_core(self):
        z, x, y, c = self.where
        self.made = [self.link.copy(self.ref.at[1 - c], self.core_ref.at[0], self.base, device(z, x, y, 1 - c))]

    def wait(self):
        for made in self.made:
            made.wait_recv()

    def to_plane(self):
        z, x, y, c = self.where
        self.wait()
        chip = self.plane_ref.at[3]
        chip[...] = self.ref[c] + self.core_ref[0]
        targets = (device(z, 1 - x, y, c), device(z, x, 1 - y, c), device(z, 1 - x, 1 - y, c))
        self.made = [
            self.link.copy(chip, self.plane_ref.at[n], self.base + 1 + n, target) for n, target in enumerate(targets)
        ]

    def to_line(self):
        z, x, y, c = self.where
        self.wait()
        got = self.plane_ref
        self.line_ref[z] = (got[3] + got[0]) + (got[1] + got[2])
        part = self.line_ref.at[z]
        self.made = [
            self.link.copy(part, part, self.base + 3 + d, device(lax.rem(z + d, 4), x, y, c)) for d in (1, 2, 3)
        ]

    def to_mate(self):
        z, x, y, c = self.where
        self.wait()
        got = self.line_ref
        part = self.core_ref.at[1 + c]
        part[...] = (got[0] + got[1]) + (got[2] + got[3])
        self.made = [self.link.copy(part, part, self.base + 7, device(z, x, y, 1 - c))]

    def total(self, half):
        return self.core_ref[1 + half]


def dot(left, right):
    return lax.dot_general(left, right, (((1,), (0,)), ((), ())), preferred_element_type=F32)


def dot_nt(left, right):
    return lax.dot_general(left, right, (((1,), (1,)), ((), ())), preferred_element_type=F32)


def dot_tn(left, right):
    return lax.dot_general(left, right, (((0,), (0,)), ((), ())), preferred_element_type=F32)


def fold(values):
    rows, width = values.shape
    return jnp.sum(values.reshape(rows // 8, 8, width), 0)


def unit_of(values):
    mean = jnp.mean(values, -1, keepdims=True)
    centred = values - mean
    variance = jnp.mean(centred * centred, -1, keepdims=True)
    scaled = lax.rsqrt(variance + EPS)
    return centred * scaled, scaled


def loop(count, step, init):
    return lax.fori_loop(0, count, step, init)


def by_rows(step, init, first=0, count=13):
    size = 32

    def one(index, carried):
        return step(pl.ds(pl.multiple_of((index + first) * size, size), size), carried)

    one.__name__ = step.__name__
    return loop(count, one, init)


def layer_kernel(*refs):
    (
        tokens, keep, places, cotangent, first_gain1, first_shift1, inner_in, query_bias1, value_bias1, outer_in, outer_bias1,
        attend_scale1, second_gain1, second_shift1, up_in, up_bias, down_in, down_bias1, feed_scale1, table_in,
        result, token_grad, packed,
        *rest,
    ) = refs
    (
        narrow, wide, small, pair, swap,
        source, upstream, normed1, normed1_t, normed2, normed2_t, qkv, bias, mask, index, probs, mix_t, attend, resid,
        dfeed, dfeed_t, hidden, slope, total, dnormed2, shifts, ups, tab, vectors,
        early, late, hits, early_core, early_plane, early_line, late_core, late_plane, late_line, hits_core, hits_plane, hits_line,
        send, recv, *buffers,
    ) = rest
    outer_out, up_out, down_out, early_out, late_out, table_out = (
        packed.at[pl.ds(first, rows)] for first, rows in ((72, 24), (96, 96), (192, 96), (288, 16), (304, 8), (312, 16))
    )
    dresid, dproj, dmixed, mixed, dattend = attend, hidden, normed2, normed2, dfeed
    where = z, x, y, c = place()
    all_here = greet(*where)
    link = Link(send, recv)
    gathers, reduces = {}, {}
    taken = 0
    for n, name in enumerate(NAMES):
        ref = narrow.at[n] if n < 4 else wide.at[(n - 4) // 2]
        gathers[name] = Gather(link, ref, name, where, n * N_COPY)
        reduces[name] = Reduce(link, ref, name, where, (len(NAMES) + n) * N_COPY)
        count = len(Reduce.buffers(name))
        reduces[name].set_buffers(*buffers[taken : taken + count])
        taken += count
    spare = 2 * len(NAMES) * N_COPY
    sums = {
        "E": Everywhere(link, early, early_core, early_plane, early_line, spare + 5, where),
        "l": Everywhere(link, late, late_core, late_plane, late_line, spare + 15, where),
        "t": Everywhere(link, hits, hits_core, hits_plane, hits_line, spare + 25, where),
    }
    mates = []
    kept = {}
    for k in range(3):
        for core in range(2):
            for part in range(3):
                start = part * 768 + (core * 3 + k) * 128
                small[k, core, :, part * 128 : part * 128 + 128] = inner_in[:, start : start + 128].astype(F32)
    for core in range(2):
        small[3, core] = outer_in[:, core * TILE : core * TILE + TILE].astype(F32)
    for k in range(2):
        cols = slice(k * TILE, k * TILE + TILE)
        wide[k, y, c, z, x] = up_in[:, cols]
        wide[2 + k, y, c, z, x] = down_in[:, cols]
    all_here()
    mate = link.copy(small.at[:, 1 - c], pair.at[:, c], spare, device(z, x, y, 1 - c))
    for name in NAMES[4:]:
        if not gathers[name].early:
            gathers[name].Z()
    pair[:, c] = small[:, c]
    mate.wait_recv()
    link.drain(None)
    for unit in range(4):
        narrow[unit, c, z, x, y] = pair[unit].reshape(48, TILE).astype(BF16)
    for name in GATHER:
        if name[0] in "IO" or gathers[name].early:
            gathers[name].Z()

    given = (first_gain1, first_shift1, query_bias1, value_bias1, outer_bias1, attend_scale1, second_gain1, second_shift1, down_bias1, feed_scale1)
    for n, ref in enumerate(given):
        vectors[n] = ref[...].reshape(1, 768)
    (first_gain, first_shift, query_bias, value_bias, outer_bias, attend_scale, second_gain, second_shift, down_bias, feed_scale) = (
        vectors.at[n] for n in range(10)
    )

    for image in range(2):
        last = pl.ds(image * PAD + 192, 16)
        source[last, :] = jnp.zeros((16, 768), BF16)
        upstream[last, :] = jnp.zeros((16, 768), BF16)
        source[pl.ds(image * PAD, 197), :] = tokens[:, image, :]
        upstream[pl.ds(image * PAD, 197), :] = cotangent[:, image, :]
    zero = jnp.zeros((8, 768), F32)
    lane = lax.broadcasted_iota(jnp.int32, (1, 128), 1)
    picks = [(lane < 64).astype(F32).astype(BF16), (lane >= 64).astype(F32).astype(BF16)]

    def rows_of(image):
        return slice(image * PAD, image * PAD + PAD)

    def keys_of(image):
        return slice(image * PAD, image * PAD + KEYS)

    def cols_of(p):
        return pl.ds(pl.multiple_of(p * 128, 128), 128)

    def half(core):
        return slice(core * TILE, core * TILE + TILE)

    def norm1(n):
        def norm_first(rows, carried):
            unit, _ = unit_of(source[rows, :].astype(F32))
            normed1[rows, :] = (unit * first_gain[...] + first_shift[...]).astype(BF16)
            lifted = upstream[rows, :].astype(F32) * feed_scale[...]
            dfeed[rows, :] = lifted.astype(BF16)
            return carried + fold(lifted)

        kept["down"] = by_rows(norm_first, kept.get("down", zero), 7 * n, 7 - n)
        if n == 0:
            return
        early[...] = jnp.zeros((2, 8, 768), F32)
        late[...] = jnp.zeros((2, 8, TILE), F32)
        early[0, 4:5, :] = jnp.sum(kept.pop("down"), 0, keepdims=True)
        zero_row = jnp.zeros((1, 128), F32)
        for p in range(6):
            cols = slice(p * 128, p * 128 + 128)
            shifts[p] = jnp.concatenate([query_bias[:, cols], zero_row, value_bias[:, cols]], axis=1)
            qkv[p, TALL:, :] = jnp.zeros((48, TILE), BF16)

    def fill():
        index[...] = jnp.full((PAD, KEYS), -1, jnp.int32)
        index[0:197, 0:197] = places[...]
        tab[...] = jnp.zeros((12, 1, 768), F32)
        for head in range(12):
            tab[head, :, 0:732] = table_in[head : head + 1, :]
        row_of = lax.broadcasted_iota(jnp.int32, (PAD, KEYS), 0)
        col_of = lax.broadcasted_iota(jnp.int32, (PAD, KEYS), 1)
        for image in range(2):
            mask[image] = jnp.full((PAD, KEYS), -1e30, F32)
            shown = jnp.where(keep[image : image + 1, :] == 1, 0.0, -1e30).astype(F32)
            mask[image, :, 0:197] = jnp.broadcast_to(shown, (PAD, 197))
            mask[image] = jnp.where(row_of == col_of, 0.0, mask[image])

    def look(k, n):
        def look_up(step, carried):
            head = 2 * ((n // 2) * 3 + k) + n % 2
            for side in range(2):
                cols = slice(side * 128, side * 128 + 128)
                spot = index[:, cols]
                low, high = spot & 127, spot >> 7
                found = jnp.zeros((PAD, 128), F32)
                for piece in range(6):
                    row = tab[head, :, piece * 128 : piece * 128 + 128]
                    picked = jnp.take_along_axis(jnp.broadcast_to(row, (PAD, 128)), low, axis=1)
                    found = jnp.where(high == piece, picked, found)
                bias[head, :, cols] = found
            return carried

        loop(1, look_up, 0)

    def turn1():
        normed1_t[...] = normed1[...].T

    def turnd():
        dfeed_t[...] = dfeed[...].T

    def proj(k):
        def project(core, carried):
            p = core * 3 + k
            weight = narrow[k, core].reshape(768, TILE)
            scaling = jnp.where(lax.broadcasted_iota(jnp.int32, (1, TILE), 1) < 128, 0.125, 1.0).astype(F32)
            value = (dot(normed1[...], weight) + shifts[p]).astype(BF16)
            qkv[p, 0:TALL, :] = (value.astype(F32) * scaling).astype(BF16)
            return carried

        loop(2, project, 0)

    def att(k):
        def attend_pair(core, carried):
            p = core * 3 + k
            first_half = lax.broadcasted_iota(jnp.int32, (PAD, 128), 1) < 64
            for image in range(2):
                query = qkv[p, rows_of(image), 0:128]
                keys = qkv[p, keys_of(image), 128:256]
                values = qkv[p, keys_of(image), 256:384]
                outs = []
                for t in range(2):
                    logits = dot_nt(query * picks[t], keys) + bias[2 * p + t] + mask[image]
                    top = jnp.max(logits, -1, keepdims=True)
                    expd = jnp.exp(logits - top)
                    share = (expd * (1.0 / jnp.sum(expd, -1, keepdims=True))).astype(BF16)
                    probs[image, 2 * p + t] = share
                    outs.append(dot(share, values))
                mixed[rows_of(image), cols_of(p)] = jnp.where(first_half, outs[0], outs[1]).astype(BF16)
            return carried

        loop(2, attend_pair, 0)

    def out():
        for core in range(2):
            attend[:, half(core)] = dot(mixed[...], narrow[3, core].reshape(768, TILE)) + outer_bias[:, half(core)]
        mix_t[...] = mixed[...].T

    def norm2():
        def norm_second(rows, carried):
            value = source[rows, :].astype(F32) + attend_scale[...] * attend[rows, :]
            resid[rows, :] = value
            unit, _ = unit_of(value)
            normed2[rows, :] = (unit * second_gain[...] + second_shift[...]).astype(BF16)
            return carried

        by_rows(norm_second, 0)
        normed2_t[...] = normed2[...].T

    def widening(k, side):
        def widen(core, carried):
            weight = wide[k, side, core].reshape(768, TILE)
            cols = pl.ds(pl.multiple_of((side * 2 + core) * 768 + k * TILE, 128), TILE)
            pre = dot(normed2[...], weight) + up_bias[:, cols]
            cumul = 0.5 * (1.0 + lax.erf(pre * ROOT_HALF))
            b = k * 4 + side * 2 + core
            hidden[b] = (pre * cumul).astype(BF16)
            slope[b] = (cumul + pre * jnp.exp(-0.5 * pre * pre) * DENSITY).astype(BF16)
            return carried

        loop(2, widen, 0)

    def joined(ref, b):
        return jnp.concatenate([ref[b], ref[b + 1]], axis=1)

    def weights(slot, side):
        return jnp.concatenate([wide[slot, side, core].reshape(768, TILE) for core in range(2)], axis=1)

    def back(k, side):
        b = k * 4 + side * 2

        def narrow_back(step, carried):
            dpre = (dot(dfeed[...], weights(2 + k, side)) * joined(slope, b).astype(F32)).astype(BF16)
            for core in range(2):
                slope[b + core] = dpre[:, half(core)]
            ups[b // 2] = jnp.sum(fold(dpre.astype(F32)), 0, keepdims=True)
            part = dot_nt(dpre, weights(k, side))
            dnormed2[...] = part if b == 0 else dnormed2[...] + part
            return carried

        loop(1, narrow_back, 0)

    def grad(k, side):
        if side == 0:
            link.drain(*(what + str(k) + part for what in "UN" for part in "ab"))
        b = k * 4 + side * 2

        def narrow_grad(step, carried):
            both = joined(hidden, b)
            part = dot_nt(both, weights(2 + k, side))
            total[...] = part if b == 0 else total[...] + part
            up_grad = dot(normed2_t[...], joined(slope, b)).astype(BF16)
            down_grad = dot(dfeed_t[...], both).astype(BF16)
            for core in range(2):
                wide[2 + k, side, core] = up_grad[:, half(core)].reshape(4, 2, 96, TILE)
                wide[k, side, core] = down_grad[:, half(core)].reshape(4, 2, 96, TILE)
            return carried

        loop(1, narrow_grad, 0)

    def sec(n):
        def second_back(rows, carried):
            gain_sum, shift_sum, scale_sum, bias_sum = carried
            unit, scaled = unit_of(resid[rows, :])
            grad = dnormed2[rows, :]
            inner = grad * second_gain[...]
            first = jnp.mean(inner, -1, keepdims=True)
            second = jnp.mean(inner * unit, -1, keepdims=True)
            back = upstream[rows, :].astype(F32) + scaled * (inner - first - unit * second)
            scale_sum = scale_sum + fold(attend[rows, :] * back)
            dresid[rows, :] = back
            lifted = attend_scale[...] * back
            dattend[rows, :] = lifted.astype(BF16)
            return gain_sum + fold(grad * unit), shift_sum + fold(grad), scale_sum, bias_sum + fold(lifted)

        kept["sec"] = by_rows(second_back, kept.get("sec", (zero,) * 4), 7 * n, 7 - n)
        if n == 1:
            for block in range(4):
                for k in range(2):
                    b = k * 4 + block
                    early[1, block : 1 + block, half(k)] = ups[b // 2, :, half(b % 2)]
            for row, value in zip((2, 3, 1, 0), kept.pop("sec")):
                early[0, row : row + 1, :] = jnp.sum(value, 0, keepdims=True)

    def res():
        def feed_out(rows, carried):
            feed = total[rows, :] + down_bias[...]
            total[rows, :] = resid[rows, :] + feed_scale[...] * feed
            return carried + fold(feed * upstream[rows, :].astype(F32))

        early[0, 5:6, :] = jnp.sum(by_rows(feed_out, zero), 0, keepdims=True)
        for image in range(2):
            result[:, image, :] = total[pl.ds(image * PAD, 197), :].astype(BF16)

    def dmix():
        parts = [dot_nt(dattend[:, half(core)], narrow[3, core].reshape(768, TILE)) for core in range(2)]
        dmixed[...] = (parts[0] + parts[1]).astype(BF16)

    def gout():
        link.drain("O")
        for core in range(2):
            narrow[3, core] = dot(mix_t[...], dattend[:, half(core)]).astype(BF16).reshape(4, 2, 2, 48, TILE)

    def attb(k):
        def attend_back(core, carried):
            p = core * 3 + k
            first_half = lax.broadcasted_iota(jnp.int32, (PAD, 128), 1) < 64
            hit = [None, None]
            for image in range(2):
                rows = rows_of(image)
                query = qkv[p, rows, 0:128]
                keys = qkv[p, keys_of(image), 128:256]
                values = qkv[p, keys_of(image), 256:384]
                above = dmixed[rows, cols_of(p)]
                dquery, dkeys, dvalues = [], [], []
                for t in range(2):
                    share = probs[image, 2 * p + t]
                    dvalues.append(dot_tn(share, above)[0:PAD])
                    dshare = dot_nt(above * picks[t], values)
                    full = share.astype(F32)
                    dlogits = full * (dshare - jnp.sum(dshare * full, -1, keepdims=True))
                    hit[t] = dlogits if image == 0 else hit[t] + dlogits
                    low = dlogits.astype(BF16)
                    dquery.append(dot(low, keys) * 0.125)
                    dkeys.append(dot_tn(low, query)[0:PAD])
                dproj[p, rows, 0:128] = jnp.where(first_half, dquery[0], dquery[1]).astype(BF16)
                dproj[p, rows, 128:256] = jnp.where(first_half, dkeys[0], dkeys[1]).astype(BF16)
                dproj[p, rows, 256:384] = jnp.where(first_half, dvalues[0], dvalues[1]).astype(BF16)
            for t in range(2):
                bias[2 * p + t] = hit[t]
            return carried

        loop(2, attend_back, 0)

    def projb(k):
        link.drain("I" + str(k))

        def project_back(core, carried):
            p = core * 3 + k
            grad = dproj[p]
            summed = jnp.sum(fold(grad.astype(F32)), 0, keepdims=True)
            late[core, 2:3, k * 128 : k * 128 + 128] = summed[:, 0:128]
            late[core, 3:4, k * 128 : k * 128 + 128] = summed[:, 256:384]
            part = dot_nt(grad, narrow[k, core].reshape(768, TILE))
            dnormed2[...] = jnp.where(core == 0, 0.0, dnormed2[...]) + part if k == 0 else dnormed2[...] + part
            narrow[k, core] = dot(normed1_t[...], grad).astype(BF16).reshape(4, 2, 2, 48, TILE)
            return carried

        loop(2, project_back, 0)

    def first(n):
        def first_back(rows, carried):
            gain_sum, shift_sum = carried
            grad = dnormed2[rows, :]
            unit, scaled = unit_of(source[rows, :].astype(F32))
            inner = grad * first_gain[...]
            mean = jnp.mean(inner, -1, keepdims=True)
            second = jnp.mean(inner * unit, -1, keepdims=True)
            dresid[rows, :] = dresid[rows, :] + scaled * (inner - mean - unit * second)
            return gain_sum + fold(grad * unit), shift_sum + fold(grad)

        kept["first"] = by_rows(first_back, kept.get("first", (zero, zero)), 7 * n, 7 - n)
        if n == 0:
            return
        found = kept.pop("first")
        for row in range(2):
            value = jnp.sum(found[row], 0, keepdims=True)
            for core in range(2):
                late[core, row : row + 1, :] = value[:, half(core)]

    def tok():
        for image in range(2):
            token_grad[:, image, :] = dresid[pl.ds(image * PAD, 197), :].astype(BF16)

    def counting(n):
        low_of = lax.broadcasted_iota(jnp.int32, (128, KEYS), 0)
        high_of = lax.broadcasted_iota(jnp.int32, (8, KEYS), 0)

        def count(group, carried):
            eight = pl.ds(pl.multiple_of((group + 5 * n) * 8, 8), 8)
            spots = index[eight, :]
            for r in range(8):
                spot = jnp.broadcast_to(spots[r : r + 1, :], (8, KEYS))
                high = (spot >> 7) == high_of
                parts = []
                for head in range(12):
                    grads = bias[head, eight, :]
                    parts.append(jnp.where(high, jnp.broadcast_to(grads[r : r + 1, :], (8, KEYS)), 0.0))
                spread = jnp.concatenate(parts, axis=0).astype(BF16)
                low = jnp.concatenate([spot & 127] * 16, axis=0)
                which = (low == low_of).astype(F32).astype(BF16)
                carried = carried + dot_nt(spread, which)
            return carried

        before = jnp.zeros((96, 128), F32) if n == 0 else hits[...].reshape(96, 128)
        hits[...] = loop(5, count, before).reshape(2, 48, 128)

    def settle(name):
        value = reduces[name].total()
        n = NAMES.index(name)
        if n < 4:
            small[n] = value.reshape(2, 24, TILE)
            swap[n, c] = small[n, c]
            mates.append(link.copy(small.at[n, 1 - c], swap.at[n, c], spare + 1 + n, device(z, x, y, 1 - c)))
        else:
            rows = slice(48 * (n % 2), 48 * (n % 2) + 48)
            if n < 8:
                down_out[rows, half((n - 4) // 2)] = value
            else:
                up_out[rows, half((n - 8) // 2)] = value

    steps = {"fill": fill, "turn1": turn1, "turnd": turnd, "out": out, "norm2": norm2, "dmix": dmix, "gout": gout, "res": res, "tok": tok}
    for k in range(3):
        steps["proj" + str(k)] = functools.partial(proj, k)
        steps["att" + str(k)] = functools.partial(att, k)
        steps["attb" + str(k)] = functools.partial(attb, k)
        steps["projb" + str(k)] = functools.partial(projb, k)
        for i in range(4):
            steps["look" + str(k) + str(i)] = functools.partial(look, k, i)
    for i in range(2):
        steps["sec" + str(i)] = functools.partial(sec, i)
        steps["norm1" + str(i)] = functools.partial(norm1, i)
        steps["first" + str(i)] = functools.partial(first, i)
        for k in range(2):
            steps["wide" + str(k) + str(i)] = functools.partial(widening, k, i)
            steps["back" + str(k) + str(i)] = functools.partial(back, k, i)
            steps["grad" + str(k) + str(i)] = functools.partial(grad, k, i)
    for n in range(5):
        steps["count" + str(n)] = functools.partial(counting, n)
    for name in NAMES:
        for event in "LmnPQRF":
            steps[event + name] = getattr(gathers[name], event)
        for event in "cdefpq":
            steps[event + name] = getattr(reduces[name], event)
        steps["g" + name] = functools.partial(settle, name)
    for what, everywhere in sums.items():
        steps[what + "0"] = everywhere.to_core
        steps[what + "1"] = everywhere.to_plane
        steps[what + "2"] = everywhere.to_line
        steps[what + "3"] = everywhere.to_mate

    def give_early():
        sums["E"].wait()
        for part in range(2):
            early_out[part * 8 : part * 8 + 8, :] = sums["E"].total(part)

    def give_late():
        sums["l"].wait()
        for core in range(2):
            late_out[:, half(core)] = sums["l"].total(core)

    def give_table():
        sums["t"].wait()
        for part in range(2):
            found = sums["t"].total(part).reshape(6, 8, 128)
            for piece in range(6):
                width = min(128, 732 - piece * 128)
                table_out[part * 6 : part * 6 + 6, piece * 128 : piece * 128 + width] = found[:, piece, 0:width]

    steps["E4"], steps["l4"], steps["t4"] = give_early, give_late, give_table
    todo = list(steps.values())
    for n in ORDER:
        todo[n]()
    for made in mates:
        made.wait_recv()
    for k in range(3):
        for core in range(2):
            for part in range(3):
                start = (core * 3 + k) * 128
                packed[part * 24 : part * 24 + 24, start : start + 128] = swap[k, core, :, part * 128 : part * 128 + 128]
    for core in range(2):
        outer_out[:, half(core)] = swap[3, core]
    link.drain()


def run_layer(*operands):
    def vmem(*shape, dtype=BF16):
        return pltpu.VMEM(shape, dtype)

    scratch = [
        vmem(4, 2, 4, 2, 2, 48, TILE),
        vmem(4, 2, 2, 4, 2, 96, TILE),
        vmem(4, 2, 24, TILE, dtype=F32),
        vmem(4, 2, 24, TILE, dtype=F32),
        vmem(4, 2, 24, TILE, dtype=F32),
        vmem(TALL, 768),
        vmem(TALL, 768),
        vmem(TALL, 768),
        vmem(768, TALL),
        vmem(TALL, 768),
        vmem(768, TALL),
        vmem(6, TALL + 48, TILE),
        vmem(12, PAD, KEYS, dtype=F32),
        vmem(2, PAD, KEYS, dtype=F32),
        vmem(PAD, KEYS, dtype=jnp.int32),
        vmem(2, 12, PAD, KEYS),
        vmem(768, TALL),
        vmem(TALL, 768, dtype=F32),
        vmem(TALL, 768, dtype=F32),
        vmem(TALL, 768),
        vmem(768, TALL),
        vmem(8, TALL, TILE),
        vmem(8, TALL, TILE),
        vmem(TALL, 768, dtype=F32),
        vmem(TALL, 768, dtype=F32),
        vmem(6, 1, TILE, dtype=F32),
        vmem(4, 1, 768, dtype=F32),
        vmem(12, 1, 768, dtype=F32),
        vmem(10, 1, 768, dtype=F32),
        vmem(2, 8, 768, dtype=F32),
        vmem(2, 8, TILE, dtype=F32),
        vmem(2, 48, 128, dtype=F32),
    ]
    for shape in ((8, 768), (8, TILE), (48, 128)):
        scratch += [vmem(3, *shape, dtype=F32), vmem(4, *shape, dtype=F32), vmem(4, *shape, dtype=F32)]
    copies = 2 * len(NAMES) * N_COPY + 40
    scratch += [pltpu.SemaphoreType.DMA((copies,)), pltpu.SemaphoreType.DMA((copies,))]
    for name in NAMES:
        scratch += [vmem(*shape) for shape in Reduce.buffers(name)]
    shapes = [((197, 2, 768), BF16), ((197, 2, 768), BF16), ((328, 768), F32)]
    return pl.pallas_call(
        layer_kernel,
        out_shape=[jax.ShapeDtypeStruct(*shape) for shape in shapes],
        in_specs=[pl.BlockSpec(memory_space=pltpu.VMEM)] * len(operands),
        out_specs=[pl.BlockSpec(memory_space=pltpu.VMEM)] * len(shapes),
        scratch_shapes=scratch,
        compiler_params=pltpu.CompilerParams(
            collective_id=0, has_side_effects=True, vmem_limit_bytes=62 * 2**20
        ),
    )(*operands)


def fast_body(*operands):
    operands = list(operands)
    operands[0] = operands[0].transpose(1, 0, 2)
    operands[3] = operands[3].transpose(1, 0, 2)
    operands[15] = operands[15].reshape(1, -1)
    operands[16] = operands[16].T
    operands[19] = operands[19].T
    result, token_grad, packed = run_layer(*operands)
    result, token_grad = result.transpose(1, 0, 2), token_grad.transpose(1, 0, 2)
    inner = jnp.concatenate([packed[0:24], packed[24:48], packed[48:72]], axis=1)
    early, late = packed[288:304], packed[304:312]
    first = (result, token_grad, inner, packed[72:96], packed[96:192], packed[192:288].T, late[0], late[1], late[2], late[3])
    table = packed[312:324, 0:732].T
    return (*first, early[0], early[1], early[2], early[3], early[8:12].reshape(3072), early[4], early[5], table)


def layer_norm(values, gain, shift):
    mean = jnp.mean(values, -1, keepdims=True)
    centred = values - mean
    variance = jnp.mean(centred * centred, -1, keepdims=True)
    scaled = lax.rsqrt(variance + EPS)
    unit = centred * scaled
    return (unit * gain + shift, unit, scaled)


def norm_back(upstream, unit, scaled, gain):
    inner = upstream * gain
    first = jnp.mean(inner, -1, keepdims=True)
    second = jnp.mean(inner * unit, -1, keepdims=True)
    return (
        scaled * (inner - first - unit * second),
        jnp.sum(upstream * unit, 0),
        jnp.sum(upstream, 0),
    )


def gelu_pair(pre):
    cumul = 0.5 * (1.0 + lax.erf(pre * ROOT_HALF))
    return (pre * cumul, cumul + pre * jnp.exp(-0.5 * pre * pre) * DENSITY)


def fetch(inner_weight, outer_weight, up_weight, down_weight):
    inner_full, outer_full = (
        lax.all_gather(inner_weight, ("dp", "mlp"), axis=0, tiled=True),
        lax.all_gather(outer_weight, ("dp", "mlp"), axis=0, tiled=True),
    )
    up_full, down_full = (
        lax.all_gather(up_weight, "dp", axis=0, tiled=True),
        lax.all_gather(down_weight, "dp", axis=1, tiled=True),
    )
    return (inner_full, outer_full, up_full, down_full)


def contract_rows(left, right):
    return lax.dot_general(
        left, right, (((0,), (0,)), ((), ())), preferred_element_type=jnp.float32
    )


def contract_cols(left, right):
    return lax.dot_general(
        left, right, (((1,), (1,)), ((), ())), preferred_element_type=jnp.float32
    )


def logits_of(query, keys, bias, allowed, factor):
    raw = jnp.einsum("qhd,khd->hqk", query, keys, preferred_element_type=jnp.float32) * factor
    return jnp.where(allowed, raw + bias, -1e30)


def body(
    tokens,
    keep_mask,
    position_index,
    cotangent,
    first_gain,
    first_shift,
    inner_weight,
    query_bias,
    value_bias,
    outer_weight,
    outer_bias,
    attend_scale,
    second_gain,
    second_shift,
    up_weight,
    up_bias,
    down_weight,
    down_bias,
    feed_scale,
    position_table,
):
    micro, rows, width = tokens.shape
    heads = position_table.shape[1]
    head_dim = width // heads
    factor = head_dim ** (-0.5)
    entries = position_table.shape[0]
    columns = up_weight.shape[1]
    col_start = lax.axis_index("mlp") * columns
    up_local = lax.dynamic_slice_in_dim(up_bias, col_start, columns, 0)
    shift_vector = jnp.concatenate([query_bias, jnp.zeros_like(query_bias), value_bias])
    table_by_head = jnp.transpose(position_table)
    bias = table_by_head[:, position_index]
    seen = jnp.arange(rows)
    diagonal = seen[:, None] == seen[None, :]
    flat_index = position_index.reshape(rows * rows)
    zero_width = jnp.zeros((width,), jnp.float32)
    sum_inner = jnp.zeros((width, 3 * width), jnp.float32)
    sum_outer = jnp.zeros((width, width), jnp.float32)
    sum_up = jnp.zeros((width, columns), jnp.float32)
    sum_down = jnp.zeros((columns, width), jnp.float32)
    sum_table_heads = jnp.zeros((heads, entries), jnp.float32)
    sum_up_bias = jnp.zeros((columns,), jnp.float32)
    sum_first_gain = zero_width
    sum_first_shift = zero_width
    sum_query_bias = zero_width
    sum_value_bias = zero_width
    sum_outer_bias = zero_width
    sum_attend_scale = zero_width
    sum_second_gain = zero_width
    sum_second_shift = zero_width
    sum_down_bias = zero_width
    sum_feed_scale = zero_width
    results = []
    input_grads = []
    for index in range(micro):
        inner_full, outer_full, up_full, down_full = fetch(
            inner_weight, outer_weight, up_weight, down_weight
        )
        source = tokens[index].astype(jnp.float32)
        allowed = jnp.logical_or(keep_mask[index][None, :] == 1, diagonal)[None]
        normed_one, unit_one, scaled_one = layer_norm(source, first_gain, first_shift)
        normed_one = normed_one.astype(jnp.bfloat16)
        projected = (
            jnp.dot(normed_one, inner_full, preferred_element_type=jnp.float32) + shift_vector
        ).astype(jnp.bfloat16)
        query = projected[:, :width].reshape(rows, heads, head_dim)
        keys = projected[:, width : 2 * width].reshape(rows, heads, head_dim)
        values = projected[:, 2 * width :].reshape(rows, heads, head_dim)
        logits = logits_of(query, keys, bias, allowed, factor)
        top = jnp.max(logits, -1, keepdims=True)
        expd = jnp.exp(logits - top)
        total = jnp.sum(expd, -1, keepdims=True)
        probs = expd / total
        log_total = top + jnp.log(total)
        mixed = jnp.einsum(
            "hqk,khd->qhd", probs.astype(jnp.bfloat16), values, preferred_element_type=jnp.float32
        )
        mixed = mixed.reshape(rows, width).astype(jnp.bfloat16)
        attend = jnp.dot(mixed, outer_full, preferred_element_type=jnp.float32) + outer_bias
        resid = source + attend_scale * attend
        normed_two, unit_two, scaled_two = layer_norm(resid, second_gain, second_shift)
        normed_two = normed_two.astype(jnp.bfloat16)
        sequence_rows = lax.all_gather(normed_two, "mlp", axis=0, tiled=True)
        pre = jnp.dot(sequence_rows, up_full, preferred_element_type=jnp.float32) + up_local
        active, slope = gelu_pair(pre)
        hidden = active.astype(jnp.bfloat16)
        feed = (
            lax.psum_scatter(
                jnp.dot(hidden, down_full, preferred_element_type=jnp.float32).astype(jnp.bfloat16),
                "mlp",
                scatter_dimension=0,
                tiled=True,
            ).astype(jnp.float32)
            + down_bias
        )
        results.append((resid + feed_scale * feed).astype(jnp.bfloat16))
        inner_full, outer_full, up_full, down_full = fetch(
            inner_weight, outer_weight, up_weight, down_weight
        )
        upstream = cotangent[index].astype(jnp.float32)
        sum_feed_scale = sum_feed_scale + jnp.sum(feed * upstream, 0)
        dfeed = feed_scale * upstream
        sum_down_bias = sum_down_bias + jnp.sum(dfeed, 0)
        upstream_all = lax.all_gather(dfeed.astype(jnp.bfloat16), "mlp", axis=0, tiled=True)
        sum_down = sum_down + contract_rows(hidden, upstream_all)
        dpre = (contract_cols(upstream_all, down_full) * slope).astype(jnp.bfloat16)
        sum_up_bias = sum_up_bias + jnp.sum(dpre.astype(jnp.float32), 0)
        sum_up = sum_up + contract_rows(sequence_rows, dpre)
        dnormed_two = lax.psum_scatter(
            contract_cols(dpre, up_full).astype(jnp.bfloat16),
            "mlp",
            scatter_dimension=0,
            tiled=True,
        ).astype(jnp.float32)
        dresid_norm, part_gain, part_shift = norm_back(
            dnormed_two, unit_two, scaled_two, second_gain
        )
        sum_second_gain = sum_second_gain + part_gain
        sum_second_shift = sum_second_shift + part_shift
        dresid = upstream + dresid_norm
        sum_attend_scale = sum_attend_scale + jnp.sum(attend * dresid, 0)
        dattend = attend_scale * dresid
        sum_outer_bias = sum_outer_bias + jnp.sum(dattend, 0)
        dattend_low = dattend.astype(jnp.bfloat16)
        sum_outer = sum_outer + contract_rows(mixed, dattend_low)
        dmixed = (
            contract_cols(dattend_low, outer_full)
            .astype(jnp.bfloat16)
            .reshape(rows, heads, head_dim)
        )
        logits = logits_of(query, keys, bias, allowed, factor)
        probs = jnp.exp(logits - log_total)
        dvalues = jnp.einsum(
            "hqk,qhd->khd", probs.astype(jnp.bfloat16), dmixed, preferred_element_type=jnp.float32
        )
        dprobs = jnp.einsum("qhd,khd->hqk", dmixed, values, preferred_element_type=jnp.float32)
        dlogits = probs * (dprobs - jnp.sum(dprobs * probs, -1, keepdims=True))
        sum_table_heads = sum_table_heads.at[:, flat_index].add(dlogits.reshape(heads, rows * rows))
        dlogits_low = dlogits.astype(jnp.bfloat16)
        dquery = (
            jnp.einsum("hqk,khd->qhd", dlogits_low, keys, preferred_element_type=jnp.float32)
            * factor
        )
        dkeys = (
            jnp.einsum("hqk,qhd->khd", dlogits_low, query, preferred_element_type=jnp.float32)
            * factor
        )
        dprojected = jnp.concatenate(
            [dquery.reshape(rows, width), dkeys.reshape(rows, width), dvalues.reshape(rows, width)],
            axis=1,
        ).astype(jnp.bfloat16)
        sum_query_bias = sum_query_bias + jnp.sum(dprojected[:, :width].astype(jnp.float32), 0)
        sum_value_bias = sum_value_bias + jnp.sum(dprojected[:, 2 * width :].astype(jnp.float32), 0)
        sum_inner = sum_inner + contract_rows(normed_one, dprojected)
        dnormed_one = contract_cols(dprojected, inner_full)
        dsource_norm, part_gain, part_shift = norm_back(
            dnormed_one, unit_one, scaled_one, first_gain
        )
        sum_first_gain = sum_first_gain + part_gain
        sum_first_shift = sum_first_shift + part_shift
        input_grads.append((dresid + dsource_norm).astype(jnp.bfloat16))
    sum_table = jnp.transpose(sum_table_heads)
    gradient_inner, gradient_outer = (
        lax.psum_scatter(sum_inner, ("dp", "mlp"), scatter_dimension=0, tiled=True),
        lax.psum_scatter(sum_outer, ("dp", "mlp"), scatter_dimension=0, tiled=True),
    )
    gradient_up, gradient_down = (
        lax.psum_scatter(sum_up, "dp", scatter_dimension=0, tiled=True),
        lax.psum_scatter(sum_down, "dp", scatter_dimension=1, tiled=True),
    )
    up_bias_full = lax.dynamic_update_slice_in_dim(
        jnp.zeros((up_bias.shape[0],), jnp.float32), sum_up_bias, col_start, 0
    )
    summed = lax.psum(
        (
            sum_first_gain,
            sum_first_shift,
            sum_query_bias,
            sum_value_bias,
            sum_outer_bias,
            sum_attend_scale,
            sum_second_gain,
            sum_second_shift,
            up_bias_full,
            sum_down_bias,
            sum_feed_scale,
            sum_table,
        ),
        ("dp", "mlp"),
    )
    return (
        jnp.stack(results),
        jnp.stack(input_grads),
        gradient_inner,
        gradient_outer,
        gradient_up,
        gradient_down,
        summed[0],
        summed[1],
        summed[2],
        summed[3],
        summed[4],
        summed[5],
        summed[6],
        summed[7],
        summed[8],
        summed[9],
        summed[10],
        summed[11],
    )


def solution(mesh):
    special = mesh.shape["dp"] == 8 and mesh.shape["mlp"] == 4
    placed = (
        P(None, ("dp", "mlp"), None),
        P(None, ("dp", "mlp")),
        P(),
        P(None, ("dp", "mlp"), None),
        P(),
        P(),
        P(("dp", "mlp"), None),
        P(),
        P(),
        P(("dp", "mlp"), None),
        P(),
        P(),
        P(),
        P(),
        P("dp", "mlp"),
        P(),
        P("mlp", "dp"),
        P(),
        P(),
        P(),
    )
    return jax.shard_map(
        fast_body if special else body,
        mesh=mesh,
        in_specs=placed,
        out_specs=(
            P(None, ("dp", "mlp"), None),
            P(None, ("dp", "mlp"), None),
            P(("dp", "mlp"), None),
            P(("dp", "mlp"), None),
            P("dp", "mlp"),
            P("mlp", "dp"),
            P(),
            P(),
            P(),
            P(),
            P(),
            P(),
            P(),
            P(),
            P(),
            P(),
            P(),
            P(),
        ),
        check_vma=False,
    )
```
